128 devices in a mesh: band: 64 (over z, y, x), mp: 2 (over core).
Axes of the slice: x: 4, y: 4, z: 4, core: 2. Of those that a mesh axis runs over, the one named last changes fastest.
Arguments:
- grid_fields: bfloat16 [131072, 100], P('band'), may hold values from -6 to 6
- w_in: bfloat16 [100, 1024], P(None, 'mp'), may hold values from -0.625 to 0.625
- enc_src: int32 [4096, 128], P('band'), may hold values from 0 to 131071, as said below
- enc_dst: int32 [4096, 128], P('band'), may hold values from 0 to 65535, as said below
- enc_weight: bfloat16 [4096, 128], P('band'), may hold values from 0.19921875 to 2
- enc_count: int32 [64], P('band'), may hold values from 32 to 64, as said below
- norm_gain: float32 [1024], replicated, may hold values from 0.1 to 1.9
- w_qkv: bfloat16 [1024, 3, 1024], P(None, None, 'mp'), may hold values from -4 to 4
- w_out_attn: bfloat16 [1024, 1024], P('mp'), may hold values from -0.1875 to 0.1875
- offsets: int32 [32], replicated, may hold values from -384 to 384, as said below
- w_decode: bfloat16 [1024, 100], P('mp'), may hold values from -0.1875 to 0.1875
- dec_src: int32 [3072, 128], P(('band', 'mp')), may hold values from 0 to 65535, as said below
- dec_dst: int32 [3072, 128], P(('band', 'mp')), may hold values from 0 to 131071, as said below
- dec_weight: bfloat16 [3072, 128], P(('band', 'mp')), may hold values from 0.19921875 to 2
Outputs:
- out_fields: bfloat16 [131072, 100], P(('band', 'mp'))
The draws below stay inside these ranges and needn't reach their ends.
Inputs may be any that keep to these rules, and one draw needn't show every extreme that they name: `enc_src`: rows s of band b = s // 64 name grid rows from (b - 1) * 2048 to (b + 2) * 2048 - 1 that lie in the grid. `enc_dst`: row s of band b = s // 64, with t = s % 8, names mesh rows b * 1024 + t * 128 to b * 1024 + (t + 1) * 128 - 1. `enc_count`: live block slots of each band; some band has all 64. `offsets`: Distinct; they include 0, 384 and -384. `dec_src`: rows s of device d = s // 24, in band b = d // 2, name mesh rows from (b - 1) * 1024 to (b + 2) * 1024 - 1 that lie in the mesh. `dec_dst`: row s of device d = s // 24, with t = s % 8, names grid rows d * 1024 + t * 128 to d * 1024 + (t + 1) * 128 - 1.
All inputs are finite; a program needn't handle non-finite values.
Results may differ from the reference program's by a relative error of at most 0.015.
Values may be sent and summed in bfloat16 or wider, within the bound.
No kernel may reach another device: no remote copies, remote signals or barrier semaphores. Data moves between devices by JAX's collectives and lax.ppermute only.
A program may use at most 128 MiB of HBM per device.

```python
import math
import jax
import jax.numpy as jnp
from jax import lax

D = 1024
C = 100
HEADS = 16
M_DEV = 1024
EDGE = 128
K_OFF = 32
G_BAND = 2048
EB = 64
HEAD = 64
DQ = 512
WIN = 384
GQ = 1024
DB = 24
GRID = 131072
MESH = 65536
N_BAND = 64
N_MP = 2


def draw_enc_src(key, part):
    key = jax.random.fold_in(key, 11)
    owner_band = jnp.arange(N_BAND * EB, dtype=jnp.int32)[:, None] // EB
    spread = jax.random.randint(key, (N_BAND * EB, EDGE), -G_BAND, 2 * G_BAND)
    return jnp.clip(owner_band * G_BAND + spread, 0, GRID - 1).astype(jnp.int32)


def draw_enc_dst(key, part):
    key = jax.random.fold_in(key, 12)
    block_rows = jnp.arange(N_BAND * EB, dtype=jnp.int32)[:, None]
    owner_band = block_rows // EB
    tile_index = block_rows % (M_DEV // EDGE)
    within = jax.random.randint(key, (N_BAND * EB, EDGE), 0, EDGE)
    return (owner_band * M_DEV + tile_index * EDGE + within).astype(jnp.int32)


def draw_enc_count(key, part):
    key = jax.random.fold_in(key, 13)
    key_counts, key_pick = jax.random.split(key)
    uniform_draw = jax.random.randint(key_counts, (N_BAND,), 0, EB + 1)
    counts = jnp.maximum(EB // 2, uniform_draw * uniform_draw // EB)
    busiest = jax.random.randint(key_pick, (), 0, N_BAND)
    return counts.at[busiest].set(EB).astype(jnp.int32)


def draw_offsets(key, part):
    key = jax.random.fold_in(key, 17)
    steps_up = jnp.arange(1, WIN, dtype=jnp.int32)
    candidates = jnp.concatenate([steps_up, -steps_up])
    shuffled = jax.random.permutation(key, candidates)[:K_OFF - 3]
    fixed_ends = jnp.array([0, WIN, -WIN], dtype=jnp.int32)
    return jnp.concatenate([fixed_ends, shuffled]).astype(jnp.int32)


def draw_w_qkv(key, part):
    key = jax.random.fold_in(key, 19)
    key_base = jax.random.fold_in(key, 0)
    base = jax.random.normal(key_base, (D, 3, D), jnp.float32) * D ** (-0.5)
    return jnp.clip(base, -4.0, 4.0).astype(jnp.bfloat16)


def draw_dec_src(key, part):
    key = jax.random.fold_in(key, 23)
    owner_device = jnp.arange(N_BAND * N_MP * DB, dtype=jnp.int32)[:, None] // DB
    owner_band = owner_device // N_MP
    spread = jax.random.randint(key, (N_BAND * N_MP * DB, EDGE), -M_DEV, 2 * M_DEV)
    return jnp.clip(owner_band * M_DEV + spread, 0, MESH - 1).astype(jnp.int32)


def draw_dec_dst(key, part):
    key = jax.random.fold_in(key, 29)
    block_rows = jnp.arange(N_BAND * N_MP * DB, dtype=jnp.int32)[:, None]
    owner_device = block_rows // DB
    tile_index = block_rows % (GQ // EDGE)
    within = jax.random.randint(key, (N_BAND * N_MP * DB, EDGE), 0, EDGE)
    return (owner_device * GQ + tile_index * EDGE + within).astype(jnp.int32)


def levels(key, shape, cuts, smallest, top_value):
    gain = 1.0
    for dim, blocks in cuts:
        steps = jax.random.uniform(jax.random.fold_in(jax.random.fold_in(key, 6), dim), (blocks,), jnp.float32, smallest / len(cuts), top_value / len(cuts))
        gain = gain * jnp.repeat(jnp.exp(steps), shape[dim] // blocks).reshape((-1,) + (1,) * (len(shape) - 1 - dim))
    return gain


def scatter_about(rng, shape, deviation, limit, shards=(), kind=jnp.bfloat16):
    drawn = jax.random.normal(rng, shape, jnp.float32) * deviation
    if len(shards) > 0:
        drawn = levels(rng, shape, shards, -0.22, 0.18) * drawn
    return jnp.clip(drawn, min=-limit, max=limit).astype(kind)


def setup_inputs(seed: int = 0) -> dict:
    splits = jax.random.split(jax.random.key(seed), 15)
    grid_fields = scatter_about(splits[0], (GRID, C), 1.0, 6.0, ((0, 64),))
    w_in = scatter_about(splits[1], (C, D), C ** -0.5, 0.625, ((1, 2),))
    enc_src = draw_enc_src(jax.random.fold_in(splits[14], 71), 0)
    enc_dst = draw_enc_dst(jax.random.fold_in(splits[14], 71), 0)
    enc_weight = jnp.clip(jnp.exp(math.log(2.0) - 2.306499 * jax.random.uniform(splits[4], (N_BAND * EB, EDGE), jnp.float32) ** levels(splits[4], (N_BAND * EB, EDGE), ((0, 64),), -0.2, 0.2)), 0.19921875, 2.0).astype(jnp.bfloat16)
    enc_count = draw_enc_count(jax.random.fold_in(splits[14], 71), 0)
    norm_gain = jnp.clip(1.0 + 0.18 * jax.random.normal(splits[6], (D,), jnp.float32), 0.1, 1.9)
    w_qkv = draw_w_qkv(jax.random.fold_in(splits[14], 71), 0)
    w_out_attn = scatter_about(splits[8], (D, D), D ** -0.5, 0.1875, ((0, 2),))
    offsets = draw_offsets(jax.random.fold_in(splits[14], 71), 0)
    w_decode = scatter_about(splits[10], (D, C), D ** -0.5, 0.1875, ((0, 2),))
    dec_src = draw_dec_src(jax.random.fold_in(splits[14], 71), 0)
    dec_dst = draw_dec_dst(jax.random.fold_in(splits[14], 71), 0)
    dec_weight = jnp.clip(jnp.exp(math.log(2.0) - 2.306499 * jax.random.uniform(splits[13], (N_BAND * N_MP * DB, EDGE), jnp.float32) ** levels(splits[13], (N_BAND * N_MP * DB, EDGE), ((0, 128),), -0.2, 0.2)), 0.19921875, 2.0).astype(jnp.bfloat16)
    return dict(grid_fields=grid_fields, w_in=w_in, enc_src=enc_src, enc_dst=enc_dst, enc_weight=enc_weight, enc_count=enc_count, norm_gain=norm_gain, w_qkv=w_qkv, w_out_attn=w_out_attn, offsets=offsets, w_decode=w_decode, dec_src=dec_src, dec_dst=dec_dst, dec_weight=dec_weight)


def embed_rows(rows, w_in):
    return jax.nn.silu(jnp.dot(rows, w_in, preferred_element_type=jnp.float32)).astype(jnp.bfloat16)

def reference(grid_fields, w_in, enc_src, enc_dst, enc_weight, enc_count, norm_gain, w_qkv, w_out_attn, offsets, w_decode, dec_src, dec_dst, dec_weight):
    embedded = lax.map(lambda block_rows: embed_rows(block_rows, w_in), grid_fields.reshape(N_BAND, G_BAND, C)).reshape(GRID, D)
    slot_live = (jnp.arange(EB, dtype=jnp.int32)[None, :] < enc_count[:, None]).astype(jnp.float32)
    band_src = enc_src.reshape(N_BAND, EB * EDGE)
    band_dst = enc_dst.reshape(N_BAND, EB * EDGE)
    band_weight = (enc_weight.astype(jnp.float32).reshape(N_BAND, EB, EDGE) * slot_live[:, :, None]).reshape(N_BAND, EB * EDGE)

    def encode_band(packed):
        band_index, sources, targets, weights = packed
        messages = embedded[sources].astype(jnp.float32) * weights[:, None]
        return jax.ops.segment_sum(messages, targets - band_index * M_DEV, num_segments=M_DEV)
    mesh_zero = lax.map(encode_band, (jnp.arange(N_BAND, dtype=jnp.int32), band_src, band_dst, band_weight))
    mesh_zero = mesh_zero.reshape(MESH, D).astype(jnp.bfloat16)

    def project_band(block_rows):
        values = block_rows.astype(jnp.float32)
        inverse = lax.rsqrt(lax.optimization_barrier(jnp.mean(values * values, axis=1, keepdims=True)) + 1e-05)
        normed = (values * inverse * norm_gain.astype(jnp.float32)).astype(jnp.bfloat16)
        return jnp.einsum('md,dtc->mtc', normed.astype(jnp.float32), w_qkv.astype(jnp.float32)).astype(jnp.bfloat16)
    qkv = lax.map(project_band, mesh_zero.reshape(N_BAND, M_DEV, D)).reshape(MESH, 3, D)
    queries_all = qkv[:, 0]
    keys_all = qkv[:, 1]
    values_all = qkv[:, 2]

    def attend_band(band_index):
        queries = lax.dynamic_slice_in_dim(queries_all, band_index * M_DEV, M_DEV, 0)
        rows_here = band_index * M_DEV + jnp.arange(M_DEV, dtype=jnp.int32)
        targets = rows_here[:, None] + offsets[None, :]
        inside = (targets >= 0) & (targets < MESH)
        safe_rows = jnp.clip(targets, 0, MESH - 1)
        picked_keys = keys_all[safe_rows].astype(jnp.float32).reshape(M_DEV, K_OFF, HEADS, HEAD)
        picked_values = values_all[safe_rows].astype(jnp.float32).reshape(M_DEV, K_OFF, HEADS, HEAD)
        head_queries = queries.astype(jnp.float32).reshape(M_DEV, HEADS, HEAD)
        scores = jnp.einsum('mhe,mkhe->mhk', head_queries, picked_keys) * HEAD ** (-0.5)
        scores = jnp.where(inside[:, None, :], scores, -1e+30)
        row_max = lax.optimization_barrier(jnp.max(scores, axis=2, keepdims=True))
        expos = jnp.exp(scores - row_max)
        probs = (expos / lax.optimization_barrier(jnp.sum(expos, axis=2, keepdims=True))).astype(jnp.bfloat16)
        attended = jnp.einsum('mhk,mkhe->mhe', probs.astype(jnp.float32), picked_values).astype(jnp.bfloat16).reshape(M_DEV, D)
        total = jnp.zeros((M_DEV, D), jnp.float32)
        for group_index in range(N_MP):
            low_col = group_index * DQ
            head_term = jnp.dot(attended[:, low_col:low_col + DQ], w_out_attn[low_col:low_col + DQ], preferred_element_type=jnp.float32).astype(jnp.bfloat16)
            total = total + head_term.astype(jnp.float32)
        own_rows = lax.dynamic_slice_in_dim(mesh_zero, band_index * M_DEV, M_DEV, 0)
        return (own_rows.astype(jnp.float32) + total).astype(jnp.bfloat16)
    mesh_one = lax.map(attend_band, jnp.arange(N_BAND, dtype=jnp.int32)).reshape(MESH, D)
    projected = jnp.dot(mesh_one, w_decode, preferred_element_type=jnp.float32)
    messages = dec_weight.astype(jnp.float32).reshape(-1)[:, None] * projected[dec_src.reshape(-1)]
    summed = jax.ops.segment_sum(messages, dec_dst.reshape(-1), num_segments=GRID)
    return (grid_fields.astype(jnp.float32) + summed).astype(jnp.bfloat16)
```

```python
import math
import jax
import jax.numpy as jnp
from jax import lax
from jax.experimental import pallas as pl
from jax.experimental.pallas import tpu as pltpu
from jax.sharding import PartitionSpec as P

D = 1024
C = 100
LANES = 128
TILE = 128
ROWS = 512
WIN = 384
K_OFF = 32
HALF = 512
G_BAND = 2048
EDGE_ROUNDS = 8
TILES = 4
STEP = 256
SPAN = TILE + 2 * WIN
WINDOW = ROWS + 2 * WIN
GQ = 1024
DEC_ROUNDS = 3
DEC_TILES = 8
MASKED = -1e30
SCALE = 64 ** (-0.5) * math.log2(math.e)
F32 = jnp.float32
BF16 = jnp.bfloat16
VMEM_BYTES = 56 * 1024 * 1024


def vmem():
    return pl.BlockSpec(memory_space=pltpu.VMEM)


def smem():
    return pl.BlockSpec(memory_space=pltpu.SMEM)


def call(body, operands, smem_count, outs, scratch, flops, touched, name):
    specs = [smem()] * smem_count + [vmem()] * (len(operands) - smem_count)
    return pl.pallas_call(
        body,
        out_shape=outs,
        in_specs=specs,
        out_specs=jax.tree.map(lambda _: vmem(), outs),
        scratch_shapes=scratch,
        compiler_params=pltpu.CompilerParams(vmem_limit_bytes=VMEM_BYTES),
        cost_estimate=pl.CostEstimate(flops=flops, bytes_accessed=touched, transcendentals=0),
        name=name,
    )(*operands)


def matmul(a, b):
    return jnp.dot(a, b, preferred_element_type=F32)


def encode_body(
    info, src, before, own, after, win_own, win_peer, dst, weight, gain,
    mesh_zero, normed,
    rows, first, second, w_in, weights, total,
):
    core, live, grid_base, mesh_base = info[0], info[1], info[2], info[3]
    rows[...] = jnp.zeros_like(rows)
    for place, part in enumerate((before, own, after)):
        rows[place * G_BAND : (place + 1) * G_BAND, :C] = part[...].astype(F32)

    @pl.when(core == 0)
    def _():
        w_in[:, :HALF] = win_own[...]
        w_in[:, HALF:] = win_peer[...]

    @pl.when(core != 0)
    def _():
        w_in[:, :HALF] = win_peer[...]
        w_in[:, HALF:] = win_own[...]

    slots = lax.broadcasted_iota(jnp.int32, weights.shape, 0)
    weights[...] = jnp.where(slots < live, weight[...].astype(F32), 0.0)
    total[...] = jnp.zeros_like(total)
    row_slots = lax.broadcasted_iota(jnp.int32, (TILE, LANES), 0)
    steps = EDGE_ROUNDS * TILE // STEP
    rounds = STEP // TILE

    def slot_of(step, part):
        tile, chunk = step // steps, step % steps
        return (chunk * rounds + part) * 2 * TILES + core * TILES + tile

    def gather(step, buffer):
        for part in range(rounds):
            slot = slot_of(step, part)
            for edge in range(TILE):
                index = src[slot, edge] - grid_base
                buffer[pl.ds(part * TILE + edge, 1), :] = rows[pl.ds(index, 1), :]

    def add(step, buffer):
        tile = step // steps
        half = matmul(buffer[...].astype(BF16), w_in[...])
        embedded = (half + half * jnp.tanh(half)).astype(BF16)
        tables = []
        for part in range(rounds):
            slot = slot_of(step, part)
            target = dst[pl.ds(slot, 1), :] - (mesh_base + tile * TILE)
            tables.append(jnp.where(row_slots == target, weights[pl.ds(slot, 1), :], 0.0))
        table = jnp.concatenate(tables, axis=1).astype(BF16)
        place = pl.ds(pl.multiple_of(tile * TILE, TILE), TILE)
        total[place, :] += matmul(table, embedded)

    gather(0, first)

    def pair(index, carry):
        gather(2 * index + 1, second)
        add(2 * index, first)
        gather(jnp.minimum(2 * index + 2, TILES * steps - 1), first)
        add(2 * index + 1, second)
        return carry

    lax.fori_loop(0, TILES * steps // 2, pair, 0)

    def finish(tile, carry):
        place = pl.ds(pl.multiple_of(tile * TILE, TILE), TILE)
        rounded = total[place, :].astype(BF16)
        mesh_zero[place, :] = rounded
        values = rounded.astype(F32)
        inverse = lax.rsqrt(jnp.mean(values * values, axis=1, keepdims=True) + 1e-05)
        normed[place, :] = (values * inverse * gain[...]).astype(BF16)
        return carry

    lax.fori_loop(0, TILES, finish, 0)


def project_body(offsets, normed, w_own, w_peer, queries, keys, values_t, bias):
    rows = normed[...]
    for half, weight in enumerate((w_own, w_peer)):
        place = slice(half * HALF, (half + 1) * HALF)
        queries[:, place] = matmul(rows, weight[:, :HALF]).astype(BF16)
        keys[:, place] = matmul(rows, weight[:, HALF : 2 * HALF]).astype(BF16)
        values = matmul(rows, weight[:, 2 * HALF : 3 * HALF])
        values_t[place, :] = values.T.astype(BF16)
    for chunk in range(SPAN // TILE):
        row = lax.broadcasted_iota(jnp.int32, (TILE, LANES), 0) + (chunk * TILE - WIN)
        away = row - lax.broadcasted_iota(jnp.int32, (TILE, LANES), 1)
        hit = away == offsets[0]
        for k in range(1, K_OFF):
            hit = hit | (away == offsets[k])
        bias[chunk * TILE : (chunk + 1) * TILE, :] = jnp.where(hit, 0.0, MASKED)


def attend_body(
    info, before, after, queries, keys_own, values_own, bias, w_own, w_peer, mesh_zero,
    out_own, out_peer, dec_own, dec_peer,
    projected,
    keys, values_t, masks, attended, w_decode,
):
    core, first_device, last_device = info[0], info[4], info[5]

    @pl.when(core == 0)
    def _():
        w_decode[:HALF, :] = dec_own[...]
        w_decode[HALF:, :] = dec_peer[...]

    @pl.when(core != 0)
    def _():
        w_decode[:HALF, :] = dec_peer[...]
        w_decode[HALF:, :] = dec_own[...]

    keys[WIN : WIN + ROWS, :] = keys_own[...]
    values_t[:, WIN : WIN + ROWS] = values_own[...]
    for begin, part in ((0, before), (WIN + ROWS, after)):
        rows = part[...]
        for half, weight in enumerate((w_own, w_peer)):
            place = slice(half * HALF, (half + 1) * HALF)
            keys[begin : begin + WIN, place] = matmul(rows, weight[:, HALF : 2 * HALF]).astype(BF16)
            values = matmul(rows, weight[:, 2 * HALF : 3 * HALF])
            values_t[place, begin : begin + WIN] = values.T.astype(BF16)
    low = jnp.where(first_device == 1, MASKED, 0.0)
    high = jnp.where(last_device == 1, MASKED, 0.0)
    for block in range(TILES):
        for chunk in range(SPAN // TILE):
            place = slice(chunk * TILE, (chunk + 1) * TILE)
            mask = bias[place, :]
            if block + chunk < WIN // TILE:
                mask = mask + low
            if block + chunk >= (WIN + ROWS) // TILE:
                mask = mask + high
            masks[block, place, :] = mask
    lane = lax.broadcasted_iota(jnp.int32, (TILE, LANES), 1)

    def head_pair(pair, carry):
        place = pl.ds(pl.multiple_of(pair * LANES, LANES), LANES)
        for block in range(TILES):
            own = slice(block * TILE, (block + 1) * TILE)
            seen = slice(block * TILE, block * TILE + SPAN)
            query = queries[own, place].astype(F32)
            stacked = jnp.concatenate(
                [jnp.where(lane < 64, query, 0.0), jnp.where(lane < 64, 0.0, query)], axis=0
            ).astype(BF16)
            score = lax.dot_general(
                keys[seen, place], stacked, (((1,), (1,)), ((), ())), preferred_element_type=F32
            )
            mask = masks[block]
            score = score * SCALE + jnp.concatenate([mask, mask], axis=1)
            top = jnp.max(score, axis=0, keepdims=True)
            expos = jnp.exp2(score - top)
            inverse = 1.0 / jnp.sum(expos, axis=0, keepdims=True)
            result = matmul(values_t[place, seen], expos.astype(BF16)) * inverse
            both = jnp.concatenate([result[:64, :TILE], result[64:, TILE:]], axis=0)
            attended[place, own] = both.astype(BF16)
        return carry

    lax.fori_loop(0, D // LANES, head_pair, 0)
    term_own = matmul(attended[:HALF, :].T, out_own[...]).astype(BF16).astype(F32)
    term_peer = matmul(attended[HALF:, :].T, out_peer[...]).astype(BF16).astype(F32)
    mesh_one = (mesh_zero[...].astype(F32) + (term_own + term_peer)).astype(BF16)
    projected[...] = matmul(mesh_one, w_decode[...]).astype(BF16)


def decode_body(
    info, src, own, peer, before_same, before_other, after_same, after_other, dst, weight, grid,
    out, rows, messages,
):
    core, mesh_base, row_base = info[0], info[6], info[7]
    other = 1 - core
    for place, part in (
        (core, before_same), (other, before_other), (2 + core, own), (2 + other, peer),
        (4 + core, after_same), (4 + other, after_other),
    ):
        rows[pl.ds(pl.multiple_of(place * ROWS, ROWS), ROWS), :] = part[...].astype(F32)
    row_slots = lax.broadcasted_iota(jnp.int32, (TILE, LANES), 0)

    def tile_sum(tile, carry):
        tables = []
        for part in range(DEC_ROUNDS):
            slot = part * DEC_TILES + tile
            for edge in range(TILE):
                index = src[slot, edge] - mesh_base
                messages[pl.ds(part * TILE + edge, 1), :] = rows[pl.ds(index, 1), :]
            target = dst[pl.ds(slot, 1), :] - (row_base + tile * TILE)
            tables.append(jnp.where(row_slots == target, weight[pl.ds(slot, 1), :], 0.0))
        table = jnp.concatenate(tables, axis=1).astype(BF16)
        summed = matmul(table, messages[...].astype(BF16))
        place = pl.ds(pl.multiple_of(tile * TILE, TILE), TILE)
        fields = grid[pl.ds(pl.multiple_of(core * GQ + tile * TILE, TILE), TILE), :]
        out[place, :] = (fields.astype(F32) + summed[:, :C]).astype(BF16)
        return carry

    lax.fori_loop(0, DEC_TILES, tile_sum, 0)


def shifted(value, step):
    bands = lax.axis_size("band")
    pairs = [(i, i + step) for i in range(bands) if 0 <= i + step < bands]
    return lax.ppermute(value, "band", pairs)


def swapped(value):
    return lax.ppermute(value, "mp", [(0, 1), (1, 0)])


def ring_shifted(value, step):
    devices = lax.axis_size("band") * 2
    pairs = [(i, i + step) for i in range(devices) if 0 <= i + step < devices]
    return lax.ppermute(value, ("band", "mp"), pairs)


def band_other(value, step):
    bands = lax.axis_size("band")
    pairs = [
        (2 * i + j, 2 * (i + step) + 1 - j)
        for i in range(bands) for j in range(2) if 0 <= i + step < bands
    ]
    return lax.ppermute(value, ("band", "mp"), pairs)


def on_device(
    grid_fields, w_in, enc_src, enc_dst, enc_weight, enc_count, norm_gain, w_qkv, w_out_attn,
    offsets, w_decode, dec_src, dec_dst, dec_weight,
):
    band = lax.axis_index("band")
    core = lax.axis_index("mp")
    bands = lax.axis_size("band")
    device = 2 * band + core
    info = jnp.stack([
        core,
        enc_count[0],
        (band - 1) * G_BAND,
        device * ROWS,
        (device == 0).astype(jnp.int32),
        (device == 2 * bands - 1).astype(jnp.int32),
        (band - 1) * 2 * ROWS,
        device * GQ,
    ]).astype(jnp.int32)
    grid_before = shifted(grid_fields, 1)
    grid_after = shifted(grid_fields, -1)
    win_own = jnp.pad(w_in * 0.5, ((0, LANES - C), (0, 0)))
    win_peer = swapped(win_own)
    dec_own = jnp.pad(w_decode, ((0, 0), (0, LANES - C)))
    dec_peer = swapped(dec_own)
    qkv_own = w_qkv.reshape(D, 3 * HALF)
    qkv_peer = swapped(qkv_own)
    out_peer = swapped(w_out_attn)
    mesh_zero, normed = call(
        encode_body,
        (info, enc_src, grid_before, grid_fields, grid_after, win_own, win_peer, enc_dst,
         enc_weight, norm_gain.reshape(1, D)),
        2,
        [jax.ShapeDtypeStruct((ROWS, D), BF16)] * 2,
        [
            pltpu.VMEM((3 * G_BAND, LANES), F32),
            pltpu.VMEM((STEP, LANES), F32),
            pltpu.VMEM((STEP, LANES), F32),
            pltpu.VMEM((LANES, D), BF16),
            pltpu.VMEM(enc_weight.shape, F32),
            pltpu.VMEM((ROWS, D), F32),
        ],
        8 * 10 ** 9, 4 * 10 ** 6, "encode",
    )
    halo_before = ring_shifted(normed[ROWS - WIN :], 1)
    halo_after = ring_shifted(normed[:WIN], -1)
    queries, keys, values_t, bias = call(
        project_body,
        (offsets, normed, qkv_own, qkv_peer),
        1,
        [
            jax.ShapeDtypeStruct((ROWS, D), BF16),
            jax.ShapeDtypeStruct((ROWS, D), BF16),
            jax.ShapeDtypeStruct((D, ROWS), BF16),
            jax.ShapeDtypeStruct((SPAN, TILE), F32),
        ],
        [],
        3 * 10 ** 9, 10 ** 7, "project",
    )
    projected = call(
        attend_body,
        (info, halo_before, halo_after, queries, keys, values_t, bias, qkv_own, qkv_peer,
         mesh_zero, w_out_attn, out_peer, dec_own, dec_peer),
        1,
        jax.ShapeDtypeStruct((ROWS, LANES), BF16),
        [
            pltpu.VMEM((WINDOW, D), BF16),
            pltpu.VMEM((D, WINDOW), BF16),
            pltpu.VMEM((TILES, SPAN, TILE), F32),
            pltpu.VMEM((D, ROWS), BF16),
            pltpu.VMEM((D, LANES), BF16),
        ],
        20 * 10 ** 9, 2 * 10 ** 7, "attend",
    )
    peer = swapped(projected)
    before_same = shifted(projected, 1)
    after_same = shifted(projected, -1)
    before_other = band_other(projected, 1)
    after_other = band_other(projected, -1)
    return call(
        decode_body,
        (info, dec_src, projected, peer, before_same, before_other, after_same, after_other,
         dec_dst, dec_weight.astype(F32), grid_fields),
        2,
        jax.ShapeDtypeStruct((GQ, C), BF16),
        [
            pltpu.VMEM((6 * ROWS, LANES), F32),
            pltpu.VMEM((DEC_ROUNDS * TILE, LANES), F32),
        ],
        10 ** 9, 3 * 10 ** 6, "decode",
    )


def solution(mesh):
    return jax.shard_map(
        on_device,
        mesh=mesh,
        in_specs=(
            P("band", None),
            P(None, "mp"),
            P("band", None),
            P("band", None),
            P("band", None),
            P("band"),
            P(),
            P(None, None, "mp"),
            P("mp", None),
            P(),
            P("mp", None),
            P(("band", "mp"), None),
            P(("band", "mp"), None),
            P(("band", "mp"), None),
        ),
        out_specs=P(("band", "mp"), None),
        check_vma=False,
    )
```

```python
import math
import jax
import jax.numpy as jnp
from jax import lax
from jax.experimental import pallas as pl
from jax.experimental.pallas import tpu as pltpu
from jax.sharding import PartitionSpec as P

D = 1024
C = 100
LANES = 128
TILE = 128
ROWS = 512
WIN = 384
K_OFF = 32
HALF = 512
G_BAND = 2048
EDGE_ROUNDS = 8
TILES = 4
STEP = 256
SPAN = TILE + 2 * WIN
GQ = 1024
DEC_ROUNDS = 3
DEC_TILES = 8
MASKED = -1e30
SCALE = 64 ** (-0.5) * math.log2(math.e)
F32 = jnp.float32
BF16 = jnp.bfloat16
VMEM_BYTES = 20 * 1024 * 1024


def vmem():
    return pl.BlockSpec(memory_space=pltpu.VMEM)


def smem():
    return pl.BlockSpec(memory_space=pltpu.SMEM)


def call(body, operands, smem_count, outs, scratch, flops, touched, name):
    specs = [smem()] * smem_count + [vmem()] * (len(operands) - smem_count)
    return pl.pallas_call(
        body,
        out_shape=outs,
        in_specs=specs,
        out_specs=jax.tree.map(lambda _: vmem(), outs),
        scratch_shapes=scratch,
        compiler_params=pltpu.CompilerParams(vmem_limit_bytes=VMEM_BYTES),
        cost_estimate=pl.CostEstimate(flops=flops, bytes_accessed=touched, transcendentals=0),
        name=name,
    )(*operands)


def matmul(a, b):
    return jnp.dot(a, b, preferred_element_type=F32)


def matmul_t(a, b):
    return lax.dot_general(a, b, (((1,), (1,)), ((), ())), preferred_element_type=F32)


def to_rows(part, wide, rows, begin):
    wide[:C, :] = part[...].astype(F32)
    for block in range(G_BAND // LANES):
        columns = slice(block * LANES, (block + 1) * LANES)
        rows[begin + block * LANES : begin + (block + 1) * LANES, :] = wide[:, columns].T


def prepare_body(offsets, grid, rows, mask, wide):
    wide[...] = jnp.zeros_like(wide)
    to_rows(grid, wide, rows, 0)
    for chunk in range(SPAN // TILE):
        row = lax.broadcasted_iota(jnp.int32, (TILE, LANES), 0) + (chunk * TILE - WIN)
        away = row - lax.broadcasted_iota(jnp.int32, (TILE, LANES), 1)
        hit = away == offsets[0]
        for k in range(1, K_OFF):
            hit = hit | (away == offsets[k])
        mask[chunk * TILE : (chunk + 1) * TILE, :] = jnp.where(hit, 0.0, MASKED).astype(BF16)


def encode_body(
    info, src, sent, swapped_rows, own_rows, win_own, win_peer, dst, weight, gain,
    mesh_zero, normed, to_peer, to_band,
    rows, wide, first, second, w_wide, w_in, weights, total,
):
    core, live, grid_base, mesh_base = info[0], info[1], info[2], info[3]
    wide[...] = jnp.zeros_like(wide)
    rows[G_BAND : 2 * G_BAND, :] = own_rows[...]
    w_wide[...] = jnp.zeros_like(w_wide)

    @pl.when(core == 0)
    def _():
        to_rows(sent, wide, rows, 0)
        to_rows(swapped_rows, wide, rows, 2 * G_BAND)
        w_wide[:C, :HALF] = win_own[...].astype(F32) * 0.5
        w_wide[:C, HALF:] = win_peer[...].astype(F32) * 0.5

    @pl.when(core != 0)
    def _():
        to_rows(swapped_rows, wide, rows, 0)
        to_rows(sent, wide, rows, 2 * G_BAND)
        w_wide[:C, :HALF] = win_peer[...].astype(F32) * 0.5
        w_wide[:C, HALF:] = win_own[...].astype(F32) * 0.5

    w_in[...] = w_wide[...].astype(BF16)
    slots = lax.broadcasted_iota(jnp.int32, weights.shape, 0)
    weights[...] = jnp.where(slots < live, weight[...].astype(F32), 0.0)
    total[...] = jnp.zeros_like(total)
    row_slots = lax.broadcasted_iota(jnp.int32, (TILE, LANES), 0)
    steps = EDGE_ROUNDS * TILE // STEP
    rounds = STEP // TILE

    def slot_of(step, part):
        tile, chunk = step // steps, step % steps
        return (chunk * rounds + part) * 2 * TILES + core * TILES + tile

    def gather(step, buffer):
        for part in range(rounds):
            slot = slot_of(step, part)
            for edge in range(TILE):
                index = src[slot, edge] - grid_base
                buffer[pl.ds(part * TILE + edge, 1), :] = rows[pl.ds(index, 1), :]

    def add(step, buffer):
        tile = step // steps
        half = matmul(buffer[...].astype(BF16), w_in[...])
        embedded = (half + half * jnp.tanh(half)).astype(BF16)
        tables = []
        for part in range(rounds):
            slot = slot_of(step, part)
            target = dst[pl.ds(slot, 1), :] - (mesh_base + tile * TILE)
            tables.append(jnp.where(row_slots == target, weights[pl.ds(slot, 1), :], 0.0))
        table = jnp.concatenate(tables, axis=1).astype(BF16)
        place = pl.ds(pl.multiple_of(tile * TILE, TILE), TILE)
        total[place, :] += matmul(table, embedded)

    gather(0, first)

    def pair(index, carry):
        gather(2 * index + 1, second)
        add(2 * index, first)
        gather(jnp.minimum(2 * index + 2, TILES * steps - 1), first)
        add(2 * index + 1, second)
        return carry

    lax.fori_loop(0, TILES * steps // 2, pair, 0)

    def finish(tile, carry):
        place = pl.ds(pl.multiple_of(tile * TILE, TILE), TILE)
        rounded = total[place, :].astype(BF16)
        mesh_zero[place, :] = rounded
        values = rounded.astype(F32)
        inverse = lax.rsqrt(jnp.mean(values * values, axis=1, keepdims=True) + 1e-05)
        normed[place, :] = (values * inverse * gain[...]).astype(BF16)
        return carry

    lax.fori_loop(0, TILES, finish, 0)

    @pl.when(core == 0)
    def _():
        to_peer[...] = normed[ROWS - WIN :, :]
        to_band[...] = normed[:WIN, :]

    @pl.when(core != 0)
    def _():
        to_peer[...] = normed[:WIN, :]
        to_band[...] = normed[ROWS - WIN :, :]


def identity_pair():
    row = lax.broadcasted_iota(jnp.int32, (TILE, LANES), 0)
    lane = lax.broadcasted_iota(jnp.int32, (TILE, LANES), 1)
    eye = jnp.where(row == lane, 1.0, 0.0).astype(BF16)
    return jnp.concatenate([eye, eye], axis=0), lane


def lanes_of(pair):
    return pl.ds(pl.multiple_of(pair * LANES, LANES), LANES)


def rows_of(block):
    return slice(block * TILE, (block + 1) * TILE)


def score_block(query, lane, eyes, keys, mask, scores):
    query = query.astype(F32)
    stacked = jnp.concatenate(
        [jnp.where(lane < 64, query, 0.0), jnp.where(lane < 64, 0.0, query)], axis=0
    ).astype(BF16)
    scores[...] = matmul_t(
        jnp.concatenate([keys, mask], axis=1), jnp.concatenate([stacked, eyes], axis=1)
    )


def column_top(scores):
    top = scores[:TILE, :]
    for begin in range(TILE, scores.shape[0], TILE):
        top = jnp.maximum(top, scores[begin : begin + TILE, :])
    return jnp.max(top, axis=0, keepdims=True)


def weigh(scores, top, values):
    expos = jnp.exp2((scores[...] - top).astype(BF16))
    ones = jnp.ones((16, scores.shape[0]), BF16)
    result = matmul(jnp.concatenate([values, ones], axis=0), expos)
    both = jnp.concatenate([result[:64, :TILE], result[64:TILE, TILE:]], axis=0)
    return both, result[TILE : TILE + 1, :]


def pipeline(score, finish, first, second):
    buffers = (first, second)
    score(0, 0, first)

    def head_pair(pair, carry):
        for block in range(TILES):
            if block + 1 < TILES:
                score(pair, block + 1, buffers[(block + 1) % 2])
            else:
                score(jnp.minimum(pair + 1, D // LANES - 1), 0, first)
            finish(pair, block, buffers[block % 2])
        return carry

    lax.fori_loop(0, D // LANES, head_pair, 0)


def project_body(
    normed, halo, w_own, w_peer, mask,
    queries, halo_keys, halo_values, sums, stats,
    keys, values_t, first, second,
):
    rows = normed[...]
    beside = halo[...]
    for half, weight in enumerate((w_own, w_peer)):
        place = slice(half * HALF, (half + 1) * HALF)
        queries[:, place] = (matmul(rows, weight[0]) * SCALE).astype(BF16)
        keys[:, place] = matmul(rows, weight[1]).astype(BF16)
        values_t[place, :] = matmul(rows, weight[2]).T.astype(BF16)
        halo_keys[:, place] = matmul(beside, weight[1]).astype(BF16)
        halo_values[place, :] = matmul(beside, weight[2]).T.astype(BF16)
    eyes, lane = identity_pair()

    def score(pair, block, scores):
        begin = WIN - block * TILE
        score_block(
            queries[rows_of(block), lanes_of(pair)], lane, eyes, keys[:, lanes_of(pair)],
            mask[begin : begin + ROWS, :], scores,
        )

    def finish(pair, block, scores):
        top = column_top(scores)
        both, total = weigh(scores, top, values_t[lanes_of(pair), :])
        sums[lanes_of(pair), rows_of(block)] = both
        columns = slice(2 * block * TILE, 2 * (block + 1) * TILE)
        stats[pair, 0:1, columns] = top
        stats[pair, 1:2, columns] = total

    pipeline(score, finish, first, second)


def attend_body(
    info, halo, peer_keys, peer_values, queries, sums, stats, mask, w_own, w_peer,
    mesh_zero, out_own, out_peer, dec_own, dec_peer,
    projected,
    keys, values_t, masks, attended, dec_wide, first, second,
):
    core, first_device, last_device = info[0], info[4], info[5]
    dec_wide[...] = jnp.zeros_like(dec_wide)

    @pl.when(core == 0)
    def _():
        dec_wide[:C, :HALF] = dec_own[...].astype(F32)
        dec_wide[:C, HALF:] = dec_peer[...].astype(F32)
        keys[WIN:, :] = peer_keys[...]
        values_t[:, WIN:] = peer_values[...]

    @pl.when(core != 0)
    def _():
        dec_wide[:C, :HALF] = dec_peer[...].astype(F32)
        dec_wide[:C, HALF:] = dec_own[...].astype(F32)
        keys[:WIN, :] = peer_keys[...]
        values_t[:, :WIN] = peer_values[...]

    begin = pl.ds(pl.multiple_of(core * WIN, WIN), WIN)
    beside = halo[...]
    for half, weight in enumerate((w_own, w_peer)):
        place = slice(half * HALF, (half + 1) * HALF)
        keys[begin, place] = matmul(beside, weight[1]).astype(BF16)
        values_t[place, begin] = matmul(beside, weight[2]).T.astype(BF16)
    low = jnp.where(first_device == 1, MASKED, 0.0)
    high = jnp.where(last_device == 1, MASKED, 0.0)
    for block in range(TILES):
        below, above = WIN - block * TILE, SPAN - block * TILE
        if below > 0:
            masks[block, :below, :] = (mask[:below, :].astype(F32) + low).astype(BF16)
        if above < SPAN:
            masks[block, below:, :] = (mask[above:, :].astype(F32) + high).astype(BF16)
    eyes, lane = identity_pair()

    def score(pair, block, scores):
        seen = slice(block * TILE, block * TILE + WIN)
        score_block(
            queries[rows_of(block), lanes_of(pair)], lane, eyes, keys[seen, lanes_of(pair)],
            masks[block], scores,
        )

    def finish(pair, block, scores):
        seen = slice(block * TILE, block * TILE + WIN)
        columns = slice(2 * block * TILE, 2 * (block + 1) * TILE)
        old, sum_old = stats[pair, 0:1, columns], stats[pair, 1:2, columns]
        top = jnp.maximum(old, column_top(scores))
        both, total = weigh(scores, top, values_t[lanes_of(pair), seen])
        shrink = jnp.exp2(old - top)
        inverse = 1.0 / (sum_old * shrink + total)
        shrink = shrink * inverse
        before = sums[lanes_of(pair), rows_of(block)]
        result = jnp.concatenate([
            before[:64] * shrink[:, :TILE] + both[:64] * inverse[:, :TILE],
            before[64:] * shrink[:, TILE:] + both[64:] * inverse[:, TILE:],
        ], axis=0)
        attended[lanes_of(pair), rows_of(block)] = result.astype(BF16)

    pipeline(score, finish, first, second)
    term_own = matmul(attended[:HALF, :].T, out_own[...]).astype(BF16).astype(F32)
    term_peer = matmul(attended[HALF:, :].T, out_peer[...]).astype(BF16).astype(F32)
    mesh_one = (mesh_zero[...].astype(F32) + (term_own + term_peer)).astype(BF16)
    projected[...] = matmul_t(mesh_one, dec_wide[...].astype(BF16)).astype(BF16)


def decode_body(
    info, src, own, sent, swapped_rows, dst, weight, grid, out, rows, messages, weights
):
    core, mesh_base, row_base = info[0], info[6], info[7]
    other = 1 - core

    def put(place, part):
        rows[pl.ds(pl.multiple_of(place * ROWS, ROWS), ROWS), :] = part.astype(F32)

    put(2 + core, own[0])
    put(2 + other, own[1])
    put(4 * core + core, sent[0])
    put(4 * core + other, sent[1])
    put(4 * other + other, swapped_rows[0])
    put(4 * other + core, swapped_rows[1])
    weights[...] = weight[...].astype(F32)
    row_slots = lax.broadcasted_iota(jnp.int32, (TILE, LANES), 0)

    def tile_sum(tile, carry):
        tables = []
        for part in range(DEC_ROUNDS):
            slot = part * DEC_TILES + tile
            for edge in range(TILE):
                index = src[slot, edge] - mesh_base
                messages[pl.ds(part * TILE + edge, 1), :] = rows[pl.ds(index, 1), :]
            target = dst[pl.ds(slot, 1), :] - (row_base + tile * TILE)
            tables.append(jnp.where(row_slots == target, weights[pl.ds(slot, 1), :], 0.0))
        table = jnp.concatenate(tables, axis=1).astype(BF16)
        summed = matmul(table, messages[...].astype(BF16)).T
        place = pl.ds(pl.multiple_of(tile * TILE, TILE), TILE)
        fields = grid[:, pl.ds(pl.multiple_of(core * GQ + tile * TILE, TILE), TILE)]
        out[:, place] = (fields.astype(F32) + summed[:C, :]).astype(BF16)
        return carry

    lax.fori_loop(0, DEC_TILES, tile_sum, 0)


def swapped(value):
    return lax.ppermute(value, "mp", [(0, 1), (1, 0)])


def up_and_down(value):
    bands = lax.axis_size("band")
    pairs = [(2 * i, 2 * i + 2) for i in range(bands - 1)]
    pairs += [(2 * i + 3, 2 * i + 1) for i in range(bands - 1)]
    return lax.ppermute(value, ("band", "mp"), pairs)


def over_the_edge(value):
    bands = lax.axis_size("band")
    pairs = [(2 * i + 1, 2 * i + 2) for i in range(bands - 1)]
    pairs += [(j, i) for i, j in pairs]
    return lax.ppermute(value, ("band", "mp"), pairs)


def on_device(
    grid_fields, w_in, enc_src, enc_dst, enc_weight, enc_count, norm_gain, w_qkv, w_out_attn,
    offsets, w_decode, dec_src, dec_dst, dec_weight,
):
    band = lax.axis_index("band")
    core = lax.axis_index("mp")
    bands = lax.axis_size("band")
    device = 2 * band + core
    grid = grid_fields.T
    grid_sent = up_and_down(grid)
    grid_swapped = swapped(grid_sent)
    info = jnp.stack([
        core,
        enc_count[0],
        (band - 1) * G_BAND,
        device * ROWS,
        (device == 0).astype(jnp.int32),
        (device == 2 * bands - 1).astype(jnp.int32),
        (band - 1) * 2 * ROWS,
        device * GQ,
    ]).astype(jnp.int32)
    win_peer = swapped(w_in)
    dec_own = w_decode.T
    dec_peer = swapped(dec_own)
    qkv_own = w_qkv.transpose(1, 0, 2)
    qkv_peer = swapped(qkv_own)
    out_peer = swapped(w_out_attn)
    own_rows, mask = call(
        prepare_body,
        (offsets, grid),
        1,
        [
            jax.ShapeDtypeStruct((G_BAND, LANES), F32),
            jax.ShapeDtypeStruct((SPAN, TILE), BF16),
        ],
        [pltpu.VMEM((LANES, G_BAND), F32)],
        10 ** 7, 2 * 10 ** 6, "prepare",
    )
    mesh_zero, normed, to_peer, to_band = call(
        encode_body,
        (info, enc_src, grid_sent, grid_swapped, own_rows, w_in, win_peer, enc_dst,
         enc_weight, norm_gain.reshape(1, D)),
        2,
        [jax.ShapeDtypeStruct((ROWS, D), BF16)] * 2 + [jax.ShapeDtypeStruct((WIN, D), BF16)] * 2,
        [
            pltpu.VMEM((3 * G_BAND, LANES), F32),
            pltpu.VMEM((LANES, G_BAND), F32),
            pltpu.VMEM((STEP, LANES), F32),
            pltpu.VMEM((STEP, LANES), F32),
            pltpu.VMEM((LANES, D), F32),
            pltpu.VMEM((LANES, D), BF16),
            pltpu.VMEM(enc_weight.shape, F32),
            pltpu.VMEM((ROWS, D), F32),
        ],
        8 * 10 ** 9, 4 * 10 ** 6, "encode",
    )
    halo_peer = swapped(to_peer)
    halo_band = over_the_edge(to_band)
    queries, peer_keys, peer_values, sums, stats = call(
        project_body,
        (normed, halo_peer, qkv_own, qkv_peer, mask),
        0,
        [
            jax.ShapeDtypeStruct((ROWS, D), BF16),
            jax.ShapeDtypeStruct((WIN, D), BF16),
            jax.ShapeDtypeStruct((D, WIN), BF16),
            jax.ShapeDtypeStruct((D, ROWS), F32),
            jax.ShapeDtypeStruct((D // LANES, 8, 2 * ROWS), F32),
        ],
        [
            pltpu.VMEM((ROWS, D), BF16),
            pltpu.VMEM((D, ROWS), BF16),
            pltpu.VMEM((ROWS, 2 * TILE), F32),
            pltpu.VMEM((ROWS, 2 * TILE), F32),
        ],
        10 ** 10, 10 ** 7, "project",
    )
    projected = call(
        attend_body,
        (info, halo_band, peer_keys, peer_values, queries, sums, stats, mask, qkv_own,
         qkv_peer, mesh_zero, w_out_attn, out_peer, dec_own, dec_peer),
        1,
        jax.ShapeDtypeStruct((ROWS, LANES), BF16),
        [
            pltpu.VMEM((2 * WIN, D), BF16),
            pltpu.VMEM((D, 2 * WIN), BF16),
            pltpu.VMEM((TILES, WIN, TILE), BF16),
            pltpu.VMEM((D, ROWS), BF16),
            pltpu.VMEM((LANES, D), F32),
            pltpu.VMEM((WIN, 2 * TILE), F32),
            pltpu.VMEM((WIN, 2 * TILE), F32),
        ],
        10 ** 10, 2 * 10 ** 7, "attend",
    )
    own_pair = jnp.stack([projected, swapped(projected)])
    pair_sent = up_and_down(own_pair)
    pair_swapped = swapped(pair_sent)
    return call(
        decode_body,
        (info, dec_src, own_pair, pair_sent, pair_swapped, dec_dst, dec_weight, grid),
        2,
        jax.ShapeDtypeStruct((C, GQ), BF16),
        [
            pltpu.VMEM((6 * ROWS, LANES), F32),
            pltpu.VMEM((DEC_ROUNDS * TILE, LANES), F32),
            pltpu.VMEM(dec_weight.shape, F32),
        ],
        10 ** 9, 3 * 10 ** 6, "decode",
    ).T


def solution(mesh):
    return jax.shard_map(
        on_device,
        mesh=mesh,
        in_specs=(
            P("band", None),
            P(None, "mp"),
            P("band", None),
            P("band", None),
            P("band", None),
            P("band"),
            P(),
            P(None, None, "mp"),
            P("mp", None),
            P(),
            P("mp", None),
            P(("band", "mp"), None),
            P(("band", "mp"), None),
            P(("band", "mp"), None),
        ),
        out_specs=P(("band", "mp"), None),
        check_vma=False,
    )
```

```python
import math
import jax
import jax.numpy as jnp
from jax import lax
from jax.experimental import pallas as pl
from jax.experimental.pallas import tpu as pltpu
from jax.sharding import PartitionSpec as P

D = 1024
C = 100
LANES = 128
TILE = 128
ROWS = 512
WIN = 384
K_OFF = 32
HALF = 512
G_BAND = 2048
EDGE_ROUNDS = 8
TILES = 4
STEP = 512
SPAN = TILE + 2 * WIN
GQ = 1024
DEC_ROUNDS = 3
DEC_TILES = 8
MASKED = -1e30
SCALE = 64 ** (-0.5) * math.log2(math.e)
F32 = jnp.float32
BF16 = jnp.bfloat16
VMEM_BYTES = 20 * 1024 * 1024


def vmem():
    return pl.BlockSpec(memory_space=pltpu.VMEM)


def smem():
    return pl.BlockSpec(memory_space=pltpu.SMEM)


def call(body, operands, smem_count, outs, scratch, flops, touched, name, aliases={}):
    specs = [smem()] * smem_count + [vmem()] * (len(operands) - smem_count)
    return pl.pallas_call(
        body,
        out_shape=outs,
        in_specs=specs,
        out_specs=jax.tree.map(lambda _: vmem(), outs),
        scratch_shapes=scratch,
        compiler_params=pltpu.CompilerParams(vmem_limit_bytes=VMEM_BYTES),
        cost_estimate=pl.CostEstimate(flops=flops, bytes_accessed=touched, transcendentals=0),
        input_output_aliases=aliases,
        name=name,
    )(*operands)


def matmul(a, b):
    return jnp.dot(a, b, preferred_element_type=F32)


def matmul_t(a, b):
    return lax.dot_general(a, b, (((1,), (1,)), ((), ())), preferred_element_type=F32)


def to_rows(part, wide, rows, begin):
    wide[:C, :] = part[...].astype(F32)
    for block in range(G_BAND // LANES):
        columns = slice(block * LANES, (block + 1) * LANES)
        place = pl.multiple_of(begin + block * LANES, LANES)
        rows[pl.ds(place, LANES), :] = wide[:, columns].T


def prepare_body(
    info, offsets, grid, src, dst, weight, gain, win_own, win_peer,
    own_rows, mask, sources, targets, weights, gains, w_in,
    wide, w_wide,
):
    core, live, mesh_base = info[0], info[1], info[3]
    wide[...] = jnp.zeros_like(wide)
    to_rows(grid, wide, own_rows, 0)
    for chunk in range(SPAN // TILE):
        row = lax.broadcasted_iota(jnp.int32, (TILE, LANES), 0) + (chunk * TILE - WIN)
        away = row - lax.broadcasted_iota(jnp.int32, (TILE, LANES), 1)
        hit = away == offsets[0]
        for k in range(1, K_OFF):
            hit = hit | (away == offsets[k])
        mask[chunk * TILE : (chunk + 1) * TILE, :] = jnp.where(hit, 0.0, MASKED).astype(BF16)
    slots = lax.broadcasted_iota(jnp.int32, weights.shape, 0)
    weights[...] = jnp.where(slots < live, weight[...].astype(F32), 0.0)
    targets[...] = dst[...] - mesh_base
    sources[...] = src[...] - info[2]
    gains[...] = gain[...]
    w_wide[...] = jnp.zeros_like(w_wide)

    @pl.when(core == 0)
    def _():
        w_wide[:C, :HALF] = win_own[...].astype(F32) * 0.5
        w_wide[:C, HALF:] = win_peer[...].astype(F32) * 0.5

    @pl.when(core != 0)
    def _():
        w_wide[:C, :HALF] = win_peer[...].astype(F32) * 0.5
        w_wide[:C, HALF:] = win_own[...].astype(F32) * 0.5

    w_in[...] = w_wide[...].astype(BF16)


def unpack_body(info, own_rows, sent, rows, wide):
    wide[...] = jnp.zeros_like(wide)
    rows[G_BAND : 2 * G_BAND, :] = own_rows[...]
    to_rows(sent, wide, rows, info[0] * 2 * G_BAND)


def encode_body(
    info, src, grid_rows, swapped_rows, w_in, targets, weights, gain,
    rows, mesh_zero, normed, to_peer, to_band,
    wide, first, second, total,
):
    core = info[0]
    wide[...] = jnp.zeros_like(wide)
    to_rows(swapped_rows, wide, rows, (1 - core) * 2 * G_BAND)
    total[...] = jnp.zeros_like(total)
    row_slots = lax.broadcasted_iota(jnp.int32, (TILE, LANES), 0)
    steps = EDGE_ROUNDS * TILE // STEP
    rounds = STEP // TILE

    def slot_of(step, part):
        tile, chunk = step // steps, step % steps
        return (chunk * rounds + part) * 2 * TILES + core * TILES + tile

    def gather(step, buffer):
        for part in range(rounds):
            slot = slot_of(step, part)
            for edge in range(TILE):
                index = src[slot, edge]
                buffer[pl.ds(part * TILE + edge, 1), :] = rows[pl.ds(index, 1), :]

    def add(step, buffer):
        tile = step // steps
        half = matmul(buffer[...].astype(BF16), w_in[...])
        embedded = (half + half * jnp.tanh(half)).astype(BF16)
        tables = []
        for part in range(rounds):
            slot = slot_of(step, part)
            target = targets[pl.ds(slot, 1), :] - tile * TILE
            tables.append(jnp.where(row_slots == target, weights[pl.ds(slot, 1), :], 0.0))
        table = jnp.concatenate(tables, axis=1).astype(BF16)
        place = pl.ds(pl.multiple_of(tile * TILE, TILE), TILE)
        total[place, :] += matmul(table, embedded)

    gather(0, first)

    def pair(index, carry):
        gather(2 * index + 1, second)
        add(2 * index, first)
        gather(jnp.minimum(2 * index + 2, TILES * steps - 1), first)
        add(2 * index + 1, second)
        return carry

    lax.fori_loop(0, TILES * steps // 2, pair, 0)

    def finish(tile, carry):
        place = pl.ds(pl.multiple_of(tile * TILE, TILE), TILE)
        rounded = total[place, :].astype(BF16)
        mesh_zero[place, :] = rounded
        values = rounded.astype(F32)
        inverse = lax.rsqrt(jnp.mean(values * values, axis=1, keepdims=True) + 1e-05)
        normed[place, :] = (values * inverse * gain[...]).astype(BF16)
        return carry

    lax.fori_loop(0, TILES, finish, 0)

    @pl.when(core == 0)
    def _():
        to_peer[...] = normed[ROWS - WIN :, :]
        to_band[...] = normed[:WIN, :]

    @pl.when(core != 0)
    def _():
        to_peer[...] = normed[:WIN, :]
        to_band[...] = normed[ROWS - WIN :, :]


def identity_pair():
    row = lax.broadcasted_iota(jnp.int32, (TILE, LANES), 0)
    lane = lax.broadcasted_iota(jnp.int32, (TILE, LANES), 1)
    eye = jnp.where(row == lane, 1.0, 0.0).astype(BF16)
    return jnp.concatenate([eye, eye], axis=0), lane


def lanes_of(pair):
    return pl.ds(pl.multiple_of(pair * LANES, LANES), LANES)


def rows_of(block):
    return slice(block * TILE, (block + 1) * TILE)


def score_block(query, lane, eyes, keys, mask, scores):
    query = query.astype(F32)
    stacked = jnp.concatenate(
        [jnp.where(lane < 64, query, 0.0), jnp.where(lane < 64, 0.0, query)], axis=0
    ).astype(BF16)
    scores[...] = matmul_t(
        jnp.concatenate([keys, mask], axis=1), jnp.concatenate([stacked, eyes], axis=1)
    )


def column_top(scores):
    top = scores[:TILE, :]
    for begin in range(TILE, scores.shape[0], TILE):
        top = jnp.maximum(top, scores[begin : begin + TILE, :])
    return jnp.max(top, axis=0, keepdims=True)


def weigh(scores, top, values):
    expos = jnp.exp2((scores[...] - top).astype(BF16))
    ones = jnp.ones((16, scores.shape[0]), BF16)
    result = matmul(jnp.concatenate([values, ones], axis=0), expos)
    both = jnp.concatenate([result[:64, :TILE], result[64:TILE, TILE:]], axis=0)
    return both, result[TILE : TILE + 1, :]


def pipeline(score, finish, first, second):
    buffers = (first, second)
    score(0, 0, first)

    def head_pair(pair, carry):
        for block in range(TILES):
            if block + 1 < TILES:
                score(pair, block + 1, buffers[(block + 1) % 2])
            else:
                score(jnp.minimum(pair + 1, D // LANES - 1), 0, first)
            finish(pair, block, buffers[block % 2])
        return carry

    lax.fori_loop(0, D // LANES, head_pair, 0)


def project_body(
    normed, halo, w_own, w_peer, mask,
    queries, halo_keys, halo_values, sums, stats,
    keys, values_t, first, second,
):
    rows = normed[...]
    beside = halo[...]
    for half, weight in enumerate((w_own, w_peer)):
        place = slice(half * HALF, (half + 1) * HALF)
        queries[:, place] = (matmul(rows, weight[0]) * SCALE).astype(BF16)
        keys[:, place] = matmul(rows, weight[1]).astype(BF16)
        values_t[place, :] = matmul(rows, weight[2]).T.astype(BF16)
        halo_keys[:, place] = matmul(beside, weight[1]).astype(BF16)
        halo_values[place, :] = matmul(beside, weight[2]).T.astype(BF16)
    eyes, lane = identity_pair()

    def score(pair, block, scores):
        begin = WIN - block * TILE
        score_block(
            queries[rows_of(block), lanes_of(pair)], lane, eyes, keys[:, lanes_of(pair)],
            mask[begin : begin + ROWS, :], scores,
        )

    def finish(pair, block, scores):
        top = column_top(scores)
        both, total = weigh(scores, top, values_t[lanes_of(pair), :])
        sums[lanes_of(pair), rows_of(block)] = both
        columns = slice(2 * block * TILE, 2 * (block + 1) * TILE)
        stats[pair, 0:1, columns] = top
        stats[pair, 1:2, columns] = total

    pipeline(score, finish, first, second)


def attend_body(
    info, halo, peer_keys, peer_values, queries, sums, stats, mask, w_own, w_peer,
    mesh_zero, out_own, out_peer, dec_own, dec_peer,
    projected,
    keys, values_t, masks, attended, dec_wide, first, second,
):
    core, first_device, last_device = info[0], info[4], info[5]
    dec_wide[...] = jnp.zeros_like(dec_wide)

    @pl.when(core == 0)
    def _():
        dec_wide[:C, :HALF] = dec_own[...].astype(F32)
        dec_wide[:C, HALF:] = dec_peer[...].astype(F32)
        keys[WIN:, :] = peer_keys[...]
        values_t[:, WIN:] = peer_values[...]

    @pl.when(core != 0)
    def _():
        dec_wide[:C, :HALF] = dec_peer[...].astype(F32)
        dec_wide[:C, HALF:] = dec_own[...].astype(F32)
        keys[:WIN, :] = peer_keys[...]
        values_t[:, :WIN] = peer_values[...]

    begin = pl.ds(pl.multiple_of(core * WIN, WIN), WIN)
    beside = halo[...]
    for half, weight in enumerate((w_own, w_peer)):
        place = slice(half * HALF, (half + 1) * HALF)
        keys[begin, place] = matmul(beside, weight[1]).astype(BF16)
        values_t[place, begin] = matmul(beside, weight[2]).T.astype(BF16)
    low = jnp.where(first_device == 1, MASKED, 0.0)
    high = jnp.where(last_device == 1, MASKED, 0.0)
    for block in range(TILES):
        below, above = WIN - block * TILE, SPAN - block * TILE
        if below > 0:
            masks[block, :below, :] = (mask[:below, :].astype(F32) + low).astype(BF16)
        if above < SPAN:
            masks[block, below:, :] = (mask[above:, :].astype(F32) + high).astype(BF16)
    eyes, lane = identity_pair()

    def score(pair, block, scores):
        seen = slice(block * TILE, block * TILE + WIN)
        score_block(
            queries[rows_of(block), lanes_of(pair)], lane, eyes, keys[seen, lanes_of(pair)],
            masks[block], scores,
        )

    def finish(pair, block, scores):
        seen = slice(block * TILE, block * TILE + WIN)
        columns = slice(2 * block * TILE, 2 * (block + 1) * TILE)
        old, sum_old = stats[pair, 0:1, columns], stats[pair, 1:2, columns]
        top = jnp.maximum(old, column_top(scores))
        both, total = weigh(scores, top, values_t[lanes_of(pair), seen])
        shrink = jnp.exp2(old - top)
        inverse = 1.0 / (sum_old * shrink + total)
        shrink = shrink * inverse
        before = sums[lanes_of(pair), rows_of(block)]
        result = jnp.concatenate([
            before[:64] * shrink[:, :TILE] + both[:64] * inverse[:, :TILE],
            before[64:] * shrink[:, TILE:] + both[64:] * inverse[:, TILE:],
        ], axis=0)
        attended[lanes_of(pair), rows_of(block)] = result.astype(BF16)

    pipeline(score, finish, first, second)
    term_own = matmul(attended[:HALF, :].T, out_own[...]).astype(BF16).astype(F32)
    term_peer = matmul(attended[HALF:, :].T, out_peer[...]).astype(BF16).astype(F32)
    mesh_one = (mesh_zero[...].astype(F32) + (term_own + term_peer)).astype(BF16)
    projected[...] = matmul_t(mesh_one, dec_wide[...].astype(BF16)).astype(BF16)


def decode_body(
    info, src, own, sent, swapped_rows, dst, weight, grid, out, rows, messages, weights
):
    core, mesh_base, row_base = info[0], info[6], info[7]
    other = 1 - core

    def put(place, part):
        rows[pl.ds(pl.multiple_of(place * ROWS, ROWS), ROWS), :] = part.astype(F32)

    put(2 + core, own[0])
    put(2 + other, own[1])
    put(4 * core + core, sent[0])
    put(4 * core + other, sent[1])
    put(4 * other + other, swapped_rows[0])
    put(4 * other + core, swapped_rows[1])
    weights[...] = weight[...].astype(F32)
    row_slots = lax.broadcasted_iota(jnp.int32, (TILE, LANES), 0)

    def tile_sum(tile, carry):
        tables = []
        for part in range(DEC_ROUNDS):
            slot = part * DEC_TILES + tile
            for edge in range(TILE):
                index = src[slot, edge] - mesh_base
                messages[pl.ds(part * TILE + edge, 1), :] = rows[pl.ds(index, 1), :]
            target = dst[pl.ds(slot, 1), :] - (row_base + tile * TILE)
            tables.append(jnp.where(row_slots == target, weights[pl.ds(slot, 1), :], 0.0))
        table = jnp.concatenate(tables, axis=1).astype(BF16)
        summed = matmul(table, messages[...].astype(BF16)).T
        place = pl.ds(pl.multiple_of(tile * TILE, TILE), TILE)
        fields = grid[:, pl.ds(pl.multiple_of(core * GQ + tile * TILE, TILE), TILE)]
        out[:, place] = (fields.astype(F32) + summed[:C, :]).astype(BF16)
        return carry

    lax.fori_loop(0, DEC_TILES, tile_sum, 0)


def swapped(value):
    return lax.ppermute(value, "mp", [(0, 1), (1, 0)])


def up_and_down(value):
    bands = lax.axis_size("band")
    pairs = [(2 * i, 2 * i + 2) for i in range(bands - 1)]
    pairs += [(2 * i + 3, 2 * i + 1) for i in range(bands - 1)]
    return lax.ppermute(value, ("band", "mp"), pairs)


def over_the_edge(value):
    bands = lax.axis_size("band")
    pairs = [(2 * i + 1, 2 * i + 2) for i in range(bands - 1)]
    pairs += [(j, i) for i, j in pairs]
    return lax.ppermute(value, ("band", "mp"), pairs)


def on_device(
    grid_fields, w_in, enc_src, enc_dst, enc_weight, enc_count, norm_gain, w_qkv, w_out_attn,
    offsets, w_decode, dec_src, dec_dst, dec_weight,
):
    band = lax.axis_index("band")
    core = lax.axis_index("mp")
    bands = lax.axis_size("band")
    device = 2 * band + core
    grid = grid_fields.T
    grid_sent = up_and_down(grid)
    info = jnp.stack([
        core,
        enc_count[0],
        (band - 1) * G_BAND,
        device * ROWS,
        (device == 0).astype(jnp.int32),
        (device == 2 * bands - 1).astype(jnp.int32),
        (band - 1) * 2 * ROWS,
        device * GQ,
    ]).astype(jnp.int32)
    win_peer = swapped(w_in)
    dec_own = w_decode.T
    dec_peer = swapped(dec_own)
    qkv_own = w_qkv.transpose(1, 0, 2)
    qkv_peer = swapped(qkv_own)
    out_peer = swapped(w_out_attn)
    edges = jax.ShapeDtypeStruct(enc_src.shape, jnp.int32)
    own_rows, mask, sources, targets, weights, gain, w_in_all = call(
        prepare_body,
        (info, offsets, grid, enc_src, enc_dst, enc_weight, norm_gain.reshape(1, D), w_in,
         win_peer),
        2,
        [
            jax.ShapeDtypeStruct((G_BAND, LANES), F32),
            jax.ShapeDtypeStruct((SPAN, TILE), BF16),
            edges,
            edges,
            jax.ShapeDtypeStruct(enc_weight.shape, F32),
            jax.ShapeDtypeStruct((1, D), F32),
            jax.ShapeDtypeStruct((LANES, D), BF16),
        ],
        [pltpu.VMEM((LANES, G_BAND), F32), pltpu.VMEM((LANES, D), F32)],
        8 * 10 ** 9, 2 * 10 ** 6, "prepare",
    )
    grid_sent, own_rows = lax.optimization_barrier((grid_sent, own_rows))
    grid_swapped = swapped(grid_sent)
    grid_rows = call(
        unpack_body,
        (info, own_rows, grid_sent),
        1,
        jax.ShapeDtypeStruct((3 * G_BAND, LANES), F32),
        [pltpu.VMEM((LANES, G_BAND), F32)],
        2 * 10 ** 9, 2 * 10 ** 6, "unpack",
    )
    _, mesh_zero, normed, to_peer, to_band = call(
        encode_body,
        (info, sources, grid_rows, grid_swapped, w_in_all, targets, weights, gain),
        2,
        [jax.ShapeDtypeStruct((3 * G_BAND, LANES), F32)]
        + [jax.ShapeDtypeStruct((ROWS, D), BF16)] * 2
        + [jax.ShapeDtypeStruct((WIN, D), BF16)] * 2,
        [
            pltpu.VMEM((LANES, G_BAND), F32),
            pltpu.VMEM((STEP, LANES), F32),
            pltpu.VMEM((STEP, LANES), F32),
            pltpu.VMEM((ROWS, D), F32),
        ],
        8 * 10 ** 9, 4 * 10 ** 6, "encode", {2: 0},
    )
    halo_peer = swapped(to_peer)
    halo_band = over_the_edge(to_band)
    queries, peer_keys, peer_values, sums, stats = call(
        project_body,
        (normed, halo_peer, qkv_own, qkv_peer, mask),
        0,
        [
            jax.ShapeDtypeStruct((ROWS, D), BF16),
            jax.ShapeDtypeStruct((WIN, D), BF16),
            jax.ShapeDtypeStruct((D, WIN), BF16),
            jax.ShapeDtypeStruct((D, ROWS), F32),
            jax.ShapeDtypeStruct((D // LANES, 8, 2 * ROWS), F32),
        ],
        [
            pltpu.VMEM((ROWS, D), BF16),
            pltpu.VMEM((D, ROWS), BF16),
            pltpu.VMEM((ROWS, 2 * TILE), F32),
            pltpu.VMEM((ROWS, 2 * TILE), F32),
        ],
        10 ** 10, 10 ** 7, "project",
    )
    projected = call(
        attend_body,
        (info, halo_band, peer_keys, peer_values, queries, sums, stats, mask, qkv_own,
         qkv_peer, mesh_zero, w_out_attn, out_peer, dec_own, dec_peer),
        1,
        jax.ShapeDtypeStruct((ROWS, LANES), BF16),
        [
            pltpu.VMEM((2 * WIN, D), BF16),
            pltpu.VMEM((D, 2 * WIN), BF16),
            pltpu.VMEM((TILES, WIN, TILE), BF16),
            pltpu.VMEM((D, ROWS), BF16),
            pltpu.VMEM((LANES, D), F32),
            pltpu.VMEM((WIN, 2 * TILE), F32),
            pltpu.VMEM((WIN, 2 * TILE), F32),
        ],
        10 ** 10, 2 * 10 ** 7, "attend",
    )
    own_pair = jnp.stack([projected, swapped(projected)])
    pair_sent = up_and_down(own_pair)
    pair_swapped = swapped(pair_sent)
    return call(
        decode_body,
        (info, dec_src, own_pair, pair_sent, pair_swapped, dec_dst, dec_weight, grid),
        2,
        jax.ShapeDtypeStruct((C, GQ), BF16),
        [
            pltpu.VMEM((6 * ROWS, LANES), F32),
            pltpu.VMEM((DEC_ROUNDS * TILE, LANES), F32),
            pltpu.VMEM(dec_weight.shape, F32),
        ],
        10 ** 9, 3 * 10 ** 6, "decode",
    ).T


def solution(mesh):
    return jax.shard_map(
        on_device,
        mesh=mesh,
        in_specs=(
            P("band", None),
            P(None, "mp"),
            P("band", None),
            P("band", None),
            P("band", None),
            P("band"),
            P(),
            P(None, None, "mp"),
            P("mp", None),
            P(),
            P("mp", None),
            P(("band", "mp"), None),
            P(("band", "mp"), None),
            P(("band", "mp"), None),
        ),
        out_specs=P(("band", "mp"), None),
        check_vma=False,
    )
```

```python
import math
import jax
import jax.numpy as jnp
from jax import lax
from jax.experimental import pallas as pl
from jax.experimental.pallas import tpu as pltpu
from jax.sharding import PartitionSpec as P

D = 1024
C = 100
LANES = 128
TILE = 128
ROWS = 512
WIN = 384
K_OFF = 32
HALF = 512
G_BAND = 2048
EDGE_ROUNDS = 8
TILES = 4
STEP = 512
SPAN = TILE + 2 * WIN
GQ = 1024
DEC_ROUNDS = 3
DEC_TILES = 8
MASKED = -1e30
SCALE = 64 ** (-0.5) * math.log2(math.e)
F32 = jnp.float32
BF16 = jnp.bfloat16
VMEM_BYTES = 20 * 1024 * 1024


def vmem():
    return pl.BlockSpec(memory_space=pltpu.VMEM)


def smem():
    return pl.BlockSpec(memory_space=pltpu.SMEM)


def call(body, operands, smem_count, outs, scratch, flops, touched, name, aliases={}):
    specs = [smem()] * smem_count + [vmem()] * (len(operands) - smem_count)
    return pl.pallas_call(
        body,
        out_shape=outs,
        in_specs=specs,
        out_specs=jax.tree.map(lambda _: vmem(), outs),
        scratch_shapes=scratch,
        compiler_params=pltpu.CompilerParams(vmem_limit_bytes=VMEM_BYTES),
        cost_estimate=pl.CostEstimate(flops=flops, bytes_accessed=touched, transcendentals=0),
        input_output_aliases=aliases,
        name=name,
    )(*operands)


def matmul(a, b):
    return jnp.dot(a, b, preferred_element_type=F32)


def matmul_t(a, b):
    return lax.dot_general(a, b, (((1,), (1,)), ((), ())), preferred_element_type=F32)


def to_rows(part, wide, rows, begin):
    wide[:C, :] = part[...].astype(F32)
    for block in range(G_BAND // LANES):
        columns = slice(block * LANES, (block + 1) * LANES)
        place = pl.multiple_of(begin + block * LANES, LANES)
        rows[pl.ds(place, LANES), :] = wide[:, columns].T


def prepare_body(
    info, offsets, grid, src, dst, weight, gain, win_own, win_peer,
    own_rows, mask, sources, targets, weights, gains, w_in,
    wide, w_wide,
):
    core, live, mesh_base = info[0], info[1], info[3]
    wide[...] = jnp.zeros_like(wide)
    to_rows(grid, wide, own_rows, 0)
    for chunk in range(SPAN // TILE):
        row = lax.broadcasted_iota(jnp.int32, (TILE, LANES), 0) + (chunk * TILE - WIN)
        away = row - lax.broadcasted_iota(jnp.int32, (TILE, LANES), 1)
        hit = away == offsets[0]
        for k in range(1, K_OFF):
            hit = hit | (away == offsets[k])
        mask[chunk * TILE : (chunk + 1) * TILE, :] = jnp.where(hit, 0.0, MASKED).astype(BF16)
    slots = lax.broadcasted_iota(jnp.int32, weights.shape, 0)
    weights[...] = jnp.where(slots < live, weight[...].astype(F32), 0.0)
    targets[...] = dst[...] - mesh_base
    sources[...] = src[...] - info[2]
    gains[...] = gain[...]
    w_wide[...] = jnp.zeros_like(w_wide)

    @pl.when(core == 0)
    def _():
        w_wide[:C, :HALF] = win_own[...].astype(F32) * 0.5
        w_wide[:C, HALF:] = win_peer[...].astype(F32) * 0.5

    @pl.when(core != 0)
    def _():
        w_wide[:C, :HALF] = win_peer[...].astype(F32) * 0.5
        w_wide[:C, HALF:] = win_own[...].astype(F32) * 0.5

    w_in[...] = w_wide[...].astype(BF16)


def unpack_body(info, own_rows, sent, rows, wide):
    wide[...] = jnp.zeros_like(wide)
    rows[G_BAND : 2 * G_BAND, :] = own_rows[...]
    to_rows(sent, wide, rows, info[0] * 2 * G_BAND)


def encode_body(
    info, src, grid_rows, swapped_rows, w_in, targets, weights, gain,
    rows, mesh_zero, normed, to_band,
    wide, first, second, total,
):
    core = info[0]
    wide[...] = jnp.zeros_like(wide)
    to_rows(swapped_rows, wide, rows, (1 - core) * 2 * G_BAND)
    total[...] = jnp.zeros_like(total)
    row_slots = lax.broadcasted_iota(jnp.int32, (TILE, LANES), 0)
    steps = EDGE_ROUNDS * TILE // STEP
    rounds = STEP // TILE

    def slot_of(step, part):
        tile, chunk = step // steps, step % steps
        return (chunk * rounds + part) * 2 * TILES + core * TILES + tile

    def gather(step, buffer):
        for part in range(rounds):
            slot = slot_of(step, part)
            for edge in range(TILE):
                index = src[slot, edge]
                buffer[pl.ds(part * TILE + edge, 1), :] = rows[pl.ds(index, 1), :]

    def add(step, buffer):
        tile = step // steps
        half = matmul(buffer[...].astype(BF16), w_in[...])
        embedded = (half + half * jnp.tanh(half)).astype(BF16)
        tables = []
        for part in range(rounds):
            slot = slot_of(step, part)
            target = targets[pl.ds(slot, 1), :] - tile * TILE
            tables.append(jnp.where(row_slots == target, weights[pl.ds(slot, 1), :], 0.0))
        table = jnp.concatenate(tables, axis=1).astype(BF16)
        place = pl.ds(pl.multiple_of(tile * TILE, TILE), TILE)
        total[place, :] += matmul(table, embedded)

    gather(0, first)

    def pair(index, carry):
        gather(2 * index + 1, second)
        add(2 * index, first)
        gather(jnp.minimum(2 * index + 2, TILES * steps - 1), first)
        add(2 * index + 1, second)
        return carry

    lax.fori_loop(0, TILES * steps // 2, pair, 0)

    def finish(tile, carry):
        place = pl.ds(pl.multiple_of(tile * TILE, TILE), TILE)
        rounded = total[place, :].astype(BF16)
        mesh_zero[place, :] = rounded
        values = rounded.astype(F32)
        inverse = lax.rsqrt(jnp.mean(values * values, axis=1, keepdims=True) + 1e-05)
        normed[place, :] = (values * inverse * gain[...]).astype(BF16)
        return carry

    lax.fori_loop(0, TILES, finish, 0)

    @pl.when(core == 0)
    def _():
        to_band[...] = normed[:WIN, :]

    @pl.when(core != 0)
    def _():
        to_band[...] = normed[ROWS - WIN :, :]


def identity_pair():
    row = lax.broadcasted_iota(jnp.int32, (TILE, LANES), 0)
    lane = lax.broadcasted_iota(jnp.int32, (TILE, LANES), 1)
    eye = jnp.where(row == lane, 1.0, 0.0).astype(BF16)
    return jnp.concatenate([eye, eye], axis=0), lane


def lanes_of(pair):
    return pl.ds(pl.multiple_of(pair * LANES, LANES), LANES)


def rows_of(block):
    return slice(block * TILE, (block + 1) * TILE)


def score_block(query, lane, eyes, keys, mask, scores):
    query = query.astype(F32)
    stacked = jnp.concatenate(
        [jnp.where(lane < 64, query, 0.0), jnp.where(lane < 64, 0.0, query)], axis=0
    ).astype(BF16)
    scores[...] = matmul_t(
        jnp.concatenate([keys, mask], axis=1), jnp.concatenate([stacked, eyes], axis=1)
    )


def column_top(scores):
    top = scores[:TILE, :]
    for begin in range(TILE, scores.shape[0], TILE):
        top = jnp.maximum(top, scores[begin : begin + TILE, :])
    return jnp.max(top, axis=0, keepdims=True)


def weigh(scores, top, values):
    expos = jnp.exp2((scores[...] - top).astype(BF16))
    ones = jnp.ones((16, scores.shape[0]), BF16)
    result = matmul(jnp.concatenate([values, ones], axis=0), expos)
    both = jnp.concatenate([result[:64, :TILE], result[64:TILE, TILE:]], axis=0)
    return both, result[TILE : TILE + 1, :]


def pipeline(score, finish, first, second):
    buffers = (first, second)
    score(0, 0, first)

    def head_pair(pair, carry):
        for block in range(TILES):
            if block + 1 < TILES:
                score(pair, block + 1, buffers[(block + 1) % 2])
            else:
                score(jnp.minimum(pair + 1, D // LANES - 1), 0, first)
            finish(pair, block, buffers[block % 2])
        return carry

    lax.fori_loop(0, D // LANES, head_pair, 0)


def project_body(
    info, normed, w_own, w_peer, queries, keys, values_t, keys_sent, values_sent
):
    rows = normed[...]
    for half, weight in enumerate((w_own, w_peer)):
        place = slice(half * HALF, (half + 1) * HALF)
        keys[:, place] = matmul(rows, weight[1]).astype(BF16)
        values_t[place, :] = matmul(rows, weight[2]).T.astype(BF16)
        queries[:, place] = (matmul(rows, weight[0]) * SCALE).astype(BF16)

    @pl.when(info[0] == 0)
    def _():
        for half in range(2):
            place = slice(half * HALF, (half + 1) * HALF)
            other = slice((1 - half) * HALF, (2 - half) * HALF)
            keys_sent[:, other] = keys[ROWS - WIN :, place]
            values_sent[other, :] = values_t[place, ROWS - WIN :]

    @pl.when(info[0] != 0)
    def _():
        for half in range(2):
            place = slice(half * HALF, (half + 1) * HALF)
            other = slice((1 - half) * HALF, (2 - half) * HALF)
            keys_sent[:, other] = keys[:WIN, place]
            values_sent[other, :] = values_t[place, :WIN]


def own_body(queries, keys, values_t, mask, sums, stats, first, second):
    eyes, lane = identity_pair()

    def score(pair, block, scores):
        begin = WIN - block * TILE
        score_block(
            queries[rows_of(block), lanes_of(pair)], lane, eyes, keys[:, lanes_of(pair)],
            mask[begin : begin + ROWS, :], scores,
        )

    def finish(pair, block, scores):
        top = column_top(scores)
        both, total = weigh(scores, top, values_t[lanes_of(pair), :])
        sums[lanes_of(pair), rows_of(block)] = both
        columns = slice(2 * block * TILE, 2 * (block + 1) * TILE)
        stats[pair, 0:1, columns] = top
        stats[pair, 1:2, columns] = total

    pipeline(score, finish, first, second)


def attend_body(
    info, halo, peer_keys, peer_values, queries, sums, stats, mask, w_own, w_peer,
    mesh_zero, out_own, out_peer, dec_own, dec_peer,
    projected,
    keys, values_t, masks, attended, dec_wide, first, second,
):
    core, first_device, last_device = info[0], info[4], info[5]
    dec_wide[...] = jnp.zeros_like(dec_wide)

    @pl.when(core == 0)
    def _():
        dec_wide[:C, :HALF] = dec_own[...].astype(F32)
        dec_wide[:C, HALF:] = dec_peer[...].astype(F32)
        keys[WIN:, :] = peer_keys[...]
        values_t[:, WIN:] = peer_values[...]

    @pl.when(core != 0)
    def _():
        dec_wide[:C, :HALF] = dec_peer[...].astype(F32)
        dec_wide[:C, HALF:] = dec_own[...].astype(F32)
        keys[:WIN, :] = peer_keys[...]
        values_t[:, :WIN] = peer_values[...]

    begin = pl.ds(pl.multiple_of(core * WIN, WIN), WIN)
    beside = halo[...]
    for half, weight in enumerate((w_own, w_peer)):
        place = slice(half * HALF, (half + 1) * HALF)
        keys[begin, place] = matmul(beside, weight[1]).astype(BF16)
        values_t[place, begin] = matmul(beside, weight[2]).T.astype(BF16)
    low = jnp.where(first_device == 1, MASKED, 0.0)
    high = jnp.where(last_device == 1, MASKED, 0.0)
    for block in range(TILES):
        below, above = WIN - block * TILE, SPAN - block * TILE
        if below > 0:
            masks[block, :below, :] = (mask[:below, :].astype(F32) + low).astype(BF16)
        if above < SPAN:
            masks[block, below:, :] = (mask[above:, :].astype(F32) + high).astype(BF16)
    eyes, lane = identity_pair()

    def score(pair, block, scores):
        seen = slice(block * TILE, block * TILE + WIN)
        score_block(
            queries[rows_of(block), lanes_of(pair)], lane, eyes, keys[seen, lanes_of(pair)],
            masks[block], scores,
        )

    def finish(pair, block, scores):
        seen = slice(block * TILE, block * TILE + WIN)
        columns = slice(2 * block * TILE, 2 * (block + 1) * TILE)
        old, sum_old = stats[pair, 0:1, columns], stats[pair, 1:2, columns]
        top = jnp.maximum(old, column_top(scores))
        both, total = weigh(scores, top, values_t[lanes_of(pair), seen])
        shrink = jnp.exp2(old - top)
        inverse = 1.0 / (sum_old * shrink + total)
        shrink = shrink * inverse
        before = sums[lanes_of(pair), rows_of(block)]
        result = jnp.concatenate([
            before[:64] * shrink[:, :TILE] + both[:64] * inverse[:, :TILE],
            before[64:] * shrink[:, TILE:] + both[64:] * inverse[:, TILE:],
        ], axis=0)
        attended[lanes_of(pair), rows_of(block)] = result.astype(BF16)

    pipeline(score, finish, first, second)
    term_own = matmul(attended[:HALF, :].T, out_own[...]).astype(BF16).astype(F32)
    term_peer = matmul(attended[HALF:, :].T, out_peer[...]).astype(BF16).astype(F32)
    mesh_one = (mesh_zero[...].astype(F32) + (term_own + term_peer)).astype(BF16)
    projected[...] = matmul_t(mesh_one, dec_wide[...].astype(BF16)).astype(BF16)


def put_half(rows, place, part):
    rows[pl.ds(pl.multiple_of(place * ROWS, ROWS), ROWS), :] = part.astype(F32)


def tables_body(info, own, src, dst, weight, rows, sources, tables, weights):
    core, mesh_base, row_base = info[0], info[6], info[7]
    put_half(rows, 2 + core, own[0])
    put_half(rows, 3 - core, own[1])
    sources[...] = src[...] - mesh_base
    weights[...] = weight[...].astype(F32)
    row_slots = lax.broadcasted_iota(jnp.int32, (TILE, LANES), 0)
    for tile in range(DEC_TILES):
        for part in range(DEC_ROUNDS):
            slot = slice(part * DEC_TILES + tile, part * DEC_TILES + tile + 1)
            target = dst[slot, :] - (row_base + tile * TILE)
            tables[rows_of(tile), rows_of(part)] = jnp.where(
                row_slots == target, weights[slot, :], 0.0
            ).astype(BF16)


def decode_body(info, src, rows_in, sent, swapped_rows, tables, grid, rows, out, messages):
    core = info[0]
    other = 1 - core
    put_half(rows, 4 * core + core, sent[0])
    put_half(rows, 4 * core + other, sent[1])
    put_half(rows, 4 * other + other, swapped_rows[0])
    put_half(rows, 4 * other + core, swapped_rows[1])

    def gather(tile, carry):
        begin = pl.multiple_of(tile * DEC_ROUNDS * TILE, TILE)
        for part in range(DEC_ROUNDS):
            for edge in range(TILE):
                index = src[part * DEC_TILES + tile, edge]
                messages[pl.ds(begin + part * TILE + edge, 1), :] = rows[pl.ds(index, 1), :]
        return carry

    lax.fori_loop(0, DEC_TILES, gather, 0)
    span = DEC_ROUNDS * TILE
    for tile in range(DEC_TILES):
        message = messages[tile * span : (tile + 1) * span, :].astype(BF16)
        summed = matmul(tables[rows_of(tile), :], message).T
        fields = grid[:, pl.ds(pl.multiple_of(core * GQ + tile * TILE, TILE), TILE)]
        out[:, rows_of(tile)] = (fields.astype(F32) + summed[:C, :]).astype(BF16)


def swapped(value):
    return lax.ppermute(value, "mp", [(0, 1), (1, 0)])


def up_and_down(value):
    bands = lax.axis_size("band")
    pairs = [(2 * i, 2 * i + 2) for i in range(bands - 1)]
    pairs += [(2 * i + 3, 2 * i + 1) for i in range(bands - 1)]
    return lax.ppermute(value, ("band", "mp"), pairs)


def over_the_edge(value):
    bands = lax.axis_size("band")
    pairs = [(2 * i + 1, 2 * i + 2) for i in range(bands - 1)]
    pairs += [(j, i) for i, j in pairs]
    return lax.ppermute(value, ("band", "mp"), pairs)


def on_device(
    grid_fields, w_in, enc_src, enc_dst, enc_weight, enc_count, norm_gain, w_qkv, w_out_attn,
    offsets, w_decode, dec_src, dec_dst, dec_weight,
):
    band = lax.axis_index("band")
    core = lax.axis_index("mp")
    bands = lax.axis_size("band")
    device = 2 * band + core
    grid = grid_fields.T
    grid_sent = up_and_down(grid)
    info = jnp.stack([
        core,
        enc_count[0],
        (band - 1) * G_BAND,
        device * ROWS,
        (device == 0).astype(jnp.int32),
        (device == 2 * bands - 1).astype(jnp.int32),
        (band - 1) * 2 * ROWS,
        device * GQ,
    ]).astype(jnp.int32)
    win_peer = swapped(w_in)
    dec_own = w_decode.T
    dec_peer = swapped(dec_own)
    qkv_own = w_qkv.transpose(1, 0, 2)
    qkv_peer = swapped(qkv_own)
    out_peer = swapped(w_out_attn)
    edges = jax.ShapeDtypeStruct(enc_src.shape, jnp.int32)
    own_rows, mask, sources, targets, weights, gain, w_in_all = call(
        prepare_body,
        (info, offsets, grid, enc_src, enc_dst, enc_weight, norm_gain.reshape(1, D), w_in,
         win_peer),
        2,
        [
            jax.ShapeDtypeStruct((G_BAND, LANES), F32),
            jax.ShapeDtypeStruct((SPAN, TILE), BF16),
            edges,
            edges,
            jax.ShapeDtypeStruct(enc_weight.shape, F32),
            jax.ShapeDtypeStruct((1, D), F32),
            jax.ShapeDtypeStruct((LANES, D), BF16),
        ],
        [pltpu.VMEM((LANES, G_BAND), F32), pltpu.VMEM((LANES, D), F32)],
        8 * 10 ** 9, 2 * 10 ** 6, "prepare",
    )
    grid_sent, own_rows = lax.optimization_barrier((grid_sent, own_rows))
    grid_swapped = swapped(grid_sent)
    grid_rows = call(
        unpack_body,
        (info, own_rows, grid_sent),
        1,
        jax.ShapeDtypeStruct((3 * G_BAND, LANES), F32),
        [pltpu.VMEM((LANES, G_BAND), F32)],
        2 * 10 ** 9, 2 * 10 ** 6, "unpack",
    )
    _, mesh_zero, normed, to_band = call(
        encode_body,
        (info, sources, grid_rows, grid_swapped, w_in_all, targets, weights, gain),
        2,
        [jax.ShapeDtypeStruct((3 * G_BAND, LANES), F32)]
        + [jax.ShapeDtypeStruct((ROWS, D), BF16)] * 2
        + [jax.ShapeDtypeStruct((WIN, D), BF16)],
        [
            pltpu.VMEM((LANES, G_BAND), F32),
            pltpu.VMEM((STEP, LANES), F32),
            pltpu.VMEM((STEP, LANES), F32),
            pltpu.VMEM((ROWS, D), F32),
        ],
        8 * 10 ** 9, 4 * 10 ** 6, "encode", {2: 0},
    )
    halo_band = over_the_edge(to_band)
    queries, keys, values_t, keys_sent, values_sent = call(
        project_body,
        (info, normed, qkv_own, qkv_peer),
        1,
        [
            jax.ShapeDtypeStruct((ROWS, D), BF16),
            jax.ShapeDtypeStruct((ROWS, D), BF16),
            jax.ShapeDtypeStruct((D, ROWS), BF16),
            jax.ShapeDtypeStruct((WIN, D), BF16),
            jax.ShapeDtypeStruct((D, WIN), BF16),
        ],
        [],
        6 * 10 ** 9, 10 ** 7, "project",
    )
    peer_keys, peer_values = swapped(keys_sent), swapped(values_sent)
    sums, stats = call(
        own_body,
        (queries, keys, values_t, mask),
        0,
        [
            jax.ShapeDtypeStruct((D, ROWS), F32),
            jax.ShapeDtypeStruct((D // LANES, 8, 2 * ROWS), F32),
        ],
        [pltpu.VMEM((ROWS, 2 * TILE), F32), pltpu.VMEM((ROWS, 2 * TILE), F32)],
        8 * 10 ** 9, 10 ** 7, "own",
    )
    projected = call(
        attend_body,
        (info, halo_band, peer_keys, peer_values, queries, sums, stats, mask, qkv_own,
         qkv_peer, mesh_zero, w_out_attn, out_peer, dec_own, dec_peer),
        1,
        jax.ShapeDtypeStruct((ROWS, LANES), BF16),
        [
            pltpu.VMEM((2 * WIN, D), BF16),
            pltpu.VMEM((D, 2 * WIN), BF16),
            pltpu.VMEM((TILES, WIN, TILE), BF16),
            pltpu.VMEM((D, ROWS), BF16),
            pltpu.VMEM((LANES, D), F32),
            pltpu.VMEM((WIN, 2 * TILE), F32),
            pltpu.VMEM((WIN, 2 * TILE), F32),
        ],
        10 ** 10, 2 * 10 ** 7, "attend",
    )
    own_pair = jnp.stack([projected, swapped(projected)])
    pair_sent = up_and_down(own_pair)
    mesh_rows, dec_sources, dec_tables = call(
        tables_body,
        (info, own_pair, dec_src, dec_dst, dec_weight),
        1,
        [
            jax.ShapeDtypeStruct((6 * ROWS, LANES), F32),
            jax.ShapeDtypeStruct(dec_src.shape, jnp.int32),
            jax.ShapeDtypeStruct((GQ, DEC_ROUNDS * TILE), BF16),
        ],
        [pltpu.VMEM(dec_weight.shape, F32)],
        3 * 10 ** 9, 2 * 10 ** 6, "tables",
    )
    pair_sent, mesh_rows = lax.optimization_barrier((pair_sent, mesh_rows))
    pair_swapped = swapped(pair_sent)
    _, out = call(
        decode_body,
        (info, dec_sources, mesh_rows, pair_sent, pair_swapped, dec_tables, grid),
        2,
        [
            jax.ShapeDtypeStruct((6 * ROWS, LANES), F32),
            jax.ShapeDtypeStruct((C, GQ), BF16),
        ],
        [pltpu.VMEM((DEC_TILES * DEC_ROUNDS * TILE, LANES), F32)],
        10 ** 9, 3 * 10 ** 6, "decode", {2: 0},
    )
    return out.T


def solution(mesh):
    return jax.shard_map(
        on_device,
        mesh=mesh,
        in_specs=(
            P("band", None),
            P(None, "mp"),
            P("band", None),
            P("band", None),
            P("band", None),
            P("band"),
            P(),
            P(None, None, "mp"),
            P("mp", None),
            P(),
            P("mp", None),
            P(("band", "mp"), None),
            P(("band", "mp"), None),
            P(("band", "mp"), None),
        ),
        out_specs=P(("band", "mp"), None),
        check_vma=False,
    )
```

```python
import math
import jax
import jax.numpy as jnp
from jax import lax
from jax.experimental import pallas as pl
from jax.experimental.pallas import tpu as pltpu
from jax.sharding import PartitionSpec as P

D = 1024
C = 100
LANES = 128
TILE = 128
ROWS = 512
WIN = 384
K_OFF = 32
HALF = 512
G_BAND = 2048
EDGE_ROUNDS = 8
TILES = 4
STEP = 512
SPAN = TILE + 2 * WIN
GQ = 1024
DEC_ROUNDS = 3
DEC_TILES = 8
GROUP = 2
MASKED = -1e30
SCALE = 64 ** (-0.5) * math.log2(math.e)
F32 = jnp.float32
BF16 = jnp.bfloat16
VMEM_BYTES = 20 * 1024 * 1024


def vmem():
    return pl.BlockSpec(memory_space=pltpu.VMEM)


def smem():
    return pl.BlockSpec(memory_space=pltpu.SMEM)


def call(body, operands, smem_count, outs, scratch, flops, touched, name, aliases={}):
    specs = [smem()] * smem_count + [vmem()] * (len(operands) - smem_count)
    return pl.pallas_call(
        body,
        out_shape=outs,
        in_specs=specs,
        out_specs=jax.tree.map(lambda _: vmem(), outs),
        scratch_shapes=scratch,
        compiler_params=pltpu.CompilerParams(vmem_limit_bytes=VMEM_BYTES),
        cost_estimate=pl.CostEstimate(flops=flops, bytes_accessed=touched, transcendentals=0),
        input_output_aliases=aliases,
        name=name,
    )(*operands)


def matmul(a, b):
    return jnp.dot(a, b, preferred_element_type=F32)


def matmul_t(a, b):
    return lax.dot_general(a, b, (((1,), (1,)), ((), ())), preferred_element_type=F32)


def to_rows(part, wide, rows, begin):
    wide[:C, :] = part[...].astype(F32)
    for block in range(G_BAND // LANES):
        columns = slice(block * LANES, (block + 1) * LANES)
        place = pl.multiple_of(begin + block * LANES, LANES)
        rows[pl.ds(place, LANES), :] = wide[:, columns].T


def prepare_body(
    info, offsets, grid, src, dst, weight, gain, win_own, win_peer,
    own_rows, mask, sources, targets, weights, gains, w_in,
    wide, w_wide,
):
    core, live, mesh_base = info[0], info[1], info[3]
    wide[...] = jnp.zeros_like(wide)
    to_rows(grid, wide, own_rows, 0)
    for chunk in range(SPAN // TILE):
        row = lax.broadcasted_iota(jnp.int32, (TILE, LANES), 0) + (chunk * TILE - WIN)
        away = row - lax.broadcasted_iota(jnp.int32, (TILE, LANES), 1)
        hit = away == offsets[0]
        for k in range(1, K_OFF):
            hit = hit | (away == offsets[k])
        mask[chunk * TILE : (chunk + 1) * TILE, :] = jnp.where(hit, 0.0, MASKED).astype(BF16)
    slots = lax.broadcasted_iota(jnp.int32, weights.shape, 0)
    weights[...] = jnp.where(slots < live, weight[...].astype(F32), 0.0)
    targets[...] = dst[...] - mesh_base
    sources[...] = src[...] - info[2]
    gains[...] = gain[...]
    w_wide[...] = jnp.zeros_like(w_wide)

    @pl.when(core == 0)
    def _():
        w_wide[:C, :HALF] = win_own[...].astype(F32) * 0.5
        w_wide[:C, HALF:] = win_peer[...].astype(F32) * 0.5

    @pl.when(core != 0)
    def _():
        w_wide[:C, :HALF] = win_peer[...].astype(F32) * 0.5
        w_wide[:C, HALF:] = win_own[...].astype(F32) * 0.5

    w_in[...] = w_wide[...].astype(BF16)


def unpack_body(info, own_rows, sent, rows, wide):
    wide[...] = jnp.zeros_like(wide)
    rows[G_BAND : 2 * G_BAND, :] = own_rows[...]
    to_rows(sent, wide, rows, info[0] * 2 * G_BAND)


def encode_body(
    info, src, grid_rows, swapped_rows, w_in, targets, weights, gain,
    rows, mesh_zero, normed, to_band,
    wide, first, second, total,
):
    core = info[0]
    wide[...] = jnp.zeros_like(wide)
    to_rows(swapped_rows, wide, rows, (1 - core) * 2 * G_BAND)
    total[...] = jnp.zeros_like(total)
    row_slots = lax.broadcasted_iota(jnp.int32, (TILE, LANES), 0)
    steps = EDGE_ROUNDS * TILE // STEP
    rounds = STEP // TILE

    def slot_of(step, part):
        tile, chunk = step // steps, step % steps
        return (chunk * rounds + part) * 2 * TILES + core * TILES + tile

    def gather(step, buffer):
        for part in range(rounds):
            slot = slot_of(step, part)
            for edge in range(TILE):
                index = src[slot, edge]
                buffer[pl.ds(part * TILE + edge, 1), :] = rows[pl.ds(index, 1), :]

    def add(step, buffer):
        tile = step // steps
        half = matmul(buffer[...].astype(BF16), w_in[...])
        embedded = (half + half * jnp.tanh(half)).astype(BF16)
        tables = []
        for part in range(rounds):
            slot = slot_of(step, part)
            target = targets[pl.ds(slot, 1), :] - tile * TILE
            tables.append(jnp.where(row_slots == target, weights[pl.ds(slot, 1), :], 0.0))
        table = jnp.concatenate(tables, axis=1).astype(BF16)
        place = pl.ds(pl.multiple_of(tile * TILE, TILE), TILE)
        total[place, :] += matmul(table, embedded)

    gather(0, first)

    def pair(index, carry):
        gather(2 * index + 1, second)
        add(2 * index, first)
        gather(jnp.minimum(2 * index + 2, TILES * steps - 1), first)
        add(2 * index + 1, second)
        return carry

    lax.fori_loop(0, TILES * steps // 2, pair, 0)

    def finish(tile, carry):
        place = pl.ds(pl.multiple_of(tile * TILE, TILE), TILE)
        rounded = total[place, :].astype(BF16)
        mesh_zero[place, :] = rounded
        values = rounded.astype(F32)
        inverse = lax.rsqrt(jnp.mean(values * values, axis=1, keepdims=True) + 1e-05)
        normed[place, :] = (values * inverse * gain[...]).astype(BF16)
        return carry

    lax.fori_loop(0, TILES, finish, 0)

    @pl.when(core == 0)
    def _():
        to_band[...] = normed[:WIN, :]

    @pl.when(core != 0)
    def _():
        to_band[...] = normed[ROWS - WIN :, :]


def identity_pair():
    row = lax.broadcasted_iota(jnp.int32, (TILE, LANES), 0)
    lane = lax.broadcasted_iota(jnp.int32, (TILE, LANES), 1)
    eye = jnp.where(row == lane, 1.0, 0.0).astype(BF16)
    return jnp.concatenate([eye, eye], axis=0), lane


def lanes_of(pair):
    return pl.ds(pl.multiple_of(pair * LANES, LANES), LANES)


def rows_of(block):
    return slice(block * TILE, (block + 1) * TILE)


def score_block(query, lane, eyes, keys, mask, scores):
    query = query.astype(F32)
    stacked = jnp.concatenate(
        [jnp.where(lane < 64, query, 0.0), jnp.where(lane < 64, 0.0, query)], axis=0
    ).astype(BF16)
    scores[...] = matmul_t(
        jnp.concatenate([keys, mask], axis=1), jnp.concatenate([stacked, eyes], axis=1)
    )


def column_top(scores):
    top = scores[:TILE, :]
    for begin in range(TILE, scores.shape[0], TILE):
        top = jnp.maximum(top, scores[begin : begin + TILE, :])
    return jnp.max(top, axis=0, keepdims=True)


def weigh(scores, top, values):
    expos = jnp.exp2(scores[...] - top).astype(BF16)
    ones = jnp.ones((16, scores.shape[0]), BF16)
    result = matmul(jnp.concatenate([values, ones], axis=0), expos)
    both = jnp.concatenate([result[:64, :TILE], result[64:TILE, TILE:]], axis=0)
    return both, result[TILE : TILE + 1, :]


def pipeline(score, finish, first, second):
    buffers = (first, second)
    groups = D // LANES // GROUP

    def part_of(buffer, member):
        return buffer.at[:, member * 2 * TILE : (member + 1) * 2 * TILE]

    for member in range(GROUP):
        score(member, 0, part_of(first, member))

    def head_group(group, carry):
        for block in range(TILES):
            here, ahead = buffers[block % 2], buffers[(block + 1) % 2]
            for member in range(GROUP):
                if block + 1 < TILES:
                    pair = group * GROUP + member
                else:
                    pair = jnp.minimum(group + 1, groups - 1) * GROUP + member
                score(pair, (block + 1) % TILES, part_of(ahead, member))
            for member in range(GROUP):
                finish(group * GROUP + member, block, part_of(here, member))
        return carry

    lax.fori_loop(0, groups, head_group, 0)


def project_body(
    info, normed, w_own, w_peer, queries, keys, values_t, keys_sent, values_sent
):
    rows = normed[...]
    for half, weight in enumerate((w_own, w_peer)):
        place = slice(half * HALF, (half + 1) * HALF)
        keys[:, place] = matmul(rows, weight[1]).astype(BF16)
        values_t[place, :] = matmul(rows, weight[2]).T.astype(BF16)
        queries[:, place] = (matmul(rows, weight[0]) * SCALE).astype(BF16)

    @pl.when(info[0] == 0)
    def _():
        for half in range(2):
            place = slice(half * HALF, (half + 1) * HALF)
            other = slice((1 - half) * HALF, (2 - half) * HALF)
            keys_sent[:, other] = keys[ROWS - WIN :, place]
            values_sent[other, :] = values_t[place, ROWS - WIN :]

    @pl.when(info[0] != 0)
    def _():
        for half in range(2):
            place = slice(half * HALF, (half + 1) * HALF)
            other = slice((1 - half) * HALF, (2 - half) * HALF)
            keys_sent[:, other] = keys[:WIN, place]
            values_sent[other, :] = values_t[place, :WIN]


def own_body(queries, keys, values_t, mask, sums, stats, first, second):
    eyes, lane = identity_pair()

    def score(pair, block, scores):
        begin = WIN - block * TILE
        score_block(
            queries[rows_of(block), lanes_of(pair)], lane, eyes, keys[:, lanes_of(pair)],
            mask[begin : begin + ROWS, :], scores,
        )

    def finish(pair, block, scores):
        top = column_top(scores)
        both, total = weigh(scores, top, values_t[lanes_of(pair), :])
        sums[lanes_of(pair), rows_of(block)] = both
        columns = slice(2 * block * TILE, 2 * (block + 1) * TILE)
        stats[pair, 0:1, columns] = top
        stats[pair, 1:2, columns] = total

    pipeline(score, finish, first, second)


def attend_body(
    info, halo, peer_keys, peer_values, queries, sums, stats, mask, w_own, w_peer,
    mesh_zero, out_own, out_peer, dec_own, dec_peer,
    projected,
    keys, values_t, masks, attended, dec_wide, first, second,
):
    core, first_device, last_device = info[0], info[4], info[5]
    dec_wide[...] = jnp.zeros_like(dec_wide)

    @pl.when(core == 0)
    def _():
        dec_wide[:C, :HALF] = dec_own[...].astype(F32)
        dec_wide[:C, HALF:] = dec_peer[...].astype(F32)
        keys[WIN:, :] = peer_keys[...]
        values_t[:, WIN:] = peer_values[...]

    @pl.when(core != 0)
    def _():
        dec_wide[:C, :HALF] = dec_peer[...].astype(F32)
        dec_wide[:C, HALF:] = dec_own[...].astype(F32)
        keys[:WIN, :] = peer_keys[...]
        values_t[:, :WIN] = peer_values[...]

    begin = pl.ds(pl.multiple_of(core * WIN, WIN), WIN)
    beside = halo[...]
    for half, weight in enumerate((w_own, w_peer)):
        place = slice(half * HALF, (half + 1) * HALF)
        keys[begin, place] = matmul(beside, weight[1]).astype(BF16)
        values_t[place, begin] = matmul(beside, weight[2]).T.astype(BF16)
    low = jnp.where(first_device == 1, MASKED, 0.0)
    high = jnp.where(last_device == 1, MASKED, 0.0)
    for block in range(TILES):
        below, above = WIN - block * TILE, SPAN - block * TILE
        if below > 0:
            masks[block, :below, :] = (mask[:below, :].astype(F32) + low).astype(BF16)
        if above < SPAN:
            masks[block, below:, :] = (mask[above:, :].astype(F32) + high).astype(BF16)
    eyes, lane = identity_pair()

    def score(pair, block, scores):
        seen = slice(block * TILE, block * TILE + WIN)
        score_block(
            queries[rows_of(block), lanes_of(pair)], lane, eyes, keys[seen, lanes_of(pair)],
            masks[block], scores,
        )

    def finish(pair, block, scores):
        seen = slice(block * TILE, block * TILE + WIN)
        columns = slice(2 * block * TILE, 2 * (block + 1) * TILE)
        old, sum_old = stats[pair, 0:1, columns], stats[pair, 1:2, columns]
        top = jnp.maximum(old, column_top(scores))
        both, total = weigh(scores, top, values_t[lanes_of(pair), seen])
        shrink = jnp.exp2(old - top)
        inverse = 1.0 / (sum_old * shrink + total)
        shrink = shrink * inverse
        before = sums[lanes_of(pair), rows_of(block)]
        result = jnp.concatenate([
            before[:64] * shrink[:, :TILE] + both[:64] * inverse[:, :TILE],
            before[64:] * shrink[:, TILE:] + both[64:] * inverse[:, TILE:],
        ], axis=0)
        attended[lanes_of(pair), rows_of(block)] = result.astype(BF16)

    pipeline(score, finish, first, second)
    term_own = matmul(attended[:HALF, :].T, out_own[...]).astype(BF16).astype(F32)
    term_peer = matmul(attended[HALF:, :].T, out_peer[...]).astype(BF16).astype(F32)
    mesh_one = (mesh_zero[...].astype(F32) + (term_own + term_peer)).astype(BF16)
    projected[...] = matmul_t(dec_wide[...].astype(BF16), mesh_one)[:C, :].astype(BF16)


def half_term(part, spread, place):
    rows = pl.ds(pl.multiple_of(place * ROWS, ROWS), ROWS)
    return matmul(part, spread[rows, :])


def spread_body(info, own, src, dst, weight, grid, spread, base, sources, tables, weights):
    core, mesh_base, row_base = info[0], info[6], info[7]
    sources[...] = src[...] - mesh_base
    weights[...] = weight[...].astype(F32)
    row_slots = lax.broadcasted_iota(jnp.int32, (TILE, LANES), 0)
    for tile in range(DEC_TILES):
        for part in range(DEC_ROUNDS):
            slot = slice(part * DEC_TILES + tile, part * DEC_TILES + tile + 1)
            target = dst[slot, :] - (row_base + tile * TILE)
            tables[rows_of(tile), rows_of(part)] = jnp.where(
                row_slots == target, weights[slot, :], 0.0
            ).astype(BF16)
    mesh_slots = lax.broadcasted_iota(jnp.int32, (ROWS, LANES), 0)

    def half(place, carry):
        begin = pl.multiple_of(place * ROWS, ROWS)
        for tile in range(DEC_TILES):
            picks = []
            for part in range(DEC_ROUNDS):
                slot = slice(part * DEC_TILES + tile, part * DEC_TILES + tile + 1)
                hit = mesh_slots == sources[slot, :] - begin
                picks.append(jnp.where(hit, 1.0, 0.0).astype(BF16))
            spread[pl.ds(begin, ROWS), rows_of(tile)] = matmul_t(
                jnp.concatenate(picks, axis=1), tables[rows_of(tile), :]
            ).astype(BF16)
        return carry

    lax.fori_loop(0, 6, half, 0)
    fields = grid[:, pl.ds(pl.multiple_of(core * GQ, GQ), GQ)].astype(F32)
    terms = half_term(own[0], spread, 2 + core) + half_term(own[1], spread, 3 - core)
    base[...] = fields + terms


def sent_body(info, sent, spread, base, total):
    core = info[0]
    total[...] = (
        base[...]
        + half_term(sent[0], spread, 5 * core)
        + half_term(sent[1], spread, 3 * core + 1)
    )


def decode_body(info, swapped_rows, spread, total, out):
    other = 1 - info[0]
    terms = half_term(swapped_rows[0], spread, 5 * other)
    terms = terms + half_term(swapped_rows[1], spread, 3 * other + 1)
    out[...] = (total[...] + terms).astype(BF16)


def swapped(value):
    return lax.ppermute(value, "mp", [(0, 1), (1, 0)])


def up_and_down(value):
    bands = lax.axis_size("band")
    pairs = [(2 * i, 2 * i + 2) for i in range(bands - 1)]
    pairs += [(2 * i + 3, 2 * i + 1) for i in range(bands - 1)]
    return lax.ppermute(value, ("band", "mp"), pairs)


def over_the_edge(value):
    bands = lax.axis_size("band")
    pairs = [(2 * i + 1, 2 * i + 2) for i in range(bands - 1)]
    pairs += [(j, i) for i, j in pairs]
    return lax.ppermute(value, ("band", "mp"), pairs)


def on_device(
    grid_fields, w_in, enc_src, enc_dst, enc_weight, enc_count, norm_gain, w_qkv, w_out_attn,
    offsets, w_decode, dec_src, dec_dst, dec_weight,
):
    band = lax.axis_index("band")
    core = lax.axis_index("mp")
    bands = lax.axis_size("band")
    device = 2 * band + core
    grid = grid_fields.T
    grid_sent = up_and_down(grid)
    info = jnp.stack([
        core,
        enc_count[0],
        (band - 1) * G_BAND,
        device * ROWS,
        (device == 0).astype(jnp.int32),
        (device == 2 * bands - 1).astype(jnp.int32),
        (band - 1) * 2 * ROWS,
        device * GQ,
    ]).astype(jnp.int32)
    win_peer = swapped(w_in)
    dec_own = w_decode.T
    dec_peer = swapped(dec_own)
    qkv_own = w_qkv.transpose(1, 0, 2)
    qkv_peer = swapped(qkv_own)
    out_peer = swapped(w_out_attn)
    edges = jax.ShapeDtypeStruct(enc_src.shape, jnp.int32)
    own_rows, mask, sources, targets, weights, gain, w_in_all = call(
        prepare_body,
        (info, offsets, grid, enc_src, enc_dst, enc_weight, norm_gain.reshape(1, D), w_in,
         win_peer),
        2,
        [
            jax.ShapeDtypeStruct((G_BAND, LANES), F32),
            jax.ShapeDtypeStruct((SPAN, TILE), BF16),
            edges,
            edges,
            jax.ShapeDtypeStruct(enc_weight.shape, F32),
            jax.ShapeDtypeStruct((1, D), F32),
            jax.ShapeDtypeStruct((LANES, D), BF16),
        ],
        [pltpu.VMEM((LANES, G_BAND), F32), pltpu.VMEM((LANES, D), F32)],
        8 * 10 ** 9, 2 * 10 ** 6, "prepare",
    )
    grid_sent, own_rows = lax.optimization_barrier((grid_sent, own_rows))
    grid_swapped = swapped(grid_sent)
    grid_rows = call(
        unpack_body,
        (info, own_rows, grid_sent),
        1,
        jax.ShapeDtypeStruct((3 * G_BAND, LANES), F32),
        [pltpu.VMEM((LANES, G_BAND), F32)],
        2 * 10 ** 9, 2 * 10 ** 6, "unpack",
    )
    _, mesh_zero, normed, to_band = call(
        encode_body,
        (info, sources, grid_rows, grid_swapped, w_in_all, targets, weights, gain),
        2,
        [jax.ShapeDtypeStruct((3 * G_BAND, LANES), F32)]
        + [jax.ShapeDtypeStruct((ROWS, D), BF16)] * 2
        + [jax.ShapeDtypeStruct((WIN, D), BF16)],
        [
            pltpu.VMEM((LANES, G_BAND), F32),
            pltpu.VMEM((STEP, LANES), F32),
            pltpu.VMEM((STEP, LANES), F32),
            pltpu.VMEM((ROWS, D), F32),
        ],
        8 * 10 ** 9, 4 * 10 ** 6, "encode", {2: 0},
    )
    halo_band = over_the_edge(to_band)
    queries, keys, values_t, keys_sent, values_sent = call(
        project_body,
        (info, normed, qkv_own, qkv_peer),
        1,
        [
            jax.ShapeDtypeStruct((ROWS, D), BF16),
            jax.ShapeDtypeStruct((ROWS, D), BF16),
            jax.ShapeDtypeStruct((D, ROWS), BF16),
            jax.ShapeDtypeStruct((WIN, D), BF16),
            jax.ShapeDtypeStruct((D, WIN), BF16),
        ],
        [],
        6 * 10 ** 9, 10 ** 7, "project",
    )
    peer_keys, peer_values = swapped(keys_sent), swapped(values_sent)
    sums, stats = call(
        own_body,
        (queries, keys, values_t, mask),
        0,
        [
            jax.ShapeDtypeStruct((D, ROWS), F32),
            jax.ShapeDtypeStruct((D // LANES, 8, 2 * ROWS), F32),
        ],
        [pltpu.VMEM((ROWS, 2 * GROUP * TILE), F32)] * 2,
        8 * 10 ** 9, 10 ** 7, "own",
    )
    projected = call(
        attend_body,
        (info, halo_band, peer_keys, peer_values, queries, sums, stats, mask, qkv_own,
         qkv_peer, mesh_zero, w_out_attn, out_peer, dec_own, dec_peer),
        1,
        jax.ShapeDtypeStruct((C, ROWS), BF16),
        [
            pltpu.VMEM((2 * WIN, D), BF16),
            pltpu.VMEM((D, 2 * WIN), BF16),
            pltpu.VMEM((TILES, WIN, TILE), BF16),
            pltpu.VMEM((D, ROWS), BF16),
            pltpu.VMEM((LANES, D), F32),
            pltpu.VMEM((WIN, 2 * GROUP * TILE), F32),
            pltpu.VMEM((WIN, 2 * GROUP * TILE), F32),
        ],
        10 ** 10, 2 * 10 ** 7, "attend",
    )
    own_pair = jnp.stack([projected, swapped(projected)])
    pair_sent = up_and_down(own_pair)
    spread, base = call(
        spread_body,
        (info, own_pair, dec_src, dec_dst, dec_weight, grid),
        1,
        [
            jax.ShapeDtypeStruct((6 * ROWS, GQ), BF16),
            jax.ShapeDtypeStruct((C, GQ), F32),
        ],
        [
            pltpu.VMEM(dec_src.shape, jnp.int32),
            pltpu.VMEM((GQ, DEC_ROUNDS * TILE), BF16),
            pltpu.VMEM(dec_weight.shape, F32),
        ],
        8 * 10 ** 9, 2 * 10 ** 6, "spread",
    )
    pair_sent, base = lax.optimization_barrier((pair_sent, base))
    pair_swapped = swapped(pair_sent)
    sums_out = jax.ShapeDtypeStruct((C, GQ), F32)
    total = call(
        sent_body, (info, pair_sent, spread, base), 1, sums_out, [],
        10 ** 9, 3 * 10 ** 6, "sent",
    )
    return call(
        decode_body, (info, pair_swapped, spread, total), 1,
        jax.ShapeDtypeStruct((C, GQ), BF16), [], 10 ** 9, 3 * 10 ** 6, "decode",
    ).T


def solution(mesh):
    return jax.shard_map(
        on_device,
        mesh=mesh,
        in_specs=(
            P("band", None),
            P(None, "mp"),
            P("band", None),
            P("band", None),
            P("band", None),
            P("band"),
            P(),
            P(None, None, "mp"),
            P("mp", None),
            P(),
            P("mp", None),
            P(("band", "mp"), None),
            P(("band", "mp"), None),
            P(("band", "mp"), None),
        ),
        out_specs=P(("band", "mp"), None),
        check_vma=False,
    )
```

```python
import math
import jax
import jax.numpy as jnp
from jax import lax
from jax.experimental import pallas as pl
from jax.experimental.pallas import tpu as pltpu
from jax.sharding import PartitionSpec as P

D = 1024
C = 100
LANES = 128
TILE = 128
ROWS = 512
WIN = 384
K_OFF = 32
HALF = 512
G_BAND = 2048
EDGE_ROUNDS = 8
TILES = 4
STEP = 512
SPAN = TILE + 2 * WIN
GQ = 1024
DEC_ROUNDS = 3
DEC_TILES = 8
GROUP = 2
MASKED = -1e30
SCALE = 64 ** (-0.5) * math.log2(math.e)
F32 = jnp.float32
BF16 = jnp.bfloat16
VMEM_BYTES = 20 * 1024 * 1024


def vmem():
    return pl.BlockSpec(memory_space=pltpu.VMEM)


def smem():
    return pl.BlockSpec(memory_space=pltpu.SMEM)


def call(body, operands, smem_count, outs, scratch, flops, touched, name, aliases={}):
    specs = [smem()] * smem_count + [vmem()] * (len(operands) - smem_count)
    return pl.pallas_call(
        body,
        out_shape=outs,
        in_specs=specs,
        out_specs=jax.tree.map(lambda _: vmem(), outs),
        scratch_shapes=scratch,
        compiler_params=pltpu.CompilerParams(vmem_limit_bytes=VMEM_BYTES),
        cost_estimate=pl.CostEstimate(flops=flops, bytes_accessed=touched, transcendentals=0),
        input_output_aliases=aliases,
        name=name,
    )(*operands)


def matmul(a, b):
    return jnp.dot(a, b, preferred_element_type=F32)


def matmul_t(a, b):
    return lax.dot_general(a, b, (((1,), (1,)), ((), ())), preferred_element_type=F32)


def to_rows(part, wide, rows, begin):
    wide[:C, :] = part[...].astype(F32)
    for block in range(G_BAND // LANES):
        columns = slice(block * LANES, (block + 1) * LANES)
        place = pl.multiple_of(begin + block * LANES, LANES)
        rows[pl.ds(place, LANES), :] = wide[:, columns].T


def by_core(core, wide, own, peer):
    @pl.when(core == 0)
    def _():
        wide[:C, :HALF] = own[...].astype(F32)
        wide[:C, HALF:] = peer[...].astype(F32)

    @pl.when(core != 0)
    def _():
        wide[:C, :HALF] = peer[...].astype(F32)
        wide[:C, HALF:] = own[...].astype(F32)


def turn_body(grid, own_rows, wide):
    wide[...] = jnp.zeros_like(wide)
    to_rows(grid, wide, own_rows, 0)


def prepare_body(
    info, offsets, own_rows, src, dst, weight, gain, win_own, win_peer, dec_own, dec_peer, w_out,
    mask, sources, targets, weights, gains, w_in, w_decode, fold,
    w_wide,
):
    core, live, mesh_base = info[0], info[1], info[3]
    w_wide[...] = jnp.zeros_like(w_wide)
    by_core(core, w_wide, win_own, win_peer)
    w_in[...] = (w_wide[...] * 0.5).astype(BF16)
    by_core(core, w_wide, dec_own, dec_peer)
    w_decode[...] = w_wide[...].astype(BF16)
    folded = matmul_t(w_decode[...], w_out[...])
    upper = folded.astype(BF16)
    fold[:LANES, :] = upper
    fold[LANES:, :] = (folded - upper.astype(F32)).astype(BF16)
    for chunk in range(SPAN // TILE):
        row = lax.broadcasted_iota(jnp.int32, (TILE, LANES), 0) + (chunk * TILE - WIN)
        away = row - lax.broadcasted_iota(jnp.int32, (TILE, LANES), 1)
        hit = away == offsets[0]
        for k in range(1, K_OFF):
            hit = hit | (away == offsets[k])
        mask[chunk * TILE : (chunk + 1) * TILE, :] = jnp.where(hit, 0.0, MASKED).astype(BF16)
    slots = lax.broadcasted_iota(jnp.int32, weights.shape, 0)
    weights[...] = jnp.where(slots < live, weight[...].astype(F32), 0.0)
    targets[...] = dst[...] - mesh_base
    sources[...] = src[...] - info[2]
    gains[...] = gain[...]


def unpack_body(info, own_rows, sent, rows, wide):
    wide[...] = jnp.zeros_like(wide)
    rows[G_BAND : 2 * G_BAND, :] = own_rows[...]
    to_rows(sent, wide, rows, info[0] * 2 * G_BAND)


def encode_tiles(
    core, order, src, w_in, targets, weights, gain, rows, mesh_zero, normed, first, second, total
):
    row_slots = lax.broadcasted_iota(jnp.int32, (TILE, LANES), 0)
    steps = EDGE_ROUNDS * TILE // STEP
    rounds = STEP // TILE
    count = len(order) * steps

    def tile_of(step):
        place = order[0] + step // steps
        return jnp.where(core == 0, place, TILES - 1 - place)

    def slot_of(step, part):
        return (step % steps * rounds + part) * 2 * TILES + core * TILES + tile_of(step)

    def gather(step, buffer):
        for part in range(rounds):
            slot = slot_of(step, part)
            for edge in range(TILE):
                index = src[slot, edge]
                buffer[pl.ds(part * TILE + edge, 1), :] = rows[pl.ds(index, 1), :]

    def add(step, buffer):
        tile = tile_of(step)
        half = matmul(buffer[...].astype(BF16), w_in[...])
        embedded = (half + half * jnp.tanh(half)).astype(BF16)
        tables = []
        for part in range(rounds):
            slot = slot_of(step, part)
            target = targets[pl.ds(slot, 1), :] - tile * TILE
            tables.append(jnp.where(row_slots == target, weights[pl.ds(slot, 1), :], 0.0))
        table = jnp.concatenate(tables, axis=1).astype(BF16)
        place = pl.ds(pl.multiple_of(tile * TILE, TILE), TILE)
        total[place, :] += matmul(table, embedded)

    for step in range(0, count, steps):
        place = pl.ds(pl.multiple_of(tile_of(step) * TILE, TILE), TILE)
        total[place, :] = jnp.zeros((TILE, D), F32)
    gather(0, first)

    def pair(index, carry):
        gather(2 * index + 1, second)
        add(2 * index, first)
        if count > 2:
            gather(jnp.minimum(2 * index + 2, count - 1), first)
        add(2 * index + 1, second)
        return carry

    lax.fori_loop(0, count // 2, pair, 0)

    def finish(step, carry):
        place = pl.ds(pl.multiple_of(tile_of(step * steps) * TILE, TILE), TILE)
        rounded = total[place, :].astype(BF16)
        mesh_zero[place, :] = rounded
        values = rounded.astype(F32)
        inverse = lax.rsqrt(jnp.mean(values * values, axis=1, keepdims=True) + 1e-05)
        normed[place, :] = (values * inverse * gain[...]).astype(BF16)
        return carry

    lax.fori_loop(0, len(order), finish, 0)


def encode_body(
    info, src, grid_rows, swapped_rows, w_in, targets, weights, gain,
    rows, mesh_zero, normed, to_band,
    wide, first, second, total,
):
    core = info[0]
    wide[...] = jnp.zeros_like(wide)
    to_rows(swapped_rows, wide, rows, (1 - core) * 2 * G_BAND)
    encode_tiles(
        core, range(TILES - 1), src, w_in, targets, weights, gain, rows, mesh_zero, normed,
        first, second, total,
    )
    to_band[...] = normed[pl.ds(pl.multiple_of(core * TILE, TILE), WIN), :]


def last_body(
    info, src, rows, w_in, targets, weights, gain, zero_in, normed_in,
    mesh_zero, normed,
    first, second, total,
):
    encode_tiles(
        info[0], range(TILES - 1, TILES), src, w_in, targets, weights, gain, rows, mesh_zero,
        normed, first, second, total,
    )


def identity_pair():
    row = lax.broadcasted_iota(jnp.int32, (TILE, LANES), 0)
    lane = lax.broadcasted_iota(jnp.int32, (TILE, LANES), 1)
    eye = jnp.where(row == lane, 1.0, 0.0).astype(BF16)
    return jnp.concatenate([eye, eye], axis=0), lane


def lanes_of(pair):
    return pl.ds(pl.multiple_of(pair * LANES, LANES), LANES)


def rows_of(block):
    return slice(block * TILE, (block + 1) * TILE)


def score_block(query, lane, eyes, keys, mask, scores):
    query = query.astype(F32)
    stacked = jnp.concatenate(
        [jnp.where(lane < 64, query, 0.0), jnp.where(lane < 64, 0.0, query)], axis=0
    ).astype(BF16)
    scores[...] = matmul_t(
        jnp.concatenate([keys, mask], axis=1), jnp.concatenate([stacked, eyes], axis=1)
    )


def column_top(scores):
    top = scores[:TILE, :]
    for begin in range(TILE, scores.shape[0], TILE):
        top = jnp.maximum(top, scores[begin : begin + TILE, :])
    return jnp.max(top, axis=0, keepdims=True)


def weigh(scores, top, values):
    expos = jnp.exp2(scores[...] - top).astype(BF16)
    ones = jnp.ones((16, scores.shape[0]), BF16)
    result = matmul(jnp.concatenate([values, ones], axis=0), expos)
    both = jnp.concatenate([result[:64, :TILE], result[64:TILE, TILE:]], axis=0)
    return both, result[TILE : TILE + 1, :]


def pipeline(score, finish, first, second):
    buffers = (first, second)
    groups = D // LANES // GROUP

    def part_of(buffer, member):
        return buffer.at[:, member * 2 * TILE : (member + 1) * 2 * TILE]

    for member in range(GROUP):
        score(member, 0, part_of(first, member))

    def head_group(group, carry):
        for block in range(TILES):
            here, ahead = buffers[block % 2], buffers[(block + 1) % 2]
            for member in range(GROUP):
                if block + 1 < TILES:
                    pair = group * GROUP + member
                else:
                    pair = jnp.minimum(group + 1, groups - 1) * GROUP + member
                score(pair, (block + 1) % TILES, part_of(ahead, member))
            for member in range(GROUP):
                finish(group * GROUP + member, block, part_of(here, member))
        return carry

    lax.fori_loop(0, groups, head_group, 0)


def project_body(
    info, normed, w_own, w_peer, mesh_zero, w_decode,
    queries, keys, values_t, keys_sent, values_sent, straight,
):
    rows = normed[...]
    straight[...] = matmul_t(w_decode[...], mesh_zero[...])
    for half, weight in enumerate((w_own, w_peer)):
        place = slice(half * HALF, (half + 1) * HALF)
        keys[:, place] = matmul(rows, weight[1]).astype(BF16)
        values_t[place, :] = matmul(rows, weight[2]).T.astype(BF16)
        queries[:, place] = (matmul(rows, weight[0]) * SCALE).astype(BF16)

    @pl.when(info[0] == 0)
    def _():
        for half in range(2):
            place = slice(half * HALF, (half + 1) * HALF)
            other = slice((1 - half) * HALF, (2 - half) * HALF)
            keys_sent[:, other] = keys[ROWS - WIN :, place]
            values_sent[other, :] = values_t[place, ROWS - WIN :]

    @pl.when(info[0] != 0)
    def _():
        for half in range(2):
            place = slice(half * HALF, (half + 1) * HALF)
            other = slice((1 - half) * HALF, (2 - half) * HALF)
            keys_sent[:, other] = keys[:WIN, place]
            values_sent[other, :] = values_t[place, :WIN]


def own_body(queries, keys, values_t, mask, sums, stats, first, second):
    eyes, lane = identity_pair()

    def score(pair, block, scores):
        begin = WIN - block * TILE
        score_block(
            queries[rows_of(block), lanes_of(pair)], lane, eyes, keys[:, lanes_of(pair)],
            mask[begin : begin + ROWS, :], scores,
        )

    def finish(pair, block, scores):
        top = column_top(scores)
        both, total = weigh(scores, top, values_t[lanes_of(pair), :])
        sums[lanes_of(pair), rows_of(block)] = both
        columns = slice(2 * block * TILE, 2 * (block + 1) * TILE)
        stats[pair, 0:1, columns] = top
        stats[pair, 1:2, columns] = total

    pipeline(score, finish, first, second)


def attend_body(
    info, halo, peer_keys, peer_values, queries, sums, stats, mask, w_own, w_peer,
    straight, fold_own, fold_peer,
    projected,
    keys, values_t, masks, attended, first, second,
):
    core, first_device, last_device = info[0], info[4], info[5]

    @pl.when(core == 0)
    def _():
        keys[WIN:, :] = peer_keys[...]
        values_t[:, WIN:] = peer_values[...]

    @pl.when(core != 0)
    def _():
        keys[:WIN, :] = peer_keys[...]
        values_t[:, :WIN] = peer_values[...]

    begin = pl.ds(pl.multiple_of(core * WIN, WIN), WIN)
    beside = halo[...]
    for half, weight in enumerate((w_own, w_peer)):
        place = slice(half * HALF, (half + 1) * HALF)
        keys[begin, place] = matmul(beside, weight[1]).astype(BF16)
        values_t[place, begin] = matmul(beside, weight[2]).T.astype(BF16)
    low = jnp.where(first_device == 1, MASKED, 0.0)
    high = jnp.where(last_device == 1, MASKED, 0.0)
    for block in range(TILES):
        below, above = WIN - block * TILE, SPAN - block * TILE
        if below > 0:
            masks[block, :below, :] = (mask[:below, :].astype(F32) + low).astype(BF16)
        if above < SPAN:
            masks[block, below:, :] = (mask[above:, :].astype(F32) + high).astype(BF16)
    eyes, lane = identity_pair()

    def score(pair, block, scores):
        seen = slice(block * TILE, block * TILE + WIN)
        score_block(
            queries[rows_of(block), lanes_of(pair)], lane, eyes, keys[seen, lanes_of(pair)],
            masks[block], scores,
        )

    def finish(pair, block, scores):
        seen = slice(block * TILE, block * TILE + WIN)
        columns = slice(2 * block * TILE, 2 * (block + 1) * TILE)
        old, sum_old = stats[pair, 0:1, columns], stats[pair, 1:2, columns]
        top = jnp.maximum(old, column_top(scores))
        both, total = weigh(scores, top, values_t[lanes_of(pair), seen])
        shrink = jnp.exp2(old - top)
        inverse = 1.0 / (sum_old * shrink + total)
        shrink = shrink * inverse
        before = sums[lanes_of(pair), rows_of(block)]
        result = jnp.concatenate([
            before[:64] * shrink[:, :TILE] + both[:64] * inverse[:, :TILE],
            before[64:] * shrink[:, TILE:] + both[64:] * inverse[:, TILE:],
        ], axis=0)
        attended[lanes_of(pair), rows_of(block)] = result.astype(BF16)

    pipeline(score, finish, first, second)
    both = matmul(fold_own[...], attended[:HALF, :]) + matmul(fold_peer[...], attended[HALF:, :])
    projected[...] = (straight[...] + both[:LANES, :] + both[LANES:, :])[:C, :].astype(BF16)


def half_term(part, spread, place):
    rows = pl.ds(pl.multiple_of(place * ROWS, ROWS), ROWS)
    return matmul(part, spread[rows, :])


def spread_body(info, own, src, dst, weight, grid, spread, base, sources, tables, weights):
    core, mesh_base, row_base = info[0], info[6], info[7]
    sources[...] = src[...] - mesh_base
    weights[...] = weight[...].astype(F32)
    row_slots = lax.broadcasted_iota(jnp.int32, (TILE, LANES), 0)
    for tile in range(DEC_TILES):
        for part in range(DEC_ROUNDS):
            slot = slice(part * DEC_TILES + tile, part * DEC_TILES + tile + 1)
            target = dst[slot, :] - (row_base + tile * TILE)
            tables[rows_of(tile), rows_of(part)] = jnp.where(
                row_slots == target, weights[slot, :], 0.0
            ).astype(BF16)
    mesh_slots = lax.broadcasted_iota(jnp.int32, (ROWS, LANES), 0)

    def half(place, carry):
        begin = pl.multiple_of(place * ROWS, ROWS)
        for tile in range(DEC_TILES):
            picks = []
            for part in range(DEC_ROUNDS):
                slot = slice(part * DEC_TILES + tile, part * DEC_TILES + tile + 1)
                hit = mesh_slots == sources[slot, :] - begin
                picks.append(jnp.where(hit, 1.0, 0.0).astype(BF16))
            spread[pl.ds(begin, ROWS), rows_of(tile)] = matmul_t(
                jnp.concatenate(picks, axis=1), tables[rows_of(tile), :]
            ).astype(BF16)
        return carry

    lax.fori_loop(0, 6, half, 0)
    fields = grid[:, pl.ds(pl.multiple_of(core * GQ, GQ), GQ)].astype(F32)
    terms = half_term(own[0], spread, 2 + core) + half_term(own[1], spread, 3 - core)
    base[...] = fields + terms


def sent_body(info, sent, spread, base, total):
    core = info[0]
    total[...] = (
        base[...]
        + half_term(sent[0], spread, 5 * core)
        + half_term(sent[1], spread, 3 * core + 1)
    )


def decode_body(info, swapped_rows, spread, total, out):
    other = 1 - info[0]
    terms = half_term(swapped_rows[0], spread, 5 * other)
    terms = terms + half_term(swapped_rows[1], spread, 3 * other + 1)
    out[...] = (total[...] + terms).astype(BF16)


def swapped(value):
    return lax.ppermute(value, "mp", [(0, 1), (1, 0)])


def up_and_down(value):
    bands = lax.axis_size("band")
    pairs = [(2 * i, 2 * i + 2) for i in range(bands - 1)]
    pairs += [(2 * i + 3, 2 * i + 1) for i in range(bands - 1)]
    return lax.ppermute(value, ("band", "mp"), pairs)


def over_the_edge(value):
    bands = lax.axis_size("band")
    pairs = [(2 * i + 1, 2 * i + 2) for i in range(bands - 1)]
    pairs += [(j, i) for i, j in pairs]
    return lax.ppermute(value, ("band", "mp"), pairs)


def on_device(
    grid_fields, w_in, enc_src, enc_dst, enc_weight, enc_count, norm_gain, w_qkv, w_out_attn,
    offsets, w_decode, dec_src, dec_dst, dec_weight,
):
    band = lax.axis_index("band")
    core = lax.axis_index("mp")
    bands = lax.axis_size("band")
    device = 2 * band + core
    grid = grid_fields.T
    grid_sent = up_and_down(grid)
    info = jnp.stack([
        core,
        enc_count[0],
        (band - 1) * G_BAND,
        device * ROWS,
        (device == 0).astype(jnp.int32),
        (device == 2 * bands - 1).astype(jnp.int32),
        (band - 1) * 2 * ROWS,
        device * GQ,
    ]).astype(jnp.int32)
    win_peer = swapped(w_in)
    dec_own = w_decode.T
    dec_peer = swapped(dec_own)
    qkv_own = w_qkv.transpose(1, 0, 2)
    qkv_peer = swapped(qkv_own)
    edges = jax.ShapeDtypeStruct(enc_src.shape, jnp.int32)
    own_rows = call(
        turn_body, (grid,), 0, jax.ShapeDtypeStruct((G_BAND, LANES), F32),
        [pltpu.VMEM((LANES, G_BAND), F32)], 5 * 10 ** 9, 2 * 10 ** 6, "turn",
    )
    mask, sources, targets, weights, gain, w_in_all, dec_all, fold_own = call(
        prepare_body,
        (info, offsets, own_rows, enc_src, enc_dst, enc_weight, norm_gain.reshape(1, D), w_in,
         win_peer, dec_own, dec_peer, w_out_attn),
        2,
        [
            jax.ShapeDtypeStruct((SPAN, TILE), BF16),
            edges,
            edges,
            jax.ShapeDtypeStruct(enc_weight.shape, F32),
            jax.ShapeDtypeStruct((1, D), F32),
            jax.ShapeDtypeStruct((LANES, D), BF16),
            jax.ShapeDtypeStruct((LANES, D), BF16),
            jax.ShapeDtypeStruct((2 * LANES, HALF), BF16),
        ],
        [pltpu.VMEM((LANES, D), F32)],
        8 * 10 ** 9, 2 * 10 ** 6, "prepare",
    )
    fold_peer = swapped(fold_own)
    grid_sent, own_rows, w_in_all = lax.optimization_barrier((grid_sent, own_rows, w_in_all))
    grid_swapped = swapped(grid_sent)
    grid_rows = call(
        unpack_body,
        (info, own_rows, grid_sent),
        1,
        jax.ShapeDtypeStruct((3 * G_BAND, LANES), F32),
        [pltpu.VMEM((LANES, G_BAND), F32)],
        2 * 10 ** 9, 2 * 10 ** 6, "unpack",
    )
    band_rows = jax.ShapeDtypeStruct((ROWS, D), BF16)
    step_buffers = [pltpu.VMEM((STEP, LANES), F32)] * 2 + [pltpu.VMEM((ROWS, D), F32)]
    grid_rows, mesh_zero, normed, to_band = call(
        encode_body,
        (info, sources, grid_rows, grid_swapped, w_in_all, targets, weights, gain),
        2,
        [
            jax.ShapeDtypeStruct((3 * G_BAND, LANES), F32),
            band_rows,
            band_rows,
            jax.ShapeDtypeStruct((WIN, D), BF16),
        ],
        [pltpu.VMEM((LANES, G_BAND), F32)] + step_buffers,
        7 * 10 ** 9, 4 * 10 ** 6, "encode", {2: 0},
    )
    halo_band = over_the_edge(to_band)
    mesh_zero, normed = call(
        last_body,
        (info, sources, grid_rows, w_in_all, targets, weights, gain, mesh_zero, normed),
        2,
        [band_rows, band_rows],
        step_buffers,
        3 * 10 ** 9, 4 * 10 ** 6, "last", {7: 0, 8: 1},
    )
    queries, keys, values_t, keys_sent, values_sent, straight = call(
        project_body,
        (info, normed, qkv_own, qkv_peer, mesh_zero, dec_all),
        1,
        [
            jax.ShapeDtypeStruct((ROWS, D), BF16),
            jax.ShapeDtypeStruct((ROWS, D), BF16),
            jax.ShapeDtypeStruct((D, ROWS), BF16),
            jax.ShapeDtypeStruct((WIN, D), BF16),
            jax.ShapeDtypeStruct((D, WIN), BF16),
            jax.ShapeDtypeStruct((LANES, ROWS), F32),
        ],
        [],
        6 * 10 ** 9, 10 ** 7, "project",
    )
    peer_keys, peer_values = swapped(keys_sent), swapped(values_sent)
    sums, stats = call(
        own_body,
        (queries, keys, values_t, mask),
        0,
        [
            jax.ShapeDtypeStruct((D, ROWS), F32),
            jax.ShapeDtypeStruct((D // LANES, 8, 2 * ROWS), F32),
        ],
        [pltpu.VMEM((ROWS, 2 * GROUP * TILE), F32)] * 2,
        8 * 10 ** 9, 10 ** 7, "own",
    )
    projected = call(
        attend_body,
        (info, halo_band, peer_keys, peer_values, queries, sums, stats, mask, qkv_own,
         qkv_peer, straight, fold_own, fold_peer),
        1,
        jax.ShapeDtypeStruct((C, ROWS), BF16),
        [
            pltpu.VMEM((2 * WIN, D), BF16),
            pltpu.VMEM((D, 2 * WIN), BF16),
            pltpu.VMEM((TILES, WIN, TILE), BF16),
            pltpu.VMEM((D, ROWS), BF16),
            pltpu.VMEM((WIN, 2 * GROUP * TILE), F32),
            pltpu.VMEM((WIN, 2 * GROUP * TILE), F32),
        ],
        10 ** 10, 2 * 10 ** 7, "attend",
    )
    own_pair = jnp.stack([projected, swapped(projected)])
    pair_sent = up_and_down(own_pair)
    spread, base = call(
        spread_body,
        (info, own_pair, dec_src, dec_dst, dec_weight, grid),
        1,
        [
            jax.ShapeDtypeStruct((6 * ROWS, GQ), BF16),
            jax.ShapeDtypeStruct((C, GQ), F32),
        ],
        [
            pltpu.VMEM(dec_src.shape, jnp.int32),
            pltpu.VMEM((GQ, DEC_ROUNDS * TILE), BF16),
            pltpu.VMEM(dec_weight.shape, F32),
        ],
        8 * 10 ** 9, 2 * 10 ** 6, "spread",
    )
    pair_sent, base = lax.optimization_barrier((pair_sent, base))
    pair_swapped = swapped(pair_sent)
    sums_out = jax.ShapeDtypeStruct((C, GQ), F32)
    total = call(
        sent_body, (info, pair_sent, spread, base), 1, sums_out, [],
        10 ** 9, 3 * 10 ** 6, "sent",
    )
    return call(
        decode_body, (info, pair_swapped, spread, total), 1,
        jax.ShapeDtypeStruct((C, GQ), BF16), [], 10 ** 9, 3 * 10 ** 6, "decode",
    ).T


def solution(mesh):
    return jax.shard_map(
        on_device,
        mesh=mesh,
        in_specs=(
            P("band", None),
            P(None, "mp"),
            P("band", None),
            P("band", None),
            P("band", None),
            P("band"),
            P(),
            P(None, None, "mp"),
            P("mp", None),
            P(),
            P("mp", None),
            P(("band", "mp"), None),
            P(("band", "mp"), None),
            P(("band", "mp"), None),
        ),
        out_specs=P(("band", "mp"), None),
        check_vma=False,
    )
```

```python
import math
import jax
import jax.numpy as jnp
from jax import lax
from jax.experimental import pallas as pl
from jax.experimental.pallas import tpu as pltpu
from jax.sharding import PartitionSpec as P

D = 1024
C = 100
LANES = 128
TILE = 128
ROWS = 512
WIN = 384
K_OFF = 32
HALF = 512
G_BAND = 2048
EDGE_ROUNDS = 8
TILES = 4
STEP = 512
SPAN = TILE + 2 * WIN
GQ = 1024
DEC_ROUNDS = 3
DEC_TILES = 8
GROUP = 2
EARLY = 3
MASKED = -1e30
SCALE = 64 ** (-0.5) * math.log2(math.e)
F32 = jnp.float32
BF16 = jnp.bfloat16
MIB = 1024 * 1024


def vmem():
    return pl.BlockSpec(memory_space=pltpu.VMEM)


def smem():
    return pl.BlockSpec(memory_space=pltpu.SMEM)


def call(body, operands, smem_count, outs, scratch, flops, room, name, aliases={}):
    specs = [smem()] * smem_count + [vmem()] * (len(operands) - smem_count)
    return pl.pallas_call(
        body,
        out_shape=outs,
        in_specs=specs,
        out_specs=jax.tree.map(lambda _: vmem(), outs),
        scratch_shapes=scratch,
        compiler_params=pltpu.CompilerParams(vmem_limit_bytes=room * MIB),
        cost_estimate=pl.CostEstimate(flops=flops, bytes_accessed=2 * 10 ** 6, transcendentals=0),
        input_output_aliases=aliases,
        name=name,
    )(*operands)


def matmul(a, b):
    return jnp.dot(a, b, preferred_element_type=F32)


def matmul_t(a, b):
    return lax.dot_general(a, b, (((1,), (1,)), ((), ())), preferred_element_type=F32)


def to_rows(part, wide, rows, begin):
    wide[:C, :] = part[...].astype(F32)
    for block in range(G_BAND // LANES):
        columns = slice(block * LANES, (block + 1) * LANES)
        place = pl.multiple_of(begin + block * LANES, LANES)
        rows[pl.ds(place, LANES), :] = wide[:, columns].T


def by_core(core, wide, own, peer):
    @pl.when(core == 0)
    def _():
        wide[:C, :HALF] = own[...].astype(F32)
        wide[:C, HALF:] = peer[...].astype(F32)

    @pl.when(core != 0)
    def _():
        wide[:C, :HALF] = peer[...].astype(F32)
        wide[:C, HALF:] = own[...].astype(F32)


def mask_body(offsets, mask):
    for chunk in range(SPAN // TILE):
        row = lax.broadcasted_iota(jnp.int32, (TILE, LANES), 0) + (chunk * TILE - WIN)
        away = row - lax.broadcasted_iota(jnp.int32, (TILE, LANES), 1)
        hit = away == offsets[0]
        for k in range(1, K_OFF):
            hit = hit | (away == offsets[k])
        mask[chunk * TILE : (chunk + 1) * TILE, :] = jnp.where(hit, 0.0, MASKED).astype(BF16)


def prepare_body(
    info, mask, src, dst, weight, gain, win_own, win_peer, dec_own, dec_peer,
    sources, targets, weights, gains, w_in, w_decode,
    w_wide,
):
    core, live, mesh_base = info[0], info[1], info[3]
    w_wide[...] = jnp.zeros_like(w_wide)
    by_core(core, w_wide, win_own, win_peer)
    w_in[...] = (w_wide[...] * 0.5).astype(BF16)
    by_core(core, w_wide, dec_own, dec_peer)
    w_decode[...] = w_wide[...].astype(BF16)
    slots = lax.broadcasted_iota(jnp.int32, weights.shape, 0)
    weights[...] = jnp.where(slots < live, weight[...].astype(F32), 0.0)
    targets[...] = dst[...] - mesh_base
    sources[...] = src[...] - info[2]
    gains[...] = gain[...]


def unpack_body(info, grid, sent, w_out, w_decode, rows, fold, wide):
    folded = matmul_t(w_decode[...], w_out[...])
    upper = folded.astype(BF16)
    fold[:LANES, :] = upper
    fold[LANES:, :] = (folded - upper.astype(F32)).astype(BF16)
    wide[...] = jnp.zeros_like(wide)
    to_rows(grid, wide, rows, G_BAND)
    to_rows(sent, wide, rows, info[0] * 2 * G_BAND)


def encode_tiles(
    core, order, src, w_in, targets, weights, gain, rows, mesh_zero, normed, first, second, total
):
    row_slots = lax.broadcasted_iota(jnp.int32, (TILE, LANES), 0)
    steps = EDGE_ROUNDS * TILE // STEP
    rounds = STEP // TILE
    count = len(order) * steps

    def tile_of(step):
        place = order[0] + step // steps
        return jnp.where(core == 0, place, TILES - 1 - place)

    def slot_of(step, part):
        return (step % steps * rounds + part) * 2 * TILES + core * TILES + tile_of(step)

    def gather(step, buffer):
        for part in range(rounds):
            slot = slot_of(step, part)
            for edge in range(TILE):
                index = src[slot, edge]
                buffer[pl.ds(part * TILE + edge, 1), :] = rows[pl.ds(index, 1), :]

    def add(step, buffer):
        tile = tile_of(step)
        half = matmul(buffer[...].astype(BF16), w_in[...])
        embedded = (half + half * jnp.tanh(half)).astype(BF16)
        tables = []
        for part in range(rounds):
            slot = slot_of(step, part)
            target = targets[pl.ds(slot, 1), :] - tile * TILE
            tables.append(jnp.where(row_slots == target, weights[pl.ds(slot, 1), :], 0.0))
        table = jnp.concatenate(tables, axis=1).astype(BF16)
        place = pl.ds(pl.multiple_of(tile * TILE, TILE), TILE)
        total[place, :] += matmul(table, embedded)

    for step in range(0, count, steps):
        place = pl.ds(pl.multiple_of(tile_of(step) * TILE, TILE), TILE)
        total[place, :] = jnp.zeros((TILE, D), F32)
    gather(0, first)

    def pair(index, carry):
        gather(2 * index + 1, second)
        add(2 * index, first)
        if count > 2:
            gather(jnp.minimum(2 * index + 2, count - 1), first)
        add(2 * index + 1, second)
        return carry

    lax.fori_loop(0, count // 2, pair, 0)

    def finish(step, carry):
        place = pl.ds(pl.multiple_of(tile_of(step * steps) * TILE, TILE), TILE)
        rounded = total[place, :].astype(BF16)
        mesh_zero[place, :] = rounded
        values = rounded.astype(F32)
        inverse = lax.rsqrt(jnp.mean(values * values, axis=1, keepdims=True) + 1e-05)
        normed[place, :] = (values * inverse * gain[...]).astype(BF16)
        return carry

    lax.fori_loop(0, len(order), finish, 0)


def encode_body(
    info, src, grid_rows, swapped_rows, w_in, targets, weights, gain,
    rows, mesh_zero, normed, to_band,
    wide, first, second, total,
):
    core = info[0]
    wide[...] = jnp.zeros_like(wide)
    to_rows(swapped_rows, wide, rows, (1 - core) * 2 * G_BAND)
    encode_tiles(
        core, range(TILES - 1), src, w_in, targets, weights, gain, rows, mesh_zero, normed,
        first, second, total,
    )
    to_band[...] = normed[pl.ds(pl.multiple_of(core * TILE, TILE), WIN), :]


def last_body(
    info, src, rows, w_in, targets, weights, gain, zero_in, normed_in,
    mesh_zero, normed,
    first, second, total,
):
    encode_tiles(
        info[0], range(TILES - 1, TILES), src, w_in, targets, weights, gain, rows, mesh_zero,
        normed, first, second, total,
    )


def identity_pair():
    row = lax.broadcasted_iota(jnp.int32, (TILE, LANES), 0)
    lane = lax.broadcasted_iota(jnp.int32, (TILE, LANES), 1)
    eye = jnp.where(row == lane, 1.0, 0.0).astype(BF16)
    return jnp.concatenate([eye, eye], axis=0), lane


def lanes_of(pair):
    return pl.ds(pl.multiple_of(pair * LANES, LANES), LANES)


def rows_of(block):
    return slice(block * TILE, (block + 1) * TILE)


def score_block(query, lane, eyes, keys, mask, scores):
    query = query.astype(F32)
    stacked = jnp.concatenate(
        [jnp.where(lane < 64, query, 0.0), jnp.where(lane < 64, 0.0, query)], axis=0
    ).astype(BF16)
    scores[...] = matmul_t(
        jnp.concatenate([keys, mask], axis=1), jnp.concatenate([stacked, eyes], axis=1)
    )


def column_top(scores):
    top = scores[:TILE, :]
    for begin in range(TILE, scores.shape[0], TILE):
        top = jnp.maximum(top, scores[begin : begin + TILE, :])
    return jnp.max(top, axis=0, keepdims=True)


def weigh(scores, top, values):
    expos = jnp.exp2(scores[...] - top).astype(BF16)
    ones = jnp.ones((16, scores.shape[0]), BF16)
    result = matmul(jnp.concatenate([values, ones], axis=0), expos)
    both = jnp.concatenate([result[:64, :TILE], result[64:TILE, TILE:]], axis=0)
    return both, result[TILE : TILE + 1, :]


def pipeline(score, finish, first, second):
    buffers = (first, second)
    groups = D // LANES // GROUP

    def part_of(buffer, member):
        return buffer.at[:, member * 2 * TILE : (member + 1) * 2 * TILE]

    for member in range(GROUP):
        score(member, 0, part_of(first, member))

    def head_group(group, carry):
        for block in range(TILES):
            here, ahead = buffers[block % 2], buffers[(block + 1) % 2]
            for member in range(GROUP):
                if block + 1 < TILES:
                    pair = group * GROUP + member
                else:
                    pair = jnp.minimum(group + 1, groups - 1) * GROUP + member
                score(pair, (block + 1) % TILES, part_of(ahead, member))
            for member in range(GROUP):
                finish(group * GROUP + member, block, part_of(here, member))
        return carry

    lax.fori_loop(0, groups, head_group, 0)


def project_body(
    info, normed, w_own, w_peer, mesh_zero, w_decode,
    queries, keys, values_t, keys_sent, values_sent, straight,
):
    rows = normed[...]
    straight[...] = matmul_t(w_decode[...], mesh_zero[...])
    for half, weight in enumerate((w_own, w_peer)):
        place = slice(half * HALF, (half + 1) * HALF)
        keys[:, place] = matmul(rows, weight[1]).astype(BF16)
        values_t[place, :] = matmul(rows, weight[2]).T.astype(BF16)
        queries[:, place] = (matmul(rows, weight[0]) * SCALE).astype(BF16)

    @pl.when(info[0] == 0)
    def _():
        for half in range(2):
            place = slice(half * HALF, (half + 1) * HALF)
            other = slice((1 - half) * HALF, (2 - half) * HALF)
            keys_sent[:, other] = keys[ROWS - WIN :, place]
            values_sent[other, :] = values_t[place, ROWS - WIN :]

    @pl.when(info[0] != 0)
    def _():
        for half in range(2):
            place = slice(half * HALF, (half + 1) * HALF)
            other = slice((1 - half) * HALF, (2 - half) * HALF)
            keys_sent[:, other] = keys[:WIN, place]
            values_sent[other, :] = values_t[place, :WIN]


def own_body(queries, keys, values_t, mask, sums, stats, first, second):
    eyes, lane = identity_pair()

    def score(pair, block, scores):
        begin = WIN - block * TILE
        score_block(
            queries[rows_of(block), lanes_of(pair)], lane, eyes, keys[:, lanes_of(pair)],
            mask[begin : begin + ROWS, :], scores,
        )

    def finish(pair, block, scores):
        top = column_top(scores)
        both, total = weigh(scores, top, values_t[lanes_of(pair), :])
        sums[lanes_of(pair), rows_of(block)] = both
        columns = slice(2 * block * TILE, 2 * (block + 1) * TILE)
        stats[pair, 0:1, columns] = top
        stats[pair, 1:2, columns] = total

    pipeline(score, finish, first, second)


def attend_body(
    info, halo, peer_keys, peer_values, queries, sums, stats, mask, w_own, w_peer,
    straight, fold_own, fold_peer,
    projected,
    keys, values_t, masks, attended, first, second,
):
    core, first_device, last_device = info[0], info[4], info[5]

    @pl.when(core == 0)
    def _():
        keys[WIN:, :] = peer_keys[...]
        values_t[:, WIN:] = peer_values[...]

    @pl.when(core != 0)
    def _():
        keys[:WIN, :] = peer_keys[...]
        values_t[:, :WIN] = peer_values[...]

    begin = pl.ds(pl.multiple_of(core * WIN, WIN), WIN)
    beside = halo[...]
    for half, weight in enumerate((w_own, w_peer)):
        place = slice(half * HALF, (half + 1) * HALF)
        keys[begin, place] = matmul(beside, weight[1]).astype(BF16)
        values_t[place, begin] = matmul(beside, weight[2]).T.astype(BF16)
    low = jnp.where(first_device == 1, MASKED, 0.0)
    high = jnp.where(last_device == 1, MASKED, 0.0)
    for block in range(TILES):
        below, above = WIN - block * TILE, SPAN - block * TILE
        if below > 0:
            masks[block, :below, :] = (mask[:below, :].astype(F32) + low).astype(BF16)
        if above < SPAN:
            masks[block, below:, :] = (mask[above:, :].astype(F32) + high).astype(BF16)
    eyes, lane = identity_pair()

    def score(pair, block, scores):
        seen = slice(block * TILE, block * TILE + WIN)
        score_block(
            queries[rows_of(block), lanes_of(pair)], lane, eyes, keys[seen, lanes_of(pair)],
            masks[block], scores,
        )

    def finish(pair, block, scores):
        seen = slice(block * TILE, block * TILE + WIN)
        columns = slice(2 * block * TILE, 2 * (block + 1) * TILE)
        old, sum_old = stats[pair, 0:1, columns], stats[pair, 1:2, columns]
        top = jnp.maximum(old, column_top(scores))
        both, total = weigh(scores, top, values_t[lanes_of(pair), seen])
        shrink = jnp.exp2(old - top)
        inverse = 1.0 / (sum_old * shrink + total)
        shrink = shrink * inverse
        before = sums[lanes_of(pair), rows_of(block)]
        result = jnp.concatenate([
            before[:64] * shrink[:, :TILE] + both[:64] * inverse[:, :TILE],
            before[64:] * shrink[:, TILE:] + both[64:] * inverse[:, TILE:],
        ], axis=0)
        attended[lanes_of(pair), rows_of(block)] = result.astype(BF16)

    pipeline(score, finish, first, second)
    both = matmul(fold_own[...], attended[:HALF, :]) + matmul(fold_peer[...], attended[HALF:, :])
    projected[...] = (straight[...] + both[:LANES, :] + both[LANES:, :])[:C, :].astype(BF16)


def half_term(part, spread, place):
    rows = pl.ds(pl.multiple_of(place * ROWS, ROWS), ROWS)
    return matmul(part, spread[rows, :])


def spread_halves(info, src, dst, weight, spread, sources, tables, weights, places):
    mesh_base, row_base = info[6], info[7]
    sources[...] = src[...] - mesh_base
    weights[...] = weight[...].astype(F32)
    row_slots = lax.broadcasted_iota(jnp.int32, (TILE, LANES), 0)
    for tile in range(DEC_TILES):
        for part in range(DEC_ROUNDS):
            slot = slice(part * DEC_TILES + tile, part * DEC_TILES + tile + 1)
            target = dst[slot, :] - (row_base + tile * TILE)
            tables[rows_of(tile), rows_of(part)] = jnp.where(
                row_slots == target, weights[slot, :], 0.0
            ).astype(BF16)
    mesh_slots = lax.broadcasted_iota(jnp.int32, (ROWS, LANES), 0)

    def half(place, carry):
        begin = pl.multiple_of(place * ROWS, ROWS)
        for tile in range(DEC_TILES):
            picks = []
            for part in range(DEC_ROUNDS):
                slot = slice(part * DEC_TILES + tile, part * DEC_TILES + tile + 1)
                hit = mesh_slots == sources[slot, :] - begin
                picks.append(jnp.where(hit, 1.0, 0.0).astype(BF16))
            spread[pl.ds(begin, ROWS), rows_of(tile)] = matmul_t(
                jnp.concatenate(picks, axis=1), tables[rows_of(tile), :]
            ).astype(BF16)
        return carry

    lax.fori_loop(places[0], places[-1] + 1, half, 0)


def early_body(info, w_in, src, dst, weight, spread, sources, tables, weights):
    spread_halves(info, src, dst, weight, spread, sources, tables, weights, range(EARLY))


def spread_body(
    info, spread_in, own, src, dst, weight, grid, spread, base, sources, tables, weights
):
    core = info[0]
    spread_halves(info, src, dst, weight, spread, sources, tables, weights, range(EARLY, 6))
    fields = grid[:, pl.ds(pl.multiple_of(core * GQ, GQ), GQ)].astype(F32)
    terms = half_term(own[0], spread, 2 + core) + half_term(own[1], spread, 3 - core)
    base[...] = fields + terms


def sent_body(info, sent, spread, base, total):
    core = info[0]
    total[...] = (
        base[...]
        + half_term(sent[0], spread, 5 * core)
        + half_term(sent[1], spread, 3 * core + 1)
    )


def decode_body(info, swapped_rows, spread, total, out):
    other = 1 - info[0]
    terms = half_term(swapped_rows[0], spread, 5 * other)
    terms = terms + half_term(swapped_rows[1], spread, 3 * other + 1)
    out[...] = (total[...] + terms).astype(BF16)


def swapped(value):
    return lax.ppermute(value, "mp", [(0, 1), (1, 0)])


def up_and_down(value):
    bands = lax.axis_size("band")
    pairs = [(2 * i, 2 * i + 2) for i in range(bands - 1)]
    pairs += [(2 * i + 3, 2 * i + 1) for i in range(bands - 1)]
    return lax.ppermute(value, ("band", "mp"), pairs)


def over_the_edge(value):
    bands = lax.axis_size("band")
    pairs = [(2 * i + 1, 2 * i + 2) for i in range(bands - 1)]
    pairs += [(j, i) for i, j in pairs]
    return lax.ppermute(value, ("band", "mp"), pairs)


def on_device(
    grid_fields, w_in, enc_src, enc_dst, enc_weight, enc_count, norm_gain, w_qkv, w_out_attn,
    offsets, w_decode, dec_src, dec_dst, dec_weight,
):
    band = lax.axis_index("band")
    core = lax.axis_index("mp")
    bands = lax.axis_size("band")
    device = 2 * band + core
    grid = grid_fields.T
    grid_sent = up_and_down(grid)
    info = jnp.stack([
        core,
        enc_count[0],
        (band - 1) * G_BAND,
        device * ROWS,
        (device == 0).astype(jnp.int32),
        (device == 2 * bands - 1).astype(jnp.int32),
        (band - 1) * 2 * ROWS,
        device * GQ,
    ]).astype(jnp.int32)
    win_peer = swapped(w_in)
    dec_own = w_decode.T
    dec_peer = swapped(dec_own)
    qkv_own = w_qkv.transpose(1, 0, 2)
    qkv_peer = swapped(qkv_own)
    edges = jax.ShapeDtypeStruct(enc_src.shape, jnp.int32)
    mask = call(
        mask_body, (offsets,), 1, jax.ShapeDtypeStruct((SPAN, TILE), BF16), [],
        5 * 10 ** 9, 4, "mask",
    )
    sources, targets, weights, gain, w_in_all, dec_all = call(
        prepare_body,
        (info, mask, enc_src, enc_dst, enc_weight, norm_gain.reshape(1, D), w_in, win_peer,
         dec_own, dec_peer),
        1,
        [
            edges,
            edges,
            jax.ShapeDtypeStruct(enc_weight.shape, F32),
            jax.ShapeDtypeStruct((1, D), F32),
            jax.ShapeDtypeStruct((LANES, D), BF16),
            jax.ShapeDtypeStruct((LANES, D), BF16),
        ],
        [pltpu.VMEM((LANES, D), F32)],
        5 * 10 ** 9, 6, "prepare",
    )
    spread_out = jax.ShapeDtypeStruct((6 * ROWS, GQ), BF16)
    spread_scratch = [
        pltpu.VMEM(dec_src.shape, jnp.int32),
        pltpu.VMEM((GQ, DEC_ROUNDS * TILE), BF16),
        pltpu.VMEM(dec_weight.shape, F32),
    ]
    spread = call(
        early_body, (info, w_in_all, dec_src, dec_dst, dec_weight), 1, spread_out,
        spread_scratch, 5 * 10 ** 9, 10, "early",
    )
    grid_sent, w_in_all, spread = lax.optimization_barrier((grid_sent, w_in_all, spread))
    grid_swapped = swapped(grid_sent)
    grid_rows, fold_own = call(
        unpack_body,
        (info, grid, grid_sent, w_out_attn, dec_all),
        1,
        [
            jax.ShapeDtypeStruct((3 * G_BAND, LANES), F32),
            jax.ShapeDtypeStruct((2 * LANES, HALF), BF16),
        ],
        [pltpu.VMEM((LANES, G_BAND), F32)],
        2 * 10 ** 9, 6, "unpack",
    )
    fold_peer = swapped(fold_own)
    band_rows = jax.ShapeDtypeStruct((ROWS, D), BF16)
    step_buffers = [pltpu.VMEM((STEP, LANES), F32)] * 2 + [pltpu.VMEM((ROWS, D), F32)]
    grid_rows, mesh_zero, normed, to_band = call(
        encode_body,
        (info, sources, grid_rows, grid_swapped, w_in_all, targets, weights, gain),
        2,
        [
            jax.ShapeDtypeStruct((3 * G_BAND, LANES), F32),
            band_rows,
            band_rows,
            jax.ShapeDtypeStruct((WIN, D), BF16),
        ],
        [pltpu.VMEM((LANES, G_BAND), F32)] + step_buffers,
        7 * 10 ** 9, 14, "encode", {2: 0},
    )
    halo_band = over_the_edge(to_band)
    mesh_zero, normed = call(
        last_body,
        (info, sources, grid_rows, w_in_all, targets, weights, gain, mesh_zero, normed),
        2,
        [band_rows, band_rows],
        step_buffers,
        3 * 10 ** 9, 14, "last", {7: 0, 8: 1},
    )
    queries, keys, values_t, keys_sent, values_sent, straight = call(
        project_body,
        (info, normed, qkv_own, qkv_peer, mesh_zero, dec_all),
        1,
        [
            jax.ShapeDtypeStruct((ROWS, D), BF16),
            jax.ShapeDtypeStruct((ROWS, D), BF16),
            jax.ShapeDtypeStruct((D, ROWS), BF16),
            jax.ShapeDtypeStruct((WIN, D), BF16),
            jax.ShapeDtypeStruct((D, WIN), BF16),
            jax.ShapeDtypeStruct((LANES, ROWS), F32),
        ],
        [],
        6 * 10 ** 9, 10, "project",
    )
    peer_keys, peer_values = swapped(keys_sent), swapped(values_sent)
    sums, stats = call(
        own_body,
        (queries, keys, values_t, mask),
        0,
        [
            jax.ShapeDtypeStruct((D, ROWS), F32),
            jax.ShapeDtypeStruct((D // LANES, 8, 2 * ROWS), F32),
        ],
        [pltpu.VMEM((ROWS, 2 * GROUP * TILE), F32)] * 2,
        8 * 10 ** 9, 12, "own",
    )
    projected = call(
        attend_body,
        (info, halo_band, peer_keys, peer_values, queries, sums, stats, mask, qkv_own,
         qkv_peer, straight, fold_own, fold_peer),
        1,
        jax.ShapeDtypeStruct((C, ROWS), BF16),
        [
            pltpu.VMEM((2 * WIN, D), BF16),
            pltpu.VMEM((D, 2 * WIN), BF16),
            pltpu.VMEM((TILES, WIN, TILE), BF16),
            pltpu.VMEM((D, ROWS), BF16),
            pltpu.VMEM((WIN, 2 * GROUP * TILE), F32),
            pltpu.VMEM((WIN, 2 * GROUP * TILE), F32),
        ],
        10 ** 10, 16, "attend",
    )
    own_pair = jnp.stack([projected, swapped(projected)])
    pair_sent = up_and_down(own_pair)
    spread, base = call(
        spread_body,
        (info, spread, own_pair, dec_src, dec_dst, dec_weight, grid),
        1,
        [spread_out, jax.ShapeDtypeStruct((C, GQ), F32)],
        spread_scratch, 8 * 10 ** 9, 10, "spread", {1: 0},
    )
    pair_sent, base = lax.optimization_barrier((pair_sent, base))
    pair_swapped = swapped(pair_sent)
    sums_out = jax.ShapeDtypeStruct((C, GQ), F32)
    total = call(
        sent_body, (info, pair_sent, spread, base), 1, sums_out, [],
        10 ** 9, 6, "sent",
    )
    return call(
        decode_body, (info, pair_swapped, spread, total), 1,
        jax.ShapeDtypeStruct((C, GQ), BF16), [], 10 ** 9, 6, "decode",
    ).T


def solution(mesh):
    return jax.shard_map(
        on_device,
        mesh=mesh,
        in_specs=(
            P("band", None),
            P(None, "mp"),
            P("band", None),
            P("band", None),
            P("band", None),
            P("band"),
            P(),
            P(None, None, "mp"),
            P("mp", None),
            P(),
            P("mp", None),
            P(("band", "mp"), None),
            P(("band", "mp"), None),
            P(("band", "mp"), None),
        ),
        out_specs=P(("band", "mp"), None),
        check_vma=False,
    )
```

```python
import math
import jax
import jax.numpy as jnp
from jax import lax
from jax.experimental import pallas as pl
from jax.experimental.pallas import tpu as pltpu
from jax.sharding import PartitionSpec as P

D = 1024
C = 100
LANES = 128
TILE = 128
ROWS = 512
WIN = 384
K_OFF = 32
HALF = 512
G_BAND = 2048
EDGE_ROUNDS = 8
TILES = 4
STEP = 512
SPAN = TILE + 2 * WIN
GQ = 1024
DEC_ROUNDS = 3
DEC_TILES = 8
GROUP = 2
EARLY = 3
MASKED = -1e30
SCALE = 64 ** (-0.5) * math.log2(math.e)
F32 = jnp.float32
BF16 = jnp.bfloat16
MIB = 1024 * 1024


def vmem():
    return pl.BlockSpec(memory_space=pltpu.VMEM)


def smem():
    return pl.BlockSpec(memory_space=pltpu.SMEM)


def call(body, operands, smem_count, outs, scratch, flops, room, name, aliases={}):
    specs = [smem()] * smem_count + [vmem()] * (len(operands) - smem_count)
    return pl.pallas_call(
        body,
        out_shape=outs,
        in_specs=specs,
        out_specs=jax.tree.map(lambda _: vmem(), outs),
        scratch_shapes=scratch,
        compiler_params=pltpu.CompilerParams(vmem_limit_bytes=room * MIB),
        cost_estimate=pl.CostEstimate(flops=flops, bytes_accessed=2 * 10 ** 6, transcendentals=0),
        input_output_aliases=aliases,
        name=name,
    )(*operands)


def matmul(a, b):
    return jnp.dot(a, b, preferred_element_type=F32)


def matmul_t(a, b):
    return lax.dot_general(a, b, (((1,), (1,)), ((), ())), preferred_element_type=F32)


def to_rows(part, wide, rows, begin):
    wide[:C, :] = part[...].astype(F32)
    for block in range(G_BAND // LANES):
        columns = slice(block * LANES, (block + 1) * LANES)
        place = pl.multiple_of(begin + block * LANES, LANES)
        rows[pl.ds(place, LANES), :] = wide[:, columns].T


def by_core(core, wide, own, peer):
    @pl.when(core == 0)
    def _():
        wide[:C, :HALF] = own[...].astype(F32)
        wide[:C, HALF:] = peer[...].astype(F32)

    @pl.when(core != 0)
    def _():
        wide[:C, :HALF] = peer[...].astype(F32)
        wide[:C, HALF:] = own[...].astype(F32)


def mask_body(offsets, mask, token, strip, mask_wide):
    lane = lax.broadcasted_iota(jnp.int32, strip.shape, 1)
    away = lax.broadcasted_iota(jnp.int32, strip.shape, 0) + (SPAN - WIN - 8) - lane
    hit = away == offsets[0]
    for k in range(1, K_OFF):
        hit = hit | (away == offsets[k])
    strip[...] = jnp.where(hit, 0.0, MASKED)
    for begin in range(0, SPAN, 8):
        shift = SPAN - 8 - begin
        mask_wide[begin : begin + 8, :] = strip[:, shift : shift + TILE]
    mask[...] = mask_wide[...].astype(BF16)
    token[...] = jnp.zeros_like(token)


def prepare_body(
    info, token, src, dst, weight, gain, win_own, win_peer, dec_own, dec_peer,
    sources, targets, weights, gains, w_in, w_decode,
    w_wide,
):
    core, live, mesh_base = info[0], info[1], info[3]
    w_wide[...] = jnp.zeros_like(w_wide)
    by_core(core, w_wide, win_own, win_peer)
    w_in[...] = (w_wide[...] * 0.5).astype(BF16)
    by_core(core, w_wide, dec_own, dec_peer)
    w_decode[...] = w_wide[...].astype(BF16)
    slots = lax.broadcasted_iota(jnp.int32, weights.shape, 0)
    weights[...] = jnp.where(slots < live, weight[...].astype(F32), 0.0)
    targets[...] = dst[...] - mesh_base
    sources[...] = src[...] - info[2]
    gains[...] = gain[...]


def unpack_body(info, grid, sent, w_out, w_decode, rows, fold, wide):
    folded = matmul_t(w_decode[...], w_out[...])
    upper = folded.astype(BF16)
    fold[:LANES, :] = upper
    fold[LANES:, :] = (folded - upper.astype(F32)).astype(BF16)
    wide[...] = jnp.zeros_like(wide)
    to_rows(grid, wide, rows, G_BAND)
    to_rows(sent, wide, rows, info[0] * 2 * G_BAND)


def encode_tiles(
    core, order, src, w_in, targets, weights, gain, rows, mesh_zero, normed, first, second, total
):
    row_slots = lax.broadcasted_iota(jnp.int32, (TILE, LANES), 0)
    steps = EDGE_ROUNDS * TILE // STEP
    rounds = STEP // TILE
    count = len(order) * steps

    def tile_of(step):
        place = order[0] + step // steps
        return jnp.where(core == 0, place, TILES - 1 - place)

    def slot_of(step, part):
        return (step % steps * rounds + part) * 2 * TILES + core * TILES + tile_of(step)

    def gather(step, buffer):
        for part in range(rounds):
            slot = slot_of(step, part)
            for edge in range(TILE):
                index = src[slot, edge]
                buffer[pl.ds(part * TILE + edge, 1), :] = rows[pl.ds(index, 1), :]

    def add(step, buffer):
        tile = tile_of(step)
        half = matmul(buffer[...].astype(BF16), w_in[...])
        embedded = (half + half * jnp.tanh(half)).astype(BF16)
        tables = []
        for part in range(rounds):
            slot = slot_of(step, part)
            target = targets[pl.ds(slot, 1), :] - tile * TILE
            tables.append(jnp.where(row_slots == target, weights[pl.ds(slot, 1), :], 0.0))
        table = jnp.concatenate(tables, axis=1).astype(BF16)
        place = pl.ds(pl.multiple_of(tile * TILE, TILE), TILE)
        total[place, :] += matmul(table, embedded)

    for step in range(0, count, steps):
        place = pl.ds(pl.multiple_of(tile_of(step) * TILE, TILE), TILE)
        total[place, :] = jnp.zeros((TILE, D), F32)
    gather(0, first)

    def pair(index, carry):
        gather(2 * index + 1, second)
        add(2 * index, first)
        if count > 2:
            gather(jnp.minimum(2 * index + 2, count - 1), first)
        add(2 * index + 1, second)
        return carry

    lax.fori_loop(0, count // 2, pair, 0)

    def finish(step, carry):
        place = pl.ds(pl.multiple_of(tile_of(step * steps) * TILE, TILE), TILE)
        rounded = total[place, :].astype(BF16)
        mesh_zero[place, :] = rounded
        values = rounded.astype(F32)
        inverse = lax.rsqrt(jnp.mean(values * values, axis=1, keepdims=True) + 1e-05)
        normed[place, :] = (values * inverse * gain[...]).astype(BF16)
        return carry

    lax.fori_loop(0, len(order), finish, 0)


def encode_body(
    info, src, grid_rows, swapped_rows, w_in, targets, weights, gain,
    rows, mesh_zero, normed, to_band,
    wide, first, second, total,
):
    core = info[0]
    wide[...] = jnp.zeros_like(wide)
    to_rows(swapped_rows, wide, rows, (1 - core) * 2 * G_BAND)
    encode_tiles(
        core, range(TILES - 1), src, w_in, targets, weights, gain, rows, mesh_zero, normed,
        first, second, total,
    )
    to_band[...] = normed[pl.ds(pl.multiple_of(core * TILE, TILE), WIN), :]


def last_body(
    info, src, rows, w_in, targets, weights, gain, zero_in, normed_in,
    mesh_zero, normed,
    first, second, total,
):
    encode_tiles(
        info[0], range(TILES - 1, TILES), src, w_in, targets, weights, gain, rows, mesh_zero,
        normed, first, second, total,
    )


def identity_pair():
    row = lax.broadcasted_iota(jnp.int32, (TILE, LANES), 0)
    lane = lax.broadcasted_iota(jnp.int32, (TILE, LANES), 1)
    eye = jnp.where(row == lane, 1.0, 0.0).astype(BF16)
    return jnp.concatenate([eye, eye], axis=0), lane


def lanes_of(pair):
    return pl.ds(pl.multiple_of(pair * LANES, LANES), LANES)


def rows_of(block):
    return slice(block * TILE, (block + 1) * TILE)


def score_block(query, lane, eyes, keys, mask, scores):
    query = query.astype(F32)
    stacked = jnp.concatenate(
        [jnp.where(lane < 64, query, 0.0), jnp.where(lane < 64, 0.0, query)], axis=0
    ).astype(BF16)
    scores[...] = matmul_t(
        jnp.concatenate([keys, mask], axis=1), jnp.concatenate([stacked, eyes], axis=1)
    )


def column_top(scores):
    top = scores[:TILE, :]
    for begin in range(TILE, scores.shape[0], TILE):
        top = jnp.maximum(top, scores[begin : begin + TILE, :])
    return jnp.max(top, axis=0, keepdims=True)


def weigh(scores, top, values):
    expos = jnp.exp2(scores[...] - top).astype(BF16)
    ones = jnp.ones((16, scores.shape[0]), BF16)
    result = matmul(jnp.concatenate([values, ones], axis=0), expos)
    both = jnp.concatenate([result[:64, :TILE], result[64:TILE, TILE:]], axis=0)
    return both, result[TILE : TILE + 1, :]


def pipeline(score, finish, first, second):
    buffers = (first, second)
    groups = D // LANES // GROUP

    def part_of(buffer, member):
        return buffer.at[:, member * 2 * TILE : (member + 1) * 2 * TILE]

    for member in range(GROUP):
        score(member, 0, part_of(first, member))

    def head_group(group, carry):
        for block in range(TILES):
            here, ahead = buffers[block % 2], buffers[(block + 1) % 2]
            for member in range(GROUP):
                if block + 1 < TILES:
                    pair = group * GROUP + member
                else:
                    pair = jnp.minimum(group + 1, groups - 1) * GROUP + member
                score(pair, (block + 1) % TILES, part_of(ahead, member))
            for member in range(GROUP):
                finish(group * GROUP + member, block, part_of(here, member))
        return carry

    lax.fori_loop(0, groups, head_group, 0)


def project_body(
    info, normed, w_own, w_peer, mesh_zero, w_decode,
    queries, keys, values_t, keys_sent, values_sent, straight,
):
    rows = normed[...]
    straight[...] = matmul_t(w_decode[...], mesh_zero[...])
    for half, weight in enumerate((w_own, w_peer)):
        place = slice(half * HALF, (half + 1) * HALF)
        keys[:, place] = matmul(rows, weight[1]).astype(BF16)
        values_t[place, :] = matmul(rows, weight[2]).T.astype(BF16)
        queries[:, place] = (matmul(rows, weight[0]) * SCALE).astype(BF16)

    @pl.when(info[0] == 0)
    def _():
        for half in range(2):
            place = slice(half * HALF, (half + 1) * HALF)
            other = slice((1 - half) * HALF, (2 - half) * HALF)
            keys_sent[:, other] = keys[ROWS - WIN :, place]
            values_sent[other, :] = values_t[place, ROWS - WIN :]

    @pl.when(info[0] != 0)
    def _():
        for half in range(2):
            place = slice(half * HALF, (half + 1) * HALF)
            other = slice((1 - half) * HALF, (2 - half) * HALF)
            keys_sent[:, other] = keys[:WIN, place]
            values_sent[other, :] = values_t[place, :WIN]


def own_body(queries, keys, values_t, mask, sums, stats, first, second):
    eyes, lane = identity_pair()

    def score(pair, block, scores):
        begin = WIN - block * TILE
        score_block(
            queries[rows_of(block), lanes_of(pair)], lane, eyes, keys[:, lanes_of(pair)],
            mask[begin : begin + ROWS, :], scores,
        )

    def finish(pair, block, scores):
        top = column_top(scores)
        both, total = weigh(scores, top, values_t[lanes_of(pair), :])
        sums[lanes_of(pair), rows_of(block)] = both
        columns = slice(2 * block * TILE, 2 * (block + 1) * TILE)
        stats[pair, 0:1, columns] = top
        stats[pair, 1:2, columns] = total

    pipeline(score, finish, first, second)


def attend_body(
    info, halo, peer_keys, peer_values, queries, sums, stats, mask, w_own, w_peer,
    straight, fold_own, fold_peer,
    projected,
    keys, values_t, masks, attended, first, second,
):
    core, first_device, last_device = info[0], info[4], info[5]

    @pl.when(core == 0)
    def _():
        keys[WIN:, :] = peer_keys[...]
        values_t[:, WIN:] = peer_values[...]

    @pl.when(core != 0)
    def _():
        keys[:WIN, :] = peer_keys[...]
        values_t[:, :WIN] = peer_values[...]

    begin = pl.ds(pl.multiple_of(core * WIN, WIN), WIN)
    beside = halo[...]
    for half, weight in enumerate((w_own, w_peer)):
        place = slice(half * HALF, (half + 1) * HALF)
        keys[begin, place] = matmul(beside, weight[1]).astype(BF16)
        values_t[place, begin] = matmul(beside, weight[2]).T.astype(BF16)
    low = jnp.where(first_device == 1, MASKED, 0.0)
    high = jnp.where(last_device == 1, MASKED, 0.0)
    for block in range(TILES):
        below, above = WIN - block * TILE, SPAN - block * TILE
        if below > 0:
            masks[block, :below, :] = (mask[:below, :].astype(F32) + low).astype(BF16)
        if above < SPAN:
            masks[block, below:, :] = (mask[above:, :].astype(F32) + high).astype(BF16)
    eyes, lane = identity_pair()

    def score(pair, block, scores):
        seen = slice(block * TILE, block * TILE + WIN)
        score_block(
            queries[rows_of(block), lanes_of(pair)], lane, eyes, keys[seen, lanes_of(pair)],
            masks[block], scores,
        )

    def finish(pair, block, scores):
        seen = slice(block * TILE, block * TILE + WIN)
        columns = slice(2 * block * TILE, 2 * (block + 1) * TILE)
        old, sum_old = stats[pair, 0:1, columns], stats[pair, 1:2, columns]
        top = jnp.maximum(old, column_top(scores))
        both, total = weigh(scores, top, values_t[lanes_of(pair), seen])
        shrink = jnp.exp2(old - top)
        inverse = 1.0 / (sum_old * shrink + total)
        shrink = shrink * inverse
        before = sums[lanes_of(pair), rows_of(block)]
        result = jnp.concatenate([
            before[:64] * shrink[:, :TILE] + both[:64] * inverse[:, :TILE],
            before[64:] * shrink[:, TILE:] + both[64:] * inverse[:, TILE:],
        ], axis=0)
        attended[lanes_of(pair), rows_of(block)] = result.astype(BF16)

    pipeline(score, finish, first, second)
    both = matmul(fold_own[...], attended[:HALF, :]) + matmul(fold_peer[...], attended[HALF:, :])
    projected[...] = (straight[...] + both[:LANES, :] + both[LANES:, :])[:C, :].astype(BF16)


def half_term(part, spread, place):
    rows = pl.ds(pl.multiple_of(place * ROWS, ROWS), ROWS)
    return matmul(part, spread[rows, :])


def spread_halves(info, src, dst, weight, spread, sources, tables, weights, places):
    mesh_base, row_base = info[6], info[7]
    sources[...] = src[...] - mesh_base
    weights[...] = weight[...].astype(F32)
    row_slots = lax.broadcasted_iota(jnp.int32, (TILE, LANES), 0)
    for tile in range(DEC_TILES):
        for part in range(DEC_ROUNDS):
            slot = slice(part * DEC_TILES + tile, part * DEC_TILES + tile + 1)
            target = dst[slot, :] - (row_base + tile * TILE)
            tables[rows_of(tile), rows_of(part)] = jnp.where(
                row_slots == target, weights[slot, :], 0.0
            ).astype(BF16)
    mesh_slots = lax.broadcasted_iota(jnp.int32, (ROWS, LANES), 0)

    def half(place, carry):
        begin = pl.multiple_of(place * ROWS, ROWS)
        for tile in range(DEC_TILES):
            picks = []
            for part in range(DEC_ROUNDS):
                slot = slice(part * DEC_TILES + tile, part * DEC_TILES + tile + 1)
                hit = mesh_slots == sources[slot, :] - begin
                picks.append(jnp.where(hit, 1.0, 0.0).astype(BF16))
            spread[pl.ds(begin, ROWS), rows_of(tile)] = matmul_t(
                jnp.concatenate(picks, axis=1), tables[rows_of(tile), :]
            ).astype(BF16)
        return carry

    lax.fori_loop(places[0], places[-1] + 1, half, 0)


def early_body(info, w_in, src, dst, weight, spread, sources, tables, weights):
    spread_halves(info, src, dst, weight, spread, sources, tables, weights, range(EARLY))


def spread_body(
    info, spread_in, own, src, dst, weight, grid, spread, base, sources, tables, weights
):
    core = info[0]
    spread_halves(info, src, dst, weight, spread, sources, tables, weights, range(EARLY, 6))
    fields = grid[:, pl.ds(pl.multiple_of(core * GQ, GQ), GQ)].astype(F32)
    terms = half_term(own[0], spread, 2 + core) + half_term(own[1], spread, 3 - core)
    base[...] = fields + terms


def sent_body(info, sent, spread, base, total):
    core = info[0]
    total[...] = (
        base[...]
        + half_term(sent[0], spread, 5 * core)
        + half_term(sent[1], spread, 3 * core + 1)
    )


def decode_body(info, swapped_rows, spread, total, out):
    other = 1 - info[0]
    terms = half_term(swapped_rows[0], spread, 5 * other)
    terms = terms + half_term(swapped_rows[1], spread, 3 * other + 1)
    out[...] = (total[...] + terms).astype(BF16)


def swapped(value):
    return lax.ppermute(value, "mp", [(0, 1), (1, 0)])


def up_and_down(value):
    bands = lax.axis_size("band")
    pairs = [(2 * i, 2 * i + 2) for i in range(bands - 1)]
    pairs += [(2 * i + 3, 2 * i + 1) for i in range(bands - 1)]
    return lax.ppermute(value, ("band", "mp"), pairs)


def over_the_edge(value):
    bands = lax.axis_size("band")
    pairs = [(2 * i + 1, 2 * i + 2) for i in range(bands - 1)]
    pairs += [(j, i) for i, j in pairs]
    return lax.ppermute(value, ("band", "mp"), pairs)


def on_device(
    grid_fields, w_in, enc_src, enc_dst, enc_weight, enc_count, norm_gain, w_qkv, w_out_attn,
    offsets, w_decode, dec_src, dec_dst, dec_weight,
):
    band = lax.axis_index("band")
    core = lax.axis_index("mp")
    bands = lax.axis_size("band")
    device = 2 * band + core
    grid = grid_fields.T
    grid_sent = up_and_down(grid)
    info = jnp.stack([
        core,
        enc_count[0],
        (band - 1) * G_BAND,
        device * ROWS,
        (device == 0).astype(jnp.int32),
        (device == 2 * bands - 1).astype(jnp.int32),
        (band - 1) * 2 * ROWS,
        device * GQ,
    ]).astype(jnp.int32)
    win_peer = swapped(w_in)
    dec_own = w_decode.T
    dec_peer = swapped(dec_own)
    qkv_own = w_qkv.transpose(1, 0, 2)
    qkv_peer = swapped(qkv_own)
    edges = jax.ShapeDtypeStruct(enc_src.shape, jnp.int32)
    mask, token = call(
        mask_body,
        (offsets,),
        1,
        [jax.ShapeDtypeStruct((SPAN, TILE), BF16), jax.ShapeDtypeStruct((8, LANES), F32)],
        [pltpu.VMEM((8, SPAN + TILE), F32), pltpu.VMEM((SPAN, TILE), F32)],
        5 * 10 ** 9, 4, "mask",
    )
    sources, targets, weights, gain, w_in_all, dec_all = call(
        prepare_body,
        (info, token, enc_src, enc_dst, enc_weight, norm_gain.reshape(1, D), w_in, win_peer,
         dec_own, dec_peer),
        1,
        [
            edges,
            edges,
            jax.ShapeDtypeStruct(enc_weight.shape, F32),
            jax.ShapeDtypeStruct((1, D), F32),
            jax.ShapeDtypeStruct((LANES, D), BF16),
            jax.ShapeDtypeStruct((LANES, D), BF16),
        ],
        [pltpu.VMEM((LANES, D), F32)],
        5 * 10 ** 9, 6, "prepare",
    )
    spread_out = jax.ShapeDtypeStruct((6 * ROWS, GQ), BF16)
    spread_scratch = [
        pltpu.VMEM(dec_src.shape, jnp.int32),
        pltpu.VMEM((GQ, DEC_ROUNDS * TILE), BF16),
        pltpu.VMEM(dec_weight.shape, F32),
    ]
    spread = call(
        early_body, (info, w_in_all, dec_src, dec_dst, dec_weight), 1, spread_out,
        spread_scratch, 5 * 10 ** 9, 10, "early",
    )
    grid_sent, w_in_all, spread = lax.optimization_barrier((grid_sent, w_in_all, spread))
    grid_swapped = swapped(grid_sent)
    grid_rows, fold_own = call(
        unpack_body,
        (info, grid, grid_sent, w_out_attn, dec_all),
        1,
        [
            jax.ShapeDtypeStruct((3 * G_BAND, LANES), F32),
            jax.ShapeDtypeStruct((2 * LANES, HALF), BF16),
        ],
        [pltpu.VMEM((LANES, G_BAND), F32)],
        2 * 10 ** 9, 6, "unpack",
    )
    fold_peer = swapped(fold_own)
    band_rows = jax.ShapeDtypeStruct((ROWS, D), BF16)
    step_buffers = [pltpu.VMEM((STEP, LANES), F32)] * 2 + [pltpu.VMEM((ROWS, D), F32)]
    grid_rows, mesh_zero, normed, to_band = call(
        encode_body,
        (info, sources, grid_rows, grid_swapped, w_in_all, targets, weights, gain),
        2,
        [
            jax.ShapeDtypeStruct((3 * G_BAND, LANES), F32),
            band_rows,
            band_rows,
            jax.ShapeDtypeStruct((WIN, D), BF16),
        ],
        [pltpu.VMEM((LANES, G_BAND), F32)] + step_buffers,
        7 * 10 ** 9, 14, "encode", {2: 0},
    )
    halo_band = over_the_edge(to_band)
    mesh_zero, normed = call(
        last_body,
        (info, sources, grid_rows, w_in_all, targets, weights, gain, mesh_zero, normed),
        2,
        [band_rows, band_rows],
        step_buffers,
        3 * 10 ** 9, 14, "last", {7: 0, 8: 1},
    )
    queries, keys, values_t, keys_sent, values_sent, straight = call(
        project_body,
        (info, normed, qkv_own, qkv_peer, mesh_zero, dec_all),
        1,
        [
            jax.ShapeDtypeStruct((ROWS, D), BF16),
            jax.ShapeDtypeStruct((ROWS, D), BF16),
            jax.ShapeDtypeStruct((D, ROWS), BF16),
            jax.ShapeDtypeStruct((WIN, D), BF16),
            jax.ShapeDtypeStruct((D, WIN), BF16),
            jax.ShapeDtypeStruct((LANES, ROWS), F32),
        ],
        [],
        6 * 10 ** 9, 10, "project",
    )
    peer_keys, peer_values = swapped(keys_sent), swapped(values_sent)
    sums, stats = call(
        own_body,
        (queries, keys, values_t, mask),
        0,
        [
            jax.ShapeDtypeStruct((D, ROWS), F32),
            jax.ShapeDtypeStruct((D // LANES, 8, 2 * ROWS), F32),
        ],
        [pltpu.VMEM((ROWS, 2 * GROUP * TILE), F32)] * 2,
        8 * 10 ** 9, 12, "own",
    )
    projected = call(
        attend_body,
        (info, halo_band, peer_keys, peer_values, queries, sums, stats, mask, qkv_own,
         qkv_peer, straight, fold_own, fold_peer),
        1,
        jax.ShapeDtypeStruct((C, ROWS), BF16),
        [
            pltpu.VMEM((2 * WIN, D), BF16),
            pltpu.VMEM((D, 2 * WIN), BF16),
            pltpu.VMEM((TILES, WIN, TILE), BF16),
            pltpu.VMEM((D, ROWS), BF16),
            pltpu.VMEM((WIN, 2 * GROUP * TILE), F32),
            pltpu.VMEM((WIN, 2 * GROUP * TILE), F32),
        ],
        10 ** 10, 16, "attend",
    )
    own_pair = jnp.stack([projected, swapped(projected)])
    pair_sent = up_and_down(own_pair)
    spread, base = call(
        spread_body,
        (info, spread, own_pair, dec_src, dec_dst, dec_weight, grid),
        1,
        [spread_out, jax.ShapeDtypeStruct((C, GQ), F32)],
        spread_scratch, 8 * 10 ** 9, 10, "spread", {1: 0},
    )
    pair_sent, base = lax.optimization_barrier((pair_sent, base))
    pair_swapped = swapped(pair_sent)
    sums_out = jax.ShapeDtypeStruct((C, GQ), F32)
    total = call(
        sent_body, (info, pair_sent, spread, base), 1, sums_out, [],
        10 ** 9, 6, "sent",
    )
    return call(
        decode_body, (info, pair_swapped, spread, total), 1,
        jax.ShapeDtypeStruct((C, GQ), BF16), [], 10 ** 9, 6, "decode",
    ).T


def solution(mesh):
    return jax.shard_map(
        on_device,
        mesh=mesh,
        in_specs=(
            P("band", None),
            P(None, "mp"),
            P("band", None),
            P("band", None),
            P("band", None),
            P("band"),
            P(),
            P(None, None, "mp"),
            P("mp", None),
            P(),
            P("mp", None),
            P(("band", "mp"), None),
            P(("band", "mp"), None),
            P(("band", "mp"), None),
        ),
        out_specs=P(("band", "mp"), None),
        check_vma=False,
    )
```

```python
import math
import jax
import jax.numpy as jnp
from jax import lax
from jax.experimental import pallas as pl
from jax.experimental.pallas import tpu as pltpu
from jax.sharding import PartitionSpec as P

D = 1024
C = 100
LANES = 128
TILE = 128
ROWS = 512
WIN = 384
K_OFF = 32
HALF = 512
G_BAND = 2048
EDGE_ROUNDS = 8
TILES = 4
STEP = 512
SPAN = TILE + 2 * WIN
GQ = 1024
DEC_ROUNDS = 3
DEC_TILES = 8
GROUP = 2
EARLY = 1
MASKED = -1e30
SCALE = 64 ** (-0.5) * math.log2(math.e)
F32 = jnp.float32
BF16 = jnp.bfloat16
MIB = 1024 * 1024


def vmem():
    return pl.BlockSpec(memory_space=pltpu.VMEM)


def smem():
    return pl.BlockSpec(memory_space=pltpu.SMEM)


def call(body, operands, smem_count, outs, scratch, flops, room, name, aliases={}):
    specs = [smem()] * smem_count + [vmem()] * (len(operands) - smem_count)
    return pl.pallas_call(
        body,
        out_shape=outs,
        in_specs=specs,
        out_specs=jax.tree.map(lambda _: vmem(), outs),
        scratch_shapes=scratch,
        compiler_params=pltpu.CompilerParams(vmem_limit_bytes=room * MIB),
        cost_estimate=pl.CostEstimate(flops=flops, bytes_accessed=2 * 10 ** 6, transcendentals=0),
        input_output_aliases=aliases,
        name=name,
    )(*operands)


def matmul(a, b):
    return jnp.dot(a, b, preferred_element_type=F32)


def matmul_t(a, b):
    return lax.dot_general(a, b, (((1,), (1,)), ((), ())), preferred_element_type=F32)


def to_rows(part, wide, rows, begin):
    wide[:C, :] = part[...].astype(F32)
    for block in range(G_BAND // LANES):
        columns = slice(block * LANES, (block + 1) * LANES)
        place = pl.multiple_of(begin + block * LANES, LANES)
        rows[pl.ds(place, LANES), :] = wide[:, columns].T


def by_core(core, wide, own, peer):
    @pl.when(core == 0)
    def _():
        wide[:C, :HALF] = own[...].astype(F32)
        wide[:C, HALF:] = peer[...].astype(F32)

    @pl.when(core != 0)
    def _():
        wide[:C, :HALF] = peer[...].astype(F32)
        wide[:C, HALF:] = own[...].astype(F32)


def mask_body(offsets, mask, token, strip, mask_wide):
    lane = lax.broadcasted_iota(jnp.int32, strip.shape, 1)
    away = lax.broadcasted_iota(jnp.int32, strip.shape, 0) + (SPAN - WIN - 8) - lane
    hit = away == offsets[0]
    for k in range(1, K_OFF):
        hit = hit | (away == offsets[k])
    strip[...] = jnp.where(hit, 0.0, MASKED)
    for begin in range(0, SPAN, 8):
        shift = SPAN - 8 - begin
        mask_wide[begin : begin + 8, :] = strip[:, shift : shift + TILE]
    mask[...] = mask_wide[...].astype(BF16)
    token[...] = jnp.zeros_like(token)


def prepare_body(
    info, token, src, dst, weight, gain, win_own, win_peer, dec_own, dec_peer,
    sources, targets, weights, gains, w_in, w_decode,
    w_wide,
):
    core, live, mesh_base = info[0], info[1], info[3]
    w_wide[...] = jnp.zeros_like(w_wide)
    by_core(core, w_wide, win_own, win_peer)
    w_in[...] = (w_wide[...] * 0.5).astype(BF16)
    by_core(core, w_wide, dec_own, dec_peer)
    w_decode[...] = w_wide[...].astype(BF16)
    slots = lax.broadcasted_iota(jnp.int32, weights.shape, 0)
    weights[...] = jnp.where(slots < live, weight[...].astype(F32), 0.0)
    targets[...] = dst[...] - mesh_base
    sources[...] = src[...] - info[2]
    gains[...] = gain[...]


def unpack_body(info, grid, sent, w_out, w_decode, rows, fold, wide):
    folded = matmul_t(w_decode[...], w_out[...])
    upper = folded.astype(BF16)
    fold[:LANES, :] = upper
    fold[LANES:, :] = (folded - upper.astype(F32)).astype(BF16)
    wide[...] = jnp.zeros_like(wide)
    to_rows(grid, wide, rows, G_BAND)
    to_rows(sent, wide, rows, info[0] * 2 * G_BAND)


def encode_tiles(
    core, order, src, w_in, targets, weights, gain, rows, mesh_zero, normed, first, second, total
):
    row_slots = lax.broadcasted_iota(jnp.int32, (TILE, LANES), 0)
    steps = EDGE_ROUNDS * TILE // STEP
    rounds = STEP // TILE
    count = len(order) * steps

    def tile_of(step):
        place = order[0] + step // steps
        return jnp.where(core == 0, place, TILES - 1 - place)

    def slot_of(step, part):
        return (step % steps * rounds + part) * 2 * TILES + core * TILES + tile_of(step)

    def gather(step, buffer):
        for part in range(rounds):
            slot = slot_of(step, part)
            for edge in range(TILE):
                index = src[slot, edge]
                buffer[pl.ds(part * TILE + edge, 1), :] = rows[pl.ds(index, 1), :]

    def add(step, buffer):
        tile = tile_of(step)
        half = matmul(buffer[...].astype(BF16), w_in[...])
        embedded = (half + half * jnp.tanh(half)).astype(BF16)
        tables = []
        for part in range(rounds):
            slot = slot_of(step, part)
            target = targets[pl.ds(slot, 1), :] - tile * TILE
            tables.append(jnp.where(row_slots == target, weights[pl.ds(slot, 1), :], 0.0))
        table = jnp.concatenate(tables, axis=1).astype(BF16)
        place = pl.ds(pl.multiple_of(tile * TILE, TILE), TILE)
        total[place, :] += matmul(table, embedded)

    for step in range(0, count, steps):
        place = pl.ds(pl.multiple_of(tile_of(step) * TILE, TILE), TILE)
        total[place, :] = jnp.zeros((TILE, D), F32)
    gather(0, first)

    def pair(index, carry):
        gather(2 * index + 1, second)
        add(2 * index, first)
        if count > 2:
            gather(jnp.minimum(2 * index + 2, count - 1), first)
        add(2 * index + 1, second)
        return carry

    lax.fori_loop(0, count // 2, pair, 0)

    def finish(step, carry):
        place = pl.ds(pl.multiple_of(tile_of(step * steps) * TILE, TILE), TILE)
        rounded = total[place, :].astype(BF16)
        mesh_zero[place, :] = rounded
        values = rounded.astype(F32)
        inverse = lax.rsqrt(jnp.mean(values * values, axis=1, keepdims=True) + 1e-05)
        normed[place, :] = (values * inverse * gain[...]).astype(BF16)
        return carry

    lax.fori_loop(0, len(order), finish, 0)


def encode_body(
    info, src, grid_rows, swapped_rows, w_in, targets, weights, gain,
    rows, mesh_zero, normed, to_band,
    wide, first, second, total,
):
    core = info[0]
    wide[...] = jnp.zeros_like(wide)
    to_rows(swapped_rows, wide, rows, (1 - core) * 2 * G_BAND)
    encode_tiles(
        core, range(TILES - 1), src, w_in, targets, weights, gain, rows, mesh_zero, normed,
        first, second, total,
    )
    to_band[...] = normed[pl.ds(pl.multiple_of(core * TILE, TILE), WIN), :]


def last_body(
    info, src, rows, w_in, targets, weights, gain, zero_in, normed_in,
    mesh_zero, normed,
    first, second, total,
):
    encode_tiles(
        info[0], range(TILES - 1, TILES), src, w_in, targets, weights, gain, rows, mesh_zero,
        normed, first, second, total,
    )


def identity_pair():
    row = lax.broadcasted_iota(jnp.int32, (TILE, LANES), 0)
    lane = lax.broadcasted_iota(jnp.int32, (TILE, LANES), 1)
    eye = jnp.where(row == lane, 1.0, 0.0).astype(BF16)
    return jnp.concatenate([eye, eye], axis=0), lane


def lanes_of(pair):
    return pl.ds(pl.multiple_of(pair * LANES, LANES), LANES)


def rows_of(block):
    return slice(block * TILE, (block + 1) * TILE)


def score_block(query, lane, eyes, keys, mask, scores):
    query = query.astype(F32)
    stacked = jnp.concatenate(
        [jnp.where(lane < 64, query, 0.0), jnp.where(lane < 64, 0.0, query)], axis=0
    ).astype(BF16)
    scores[...] = matmul_t(
        jnp.concatenate([keys, mask], axis=1), jnp.concatenate([stacked, eyes], axis=1)
    )


def column_top(scores):
    top = scores[:TILE, :]
    for begin in range(TILE, scores.shape[0], TILE):
        top = jnp.maximum(top, scores[begin : begin + TILE, :])
    return jnp.max(top, axis=0, keepdims=True)


def weigh(scores, top, values):
    expos = jnp.exp2(scores[...] - top).astype(BF16)
    ones = jnp.ones((16, scores.shape[0]), BF16)
    result = matmul(jnp.concatenate([values, ones], axis=0), expos)
    both = jnp.concatenate([result[:64, :TILE], result[64:TILE, TILE:]], axis=0)
    return both, result[TILE : TILE + 1, :]


def pipeline(score, finish, first, second):
    buffers = (first, second)
    groups = D // LANES // GROUP

    def part_of(buffer, member):
        return buffer.at[:, member * 2 * TILE : (member + 1) * 2 * TILE]

    for member in range(GROUP):
        score(member, 0, part_of(first, member))

    def head_group(group, carry):
        for block in range(TILES):
            here, ahead = buffers[block % 2], buffers[(block + 1) % 2]
            for member in range(GROUP):
                if block + 1 < TILES:
                    pair = group * GROUP + member
                else:
                    pair = jnp.minimum(group + 1, groups - 1) * GROUP + member
                score(pair, (block + 1) % TILES, part_of(ahead, member))
            for member in range(GROUP):
                finish(group * GROUP + member, block, part_of(here, member))
        return carry

    lax.fori_loop(0, groups, head_group, 0)


def project_body(
    info, normed, w_own, w_peer, mesh_zero, w_decode,
    queries, keys, values_t, keys_sent, values_sent, straight,
):
    rows = normed[...]
    straight[...] = matmul_t(w_decode[...], mesh_zero[...])
    for half, weight in enumerate((w_own, w_peer)):
        place = slice(half * HALF, (half + 1) * HALF)
        keys[:, place] = matmul(rows, weight[1]).astype(BF16)
        values_t[place, :] = matmul(rows, weight[2]).T.astype(BF16)
        queries[:, place] = (matmul(rows, weight[0]) * SCALE).astype(BF16)

    @pl.when(info[0] == 0)
    def _():
        for half in range(2):
            place = slice(half * HALF, (half + 1) * HALF)
            other = slice((1 - half) * HALF, (2 - half) * HALF)
            keys_sent[:, other] = keys[ROWS - WIN :, place]
            values_sent[other, :] = values_t[place, ROWS - WIN :]

    @pl.when(info[0] != 0)
    def _():
        for half in range(2):
            place = slice(half * HALF, (half + 1) * HALF)
            other = slice((1 - half) * HALF, (2 - half) * HALF)
            keys_sent[:, other] = keys[:WIN, place]
            values_sent[other, :] = values_t[place, :WIN]


def own_body(queries, keys, values_t, mask, sums, stats, first, second):
    eyes, lane = identity_pair()

    def score(pair, block, scores):
        begin = WIN - block * TILE
        score_block(
            queries[rows_of(block), lanes_of(pair)], lane, eyes, keys[:, lanes_of(pair)],
            mask[begin : begin + ROWS, :], scores,
        )

    def finish(pair, block, scores):
        top = column_top(scores)
        both, total = weigh(scores, top, values_t[lanes_of(pair), :])
        sums[lanes_of(pair), rows_of(block)] = both
        columns = slice(2 * block * TILE, 2 * (block + 1) * TILE)
        stats[pair, 0:1, columns] = top
        stats[pair, 1:2, columns] = total

    pipeline(score, finish, first, second)


def attend_body(
    info, halo, peer_keys, peer_values, queries, sums, stats, mask, w_own, w_peer,
    straight, fold_own, fold_peer,
    projected,
    keys, values_t, masks, attended, first, second,
):
    core, first_device, last_device = info[0], info[4], info[5]

    @pl.when(core == 0)
    def _():
        keys[WIN:, :] = peer_keys[...]
        values_t[:, WIN:] = peer_values[...]

    @pl.when(core != 0)
    def _():
        keys[:WIN, :] = peer_keys[...]
        values_t[:, :WIN] = peer_values[...]

    begin = pl.ds(pl.multiple_of(core * WIN, WIN), WIN)
    beside = halo[...]
    for half, weight in enumerate((w_own, w_peer)):
        place = slice(half * HALF, (half + 1) * HALF)
        keys[begin, place] = matmul(beside, weight[1]).astype(BF16)
        values_t[place, begin] = matmul(beside, weight[2]).T.astype(BF16)
    low = jnp.where(first_device == 1, MASKED, 0.0)
    high = jnp.where(last_device == 1, MASKED, 0.0)
    for block in range(TILES):
        below, above = WIN - block * TILE, SPAN - block * TILE
        if below > 0:
            masks[block, :below, :] = (mask[:below, :].astype(F32) + low).astype(BF16)
        if above < SPAN:
            masks[block, below:, :] = (mask[above:, :].astype(F32) + high).astype(BF16)
    eyes, lane = identity_pair()

    def score(pair, block, scores):
        seen = slice(block * TILE, block * TILE + WIN)
        score_block(
            queries[rows_of(block), lanes_of(pair)], lane, eyes, keys[seen, lanes_of(pair)],
            masks[block], scores,
        )

    def finish(pair, block, scores):
        seen = slice(block * TILE, block * TILE + WIN)
        columns = slice(2 * block * TILE, 2 * (block + 1) * TILE)
        old, sum_old = stats[pair, 0:1, columns], stats[pair, 1:2, columns]
        top = jnp.maximum(old, column_top(scores))
        both, total = weigh(scores, top, values_t[lanes_of(pair), seen])
        shrink = jnp.exp2(old - top)
        inverse = 1.0 / (sum_old * shrink + total)
        shrink = shrink * inverse
        before = sums[lanes_of(pair), rows_of(block)]
        result = jnp.concatenate([
            before[:64] * shrink[:, :TILE] + both[:64] * inverse[:, :TILE],
            before[64:] * shrink[:, TILE:] + both[64:] * inverse[:, TILE:],
        ], axis=0)
        attended[lanes_of(pair), rows_of(block)] = result.astype(BF16)

    pipeline(score, finish, first, second)
    both = matmul(fold_own[...], attended[:HALF, :]) + matmul(fold_peer[...], attended[HALF:, :])
    projected[...] = (straight[...] + both[:LANES, :] + both[LANES:, :])[:C, :].astype(BF16)


def half_term(part, spread, place):
    rows = pl.ds(pl.multiple_of(place * ROWS, ROWS), ROWS)
    return matmul(part, spread[rows, :])


def spread_halves(info, src, dst, weight, spread, sources, tables, weights, places):
    mesh_base, row_base = info[6], info[7]
    sources[...] = src[...] - mesh_base
    weights[...] = weight[...].astype(F32)
    row_slots = lax.broadcasted_iota(jnp.int32, (TILE, LANES), 0)
    for tile in range(DEC_TILES):
        for part in range(DEC_ROUNDS):
            slot = slice(part * DEC_TILES + tile, part * DEC_TILES + tile + 1)
            target = dst[slot, :] - (row_base + tile * TILE)
            tables[rows_of(tile), rows_of(part)] = jnp.where(
                row_slots == target, weights[slot, :], 0.0
            ).astype(BF16)
    mesh_slots = lax.broadcasted_iota(jnp.int32, (ROWS, LANES), 0)

    def half(place, carry):
        begin = pl.multiple_of(place * ROWS, ROWS)
        for tile in range(DEC_TILES):
            picks = []
            for part in range(DEC_ROUNDS):
                slot = slice(part * DEC_TILES + tile, part * DEC_TILES + tile + 1)
                hit = mesh_slots == sources[slot, :] - begin
                picks.append(jnp.where(hit, 1.0, 0.0).astype(BF16))
            spread[pl.ds(begin, ROWS), rows_of(tile)] = matmul_t(
                jnp.concatenate(picks, axis=1), tables[rows_of(tile), :]
            ).astype(BF16)
        return carry

    lax.fori_loop(places[0], places[-1] + 1, half, 0)


def early_body(info, w_in, src, dst, weight, spread, sources, tables, weights):
    spread_halves(info, src, dst, weight, spread, sources, tables, weights, range(EARLY))


def spread_body(
    info, spread_in, own, src, dst, weight, grid, spread, base, sources, tables, weights
):
    core = info[0]
    spread_halves(info, src, dst, weight, spread, sources, tables, weights, range(EARLY, 6))
    fields = grid[:, pl.ds(pl.multiple_of(core * GQ, GQ), GQ)].astype(F32)
    terms = half_term(own[0], spread, 2 + core) + half_term(own[1], spread, 3 - core)
    base[...] = fields + terms


def sent_body(info, sent, spread, base, total):
    core = info[0]
    total[...] = (
        base[...]
        + half_term(sent[0], spread, 5 * core)
        + half_term(sent[1], spread, 3 * core + 1)
    )


def decode_body(info, swapped_rows, spread, total, out):
    other = 1 - info[0]
    terms = half_term(swapped_rows[0], spread, 5 * other)
    terms = terms + half_term(swapped_rows[1], spread, 3 * other + 1)
    out[...] = (total[...] + terms).astype(BF16)


def swapped(value):
    return lax.ppermute(value, "mp", [(0, 1), (1, 0)])


def up_and_down(value):
    bands = lax.axis_size("band")
    pairs = [(2 * i, 2 * i + 2) for i in range(bands - 1)]
    pairs += [(2 * i + 3, 2 * i + 1) for i in range(bands - 1)]
    return lax.ppermute(value, ("band", "mp"), pairs)


def over_the_edge(value):
    bands = lax.axis_size("band")
    pairs = [(2 * i + 1, 2 * i + 2) for i in range(bands - 1)]
    pairs += [(j, i) for i, j in pairs]
    return lax.ppermute(value, ("band", "mp"), pairs)


def on_device(
    grid_fields, w_in, enc_src, enc_dst, enc_weight, enc_count, norm_gain, w_qkv, w_out_attn,
    offsets, w_decode, dec_src, dec_dst, dec_weight,
):
    band = lax.axis_index("band")
    core = lax.axis_index("mp")
    bands = lax.axis_size("band")
    device = 2 * band + core
    grid = grid_fields.T
    grid_sent = up_and_down(grid)
    info = jnp.stack([
        core,
        enc_count[0],
        (band - 1) * G_BAND,
        device * ROWS,
        (device == 0).astype(jnp.int32),
        (device == 2 * bands - 1).astype(jnp.int32),
        (band - 1) * 2 * ROWS,
        device * GQ,
    ]).astype(jnp.int32)
    win_peer = swapped(w_in)
    dec_own = w_decode.T
    dec_peer = swapped(dec_own)
    qkv_own = w_qkv.transpose(1, 0, 2)
    qkv_peer = swapped(qkv_own)
    edges = jax.ShapeDtypeStruct(enc_src.shape, jnp.int32)
    mask, token = call(
        mask_body,
        (offsets,),
        1,
        [jax.ShapeDtypeStruct((SPAN, TILE), BF16), jax.ShapeDtypeStruct((8, LANES), F32)],
        [pltpu.VMEM((8, SPAN + TILE), F32), pltpu.VMEM((SPAN, TILE), F32)],
        5 * 10 ** 9, 4, "mask",
    )
    sources, targets, weights, gain, w_in_all, dec_all = call(
        prepare_body,
        (info, token, enc_src, enc_dst, enc_weight, norm_gain.reshape(1, D), w_in, win_peer,
         dec_own, dec_peer),
        1,
        [
            edges,
            edges,
            jax.ShapeDtypeStruct(enc_weight.shape, F32),
            jax.ShapeDtypeStruct((1, D), F32),
            jax.ShapeDtypeStruct((LANES, D), BF16),
            jax.ShapeDtypeStruct((LANES, D), BF16),
        ],
        [pltpu.VMEM((LANES, D), F32)],
        5 * 10 ** 9, 6, "prepare",
    )
    spread_out = jax.ShapeDtypeStruct((6 * ROWS, GQ), BF16)
    spread_scratch = [
        pltpu.VMEM(dec_src.shape, jnp.int32),
        pltpu.VMEM((GQ, DEC_ROUNDS * TILE), BF16),
        pltpu.VMEM(dec_weight.shape, F32),
    ]
    spread = call(
        early_body, (info, w_in_all, dec_src, dec_dst, dec_weight), 1, spread_out,
        spread_scratch, 5 * 10 ** 9, 10, "early",
    )
    grid_sent, w_in_all, spread = lax.optimization_barrier((grid_sent, w_in_all, spread))
    grid_swapped = swapped(grid_sent)
    grid_rows, fold_own = call(
        unpack_body,
        (info, grid, grid_sent, w_out_attn, dec_all),
        1,
        [
            jax.ShapeDtypeStruct((3 * G_BAND, LANES), F32),
            jax.ShapeDtypeStruct((2 * LANES, HALF), BF16),
        ],
        [pltpu.VMEM((LANES, G_BAND), F32)],
        2 * 10 ** 9, 6, "unpack",
    )
    fold_peer = swapped(fold_own)
    band_rows = jax.ShapeDtypeStruct((ROWS, D), BF16)
    step_buffers = [pltpu.VMEM((STEP, LANES), F32)] * 2 + [pltpu.VMEM((ROWS, D), F32)]
    grid_rows, mesh_zero, normed, to_band = call(
        encode_body,
        (info, sources, grid_rows, grid_swapped, w_in_all, targets, weights, gain),
        2,
        [
            jax.ShapeDtypeStruct((3 * G_BAND, LANES), F32),
            band_rows,
            band_rows,
            jax.ShapeDtypeStruct((WIN, D), BF16),
        ],
        [pltpu.VMEM((LANES, G_BAND), F32)] + step_buffers,
        7 * 10 ** 9, 14, "encode", {2: 0},
    )
    halo_band = over_the_edge(to_band)
    mesh_zero, normed = call(
        last_body,
        (info, sources, grid_rows, w_in_all, targets, weights, gain, mesh_zero, normed),
        2,
        [band_rows, band_rows],
        step_buffers,
        3 * 10 ** 9, 14, "last", {7: 0, 8: 1},
    )
    queries, keys, values_t, keys_sent, values_sent, straight = call(
        project_body,
        (info, normed, qkv_own, qkv_peer, mesh_zero, dec_all),
        1,
        [
            jax.ShapeDtypeStruct((ROWS, D), BF16),
            jax.ShapeDtypeStruct((ROWS, D), BF16),
            jax.ShapeDtypeStruct((D, ROWS), BF16),
            jax.ShapeDtypeStruct((WIN, D), BF16),
            jax.ShapeDtypeStruct((D, WIN), BF16),
            jax.ShapeDtypeStruct((LANES, ROWS), F32),
        ],
        [],
        6 * 10 ** 9, 10, "project",
    )
    peer_keys, peer_values = swapped(keys_sent), swapped(values_sent)
    sums, stats = call(
        own_body,
        (queries, keys, values_t, mask),
        0,
        [
            jax.ShapeDtypeStruct((D, ROWS), F32),
            jax.ShapeDtypeStruct((D // LANES, 8, 2 * ROWS), F32),
        ],
        [pltpu.VMEM((ROWS, 2 * GROUP * TILE), F32)] * 2,
        8 * 10 ** 9, 12, "own",
    )
    projected = call(
        attend_body,
        (info, halo_band, peer_keys, peer_values, queries, sums, stats, mask, qkv_own,
         qkv_peer, straight, fold_own, fold_peer),
        1,
        jax.ShapeDtypeStruct((C, ROWS), BF16),
        [
            pltpu.VMEM((2 * WIN, D), BF16),
            pltpu.VMEM((D, 2 * WIN), BF16),
            pltpu.VMEM((TILES, WIN, TILE), BF16),
            pltpu.VMEM((D, ROWS), BF16),
            pltpu.VMEM((WIN, 2 * GROUP * TILE), F32),
            pltpu.VMEM((WIN, 2 * GROUP * TILE), F32),
        ],
        10 ** 10, 16, "attend",
    )
    own_pair = jnp.stack([projected, swapped(projected)])
    pair_sent = up_and_down(own_pair)
    spread, base = call(
        spread_body,
        (info, spread, own_pair, dec_src, dec_dst, dec_weight, grid),
        1,
        [spread_out, jax.ShapeDtypeStruct((C, GQ), F32)],
        spread_scratch, 8 * 10 ** 9, 10, "spread", {1: 0},
    )
    pair_sent, base = lax.optimization_barrier((pair_sent, base))
    pair_swapped = swapped(pair_sent)
    sums_out = jax.ShapeDtypeStruct((C, GQ), F32)
    total = call(
        sent_body, (info, pair_sent, spread, base), 1, sums_out, [],
        10 ** 9, 6, "sent",
    )
    return call(
        decode_body, (info, pair_swapped, spread, total), 1,
        jax.ShapeDtypeStruct((C, GQ), BF16), [], 10 ** 9, 6, "decode",
    ).T


def solution(mesh):
    return jax.shard_map(
        on_device,
        mesh=mesh,
        in_specs=(
            P("band", None),
            P(None, "mp"),
            P("band", None),
            P("band", None),
            P("band", None),
            P("band"),
            P(),
            P(None, None, "mp"),
            P("mp", None),
            P(),
            P("mp", None),
            P(("band", "mp"), None),
            P(("band", "mp"), None),
            P(("band", "mp"), None),
        ),
        out_specs=P(("band", "mp"), None),
        check_vma=False,
    )
```

```python
import math
import jax
import jax.numpy as jnp
from jax import lax
from jax.experimental import pallas as pl
from jax.experimental.pallas import tpu as pltpu
from jax.sharding import PartitionSpec as P

D = 1024
C = 100
LANES = 128
TILE = 128
ROWS = 512
WIN = 384
K_OFF = 32
HALF = 512
G_BAND = 2048
EDGE_ROUNDS = 8
TILES = 4
STEP = 512
SPAN = TILE + 2 * WIN
GQ = 1024
DEC_ROUNDS = 3
DEC_TILES = 8
GROUP = 2
EARLY = 2
MASKED = -1e30
SCALE = 64 ** (-0.5) * math.log2(math.e)
F32 = jnp.float32
BF16 = jnp.bfloat16
MIB = 1024 * 1024


def vmem():
    return pl.BlockSpec(memory_space=pltpu.VMEM)


def smem():
    return pl.BlockSpec(memory_space=pltpu.SMEM)


def call(body, operands, smem_count, outs, scratch, flops, room, name, aliases={}):
    specs = [smem()] * smem_count + [vmem()] * (len(operands) - smem_count)
    return pl.pallas_call(
        body,
        out_shape=outs,
        in_specs=specs,
        out_specs=jax.tree.map(lambda _: vmem(), outs),
        scratch_shapes=scratch,
        compiler_params=pltpu.CompilerParams(vmem_limit_bytes=room * MIB),
        cost_estimate=pl.CostEstimate(flops=flops, bytes_accessed=2 * 10 ** 6, transcendentals=0),
        input_output_aliases=aliases,
        name=name,
    )(*operands)


def matmul(a, b):
    return jnp.dot(a, b, preferred_element_type=F32)


def matmul_t(a, b):
    return lax.dot_general(a, b, (((1,), (1,)), ((), ())), preferred_element_type=F32)


def to_rows(part, wide, rows, begin):
    wide[:C, :] = part[...].astype(F32)
    for block in range(G_BAND // LANES):
        columns = slice(block * LANES, (block + 1) * LANES)
        place = pl.multiple_of(begin + block * LANES, LANES)
        rows[pl.ds(place, LANES), :] = wide[:, columns].T


def by_core(core, wide, own, peer):
    @pl.when(core == 0)
    def _():
        wide[:C, :HALF] = own[...].astype(F32)
        wide[:C, HALF:] = peer[...].astype(F32)

    @pl.when(core != 0)
    def _():
        wide[:C, :HALF] = peer[...].astype(F32)
        wide[:C, HALF:] = own[...].astype(F32)


def make_mask(offsets, mask, strip, mask_wide):
    lane = lax.broadcasted_iota(jnp.int32, strip.shape, 1)
    away = lax.broadcasted_iota(jnp.int32, strip.shape, 0) + (SPAN - WIN - 8) - lane
    hit = away == offsets[0]
    for k in range(1, K_OFF):
        hit = hit | (away == offsets[k])
    strip[...] = jnp.where(hit, 0.0, MASKED)
    for begin in range(0, SPAN, 8):
        shift = SPAN - 8 - begin
        mask_wide[begin : begin + 8, :] = strip[:, shift : shift + TILE]
    mask[...] = mask_wide[...].astype(BF16)


def prepare_body(
    info, src, dst, weight, gain, win_own, win_peer, dec_own, dec_peer,
    sources, targets, weights, gains, w_in, w_decode,
    w_wide,
):
    core, live, mesh_base = info[0], info[1], info[3]
    w_wide[...] = jnp.zeros_like(w_wide)
    by_core(core, w_wide, win_own, win_peer)
    w_in[...] = (w_wide[...] * 0.5).astype(BF16)
    by_core(core, w_wide, dec_own, dec_peer)
    w_decode[...] = w_wide[...].astype(BF16)
    slots = lax.broadcasted_iota(jnp.int32, weights.shape, 0)
    weights[...] = jnp.where(slots < live, weight[...].astype(F32), 0.0)
    targets[...] = dst[...] - mesh_base
    sources[...] = src[...] - info[2]
    gains[...] = gain[...]


def unpack_body(info, grid, sent, w_out, w_decode, rows, fold, wide):
    folded = matmul_t(w_decode[...], w_out[...])
    upper = folded.astype(BF16)
    fold[:LANES, :] = upper
    fold[LANES:, :] = (folded - upper.astype(F32)).astype(BF16)
    wide[...] = jnp.zeros_like(wide)
    to_rows(grid, wide, rows, G_BAND)
    to_rows(sent, wide, rows, info[0] * 2 * G_BAND)


def encode_tiles(
    core, order, src, w_in, targets, weights, gain, rows, mesh_zero, normed, first, second, total
):
    row_slots = lax.broadcasted_iota(jnp.int32, (TILE, LANES), 0)
    steps = EDGE_ROUNDS * TILE // STEP
    rounds = STEP // TILE
    count = len(order) * steps

    def tile_of(step):
        place = order[0] + step // steps
        return jnp.where(core == 0, place, TILES - 1 - place)

    def slot_of(step, part):
        return (step % steps * rounds + part) * 2 * TILES + core * TILES + tile_of(step)

    def gather(step, buffer):
        for part in range(rounds):
            slot = slot_of(step, part)
            for edge in range(TILE):
                index = src[slot, edge]
                buffer[pl.ds(part * TILE + edge, 1), :] = rows[pl.ds(index, 1), :]

    def add(step, buffer):
        tile = tile_of(step)
        half = matmul(buffer[...].astype(BF16), w_in[...])
        embedded = (half + half * jnp.tanh(half)).astype(BF16)
        tables = []
        for part in range(rounds):
            slot = slot_of(step, part)
            target = targets[pl.ds(slot, 1), :] - tile * TILE
            tables.append(jnp.where(row_slots == target, weights[pl.ds(slot, 1), :], 0.0))
        table = jnp.concatenate(tables, axis=1).astype(BF16)
        place = pl.ds(pl.multiple_of(tile * TILE, TILE), TILE)
        total[place, :] += matmul(table, embedded)

    for step in range(0, count, steps):
        place = pl.ds(pl.multiple_of(tile_of(step) * TILE, TILE), TILE)
        total[place, :] = jnp.zeros((TILE, D), F32)
    gather(0, first)

    def pair(index, carry):
        gather(2 * index + 1, second)
        add(2 * index, first)
        if count > 2:
            gather(jnp.minimum(2 * index + 2, count - 1), first)
        add(2 * index + 1, second)
        return carry

    lax.fori_loop(0, count // 2, pair, 0)

    def finish(step, carry):
        place = pl.ds(pl.multiple_of(tile_of(step * steps) * TILE, TILE), TILE)
        rounded = total[place, :].astype(BF16)
        mesh_zero[place, :] = rounded
        values = rounded.astype(F32)
        inverse = lax.rsqrt(jnp.mean(values * values, axis=1, keepdims=True) + 1e-05)
        normed[place, :] = (values * inverse * gain[...]).astype(BF16)
        return carry

    lax.fori_loop(0, len(order), finish, 0)


def encode_body(
    info, src, grid_rows, swapped_rows, w_in, targets, weights, gain,
    rows, mesh_zero, normed, to_band,
    wide, first, second, total,
):
    core = info[0]
    wide[...] = jnp.zeros_like(wide)
    to_rows(swapped_rows, wide, rows, (1 - core) * 2 * G_BAND)
    encode_tiles(
        core, range(TILES), src, w_in, targets, weights, gain, rows, mesh_zero, normed,
        first, second, total,
    )
    to_band[...] = normed[pl.ds(pl.multiple_of(core * TILE, TILE), WIN), :]


def identity_pair():
    row = lax.broadcasted_iota(jnp.int32, (TILE, LANES), 0)
    lane = lax.broadcasted_iota(jnp.int32, (TILE, LANES), 1)
    eye = jnp.where(row == lane, 1.0, 0.0).astype(BF16)
    return jnp.concatenate([eye, eye], axis=0), lane


def lanes_of(pair):
    return pl.ds(pl.multiple_of(pair * LANES, LANES), LANES)


def rows_of(block):
    return slice(block * TILE, (block + 1) * TILE)


def score_block(query, lane, eyes, keys, mask, scores):
    query = query.astype(F32)
    stacked = jnp.concatenate(
        [jnp.where(lane < 64, query, 0.0), jnp.where(lane < 64, 0.0, query)], axis=0
    ).astype(BF16)
    scores[...] = matmul_t(
        jnp.concatenate([keys, mask], axis=1), jnp.concatenate([stacked, eyes], axis=1)
    )


def column_top(scores):
    top = scores[:TILE, :]
    for begin in range(TILE, scores.shape[0], TILE):
        top = jnp.maximum(top, scores[begin : begin + TILE, :])
    return jnp.max(top, axis=0, keepdims=True)


def weigh(scores, top, values):
    expos = jnp.exp2(scores[...] - top).astype(BF16)
    ones = jnp.ones((16, scores.shape[0]), BF16)
    result = matmul(jnp.concatenate([values, ones], axis=0), expos)
    both = jnp.concatenate([result[:64, :TILE], result[64:TILE, TILE:]], axis=0)
    return both, result[TILE : TILE + 1, :]


def pipeline(score, finish, first, second):
    buffers = (first, second)
    groups = D // LANES // GROUP

    def part_of(buffer, member):
        return buffer.at[:, member * 2 * TILE : (member + 1) * 2 * TILE]

    for member in range(GROUP):
        score(member, 0, part_of(first, member))

    def head_group(group, carry):
        for block in range(TILES):
            here, ahead = buffers[block % 2], buffers[(block + 1) % 2]
            for member in range(GROUP):
                if block + 1 < TILES:
                    pair = group * GROUP + member
                else:
                    pair = jnp.minimum(group + 1, groups - 1) * GROUP + member
                score(pair, (block + 1) % TILES, part_of(ahead, member))
            for member in range(GROUP):
                finish(group * GROUP + member, block, part_of(here, member))
        return carry

    lax.fori_loop(0, groups, head_group, 0)


def project_body(
    info, normed, w_own, w_peer, mesh_zero, w_decode,
    queries, keys, values_t, keys_sent, values_sent, straight,
):
    rows = normed[...]
    straight[...] = matmul_t(w_decode[...], mesh_zero[...])
    for half, weight in enumerate((w_own, w_peer)):
        place = slice(half * HALF, (half + 1) * HALF)
        keys[:, place] = matmul(rows, weight[1]).astype(BF16)
        values_t[place, :] = matmul(rows, weight[2]).T.astype(BF16)
        queries[:, place] = (matmul(rows, weight[0]) * SCALE).astype(BF16)

    @pl.when(info[0] == 0)
    def _():
        for half in range(2):
            place = slice(half * HALF, (half + 1) * HALF)
            other = slice((1 - half) * HALF, (2 - half) * HALF)
            keys_sent[:, other] = keys[ROWS - WIN :, place]
            values_sent[other, :] = values_t[place, ROWS - WIN :]

    @pl.when(info[0] != 0)
    def _():
        for half in range(2):
            place = slice(half * HALF, (half + 1) * HALF)
            other = slice((1 - half) * HALF, (2 - half) * HALF)
            keys_sent[:, other] = keys[:WIN, place]
            values_sent[other, :] = values_t[place, :WIN]


def own_body(
    offsets, queries, keys, values_t, sums, stats, mask, first, second, strip, mask_wide
):
    make_mask(offsets, mask, strip, mask_wide)
    eyes, lane = identity_pair()

    def score(pair, block, scores):
        begin = WIN - block * TILE
        score_block(
            queries[rows_of(block), lanes_of(pair)], lane, eyes, keys[:, lanes_of(pair)],
            mask[begin : begin + ROWS, :], scores,
        )

    def finish(pair, block, scores):
        top = column_top(scores)
        both, total = weigh(scores, top, values_t[lanes_of(pair), :])
        sums[lanes_of(pair), rows_of(block)] = both
        columns = slice(2 * block * TILE, 2 * (block + 1) * TILE)
        stats[pair, 0:1, columns] = top
        stats[pair, 1:2, columns] = total

    pipeline(score, finish, first, second)


def attend_body(
    info, halo, peer_keys, peer_values, queries, sums, stats, mask, w_own, w_peer,
    straight, fold_own, fold_peer,
    projected,
    keys, values_t, masks, attended, first, second,
):
    core, first_device, last_device = info[0], info[4], info[5]

    @pl.when(core == 0)
    def _():
        keys[WIN:, :] = peer_keys[...]
        values_t[:, WIN:] = peer_values[...]

    @pl.when(core != 0)
    def _():
        keys[:WIN, :] = peer_keys[...]
        values_t[:, :WIN] = peer_values[...]

    begin = pl.ds(pl.multiple_of(core * WIN, WIN), WIN)
    beside = halo[...]
    for half, weight in enumerate((w_own, w_peer)):
        place = slice(half * HALF, (half + 1) * HALF)
        keys[begin, place] = matmul(beside, weight[1]).astype(BF16)
        values_t[place, begin] = matmul(beside, weight[2]).T.astype(BF16)
    low = jnp.where(first_device == 1, MASKED, 0.0)
    high = jnp.where(last_device == 1, MASKED, 0.0)
    for block in range(TILES):
        below, above = WIN - block * TILE, SPAN - block * TILE
        if below > 0:
            masks[block, :below, :] = (mask[:below, :].astype(F32) + low).astype(BF16)
        if above < SPAN:
            masks[block, below:, :] = (mask[above:, :].astype(F32) + high).astype(BF16)
    eyes, lane = identity_pair()

    def score(pair, block, scores):
        seen = slice(block * TILE, block * TILE + WIN)
        score_block(
            queries[rows_of(block), lanes_of(pair)], lane, eyes, keys[seen, lanes_of(pair)],
            masks[block], scores,
        )

    def finish(pair, block, scores):
        seen = slice(block * TILE, block * TILE + WIN)
        columns = slice(2 * block * TILE, 2 * (block + 1) * TILE)
        old, sum_old = stats[pair, 0:1, columns], stats[pair, 1:2, columns]
        top = jnp.maximum(old, column_top(scores))
        both, total = weigh(scores, top, values_t[lanes_of(pair), seen])
        shrink = jnp.exp2(old - top)
        inverse = 1.0 / (sum_old * shrink + total)
        shrink = shrink * inverse
        before = sums[lanes_of(pair), rows_of(block)]
        result = jnp.concatenate([
            before[:64] * shrink[:, :TILE] + both[:64] * inverse[:, :TILE],
            before[64:] * shrink[:, TILE:] + both[64:] * inverse[:, TILE:],
        ], axis=0)
        attended[lanes_of(pair), rows_of(block)] = result.astype(BF16)

    pipeline(score, finish, first, second)
    both = matmul(fold_own[...], attended[:HALF, :]) + matmul(fold_peer[...], attended[HALF:, :])
    projected[...] = (straight[...] + both[:LANES, :] + both[LANES:, :])[:C, :].astype(BF16)


def half_term(part, spread, place):
    rows = pl.ds(pl.multiple_of(place * ROWS, ROWS), ROWS)
    return matmul(part, spread[rows, :])


def spread_halves(info, src, dst, weight, spread, sources, tables, weights, places):
    mesh_base, row_base = info[6], info[7]
    sources[...] = src[...] - mesh_base
    weights[...] = weight[...].astype(F32)
    row_slots = lax.broadcasted_iota(jnp.int32, (TILE, LANES), 0)
    for tile in range(DEC_TILES):
        for part in range(DEC_ROUNDS):
            slot = slice(part * DEC_TILES + tile, part * DEC_TILES + tile + 1)
            target = dst[slot, :] - (row_base + tile * TILE)
            tables[rows_of(tile), rows_of(part)] = jnp.where(
                row_slots == target, weights[slot, :], 0.0
            ).astype(BF16)
    mesh_slots = lax.broadcasted_iota(jnp.int32, (ROWS, LANES), 0)

    def half(place, carry):
        begin = pl.multiple_of(place * ROWS, ROWS)
        for tile in range(DEC_TILES):
            picks = []
            for part in range(DEC_ROUNDS):
                slot = slice(part * DEC_TILES + tile, part * DEC_TILES + tile + 1)
                hit = mesh_slots == sources[slot, :] - begin
                picks.append(jnp.where(hit, 1.0, 0.0).astype(BF16))
            spread[pl.ds(begin, ROWS), rows_of(tile)] = matmul_t(
                jnp.concatenate(picks, axis=1), tables[rows_of(tile), :]
            ).astype(BF16)
        return carry

    lax.fori_loop(places[0], places[-1] + 1, half, 0)


def early_body(info, src, dst, weight, spread, sources, tables, weights):
    spread_halves(info, src, dst, weight, spread, sources, tables, weights, range(EARLY))


def spread_body(
    info, spread_in, own, src, dst, weight, grid, spread, base, sources, tables, weights
):
    core = info[0]
    spread_halves(info, src, dst, weight, spread, sources, tables, weights, range(EARLY, 6))
    fields = grid[:, pl.ds(pl.multiple_of(core * GQ, GQ), GQ)].astype(F32)
    terms = half_term(own[0], spread, 2 + core) + half_term(own[1], spread, 3 - core)
    base[...] = fields + terms


def sent_body(info, sent, spread, base, total):
    core = info[0]
    total[...] = (
        base[...]
        + half_term(sent[0], spread, 5 * core)
        + half_term(sent[1], spread, 3 * core + 1)
    )


def decode_body(info, swapped_rows, spread, total, out):
    other = 1 - info[0]
    terms = half_term(swapped_rows[0], spread, 5 * other)
    terms = terms + half_term(swapped_rows[1], spread, 3 * other + 1)
    out[...] = (total[...] + terms).astype(BF16)


def swapped(value):
    return lax.ppermute(value, "mp", [(0, 1), (1, 0)])


def up_and_down(value):
    bands = lax.axis_size("band")
    pairs = [(2 * i, 2 * i + 2) for i in range(bands - 1)]
    pairs += [(2 * i + 3, 2 * i + 1) for i in range(bands - 1)]
    return lax.ppermute(value, ("band", "mp"), pairs)


def over_the_edge(value):
    bands = lax.axis_size("band")
    pairs = [(2 * i + 1, 2 * i + 2) for i in range(bands - 1)]
    pairs += [(j, i) for i, j in pairs]
    return lax.ppermute(value, ("band", "mp"), pairs)


def on_device(
    grid_fields, w_in, enc_src, enc_dst, enc_weight, enc_count, norm_gain, w_qkv, w_out_attn,
    offsets, w_decode, dec_src, dec_dst, dec_weight,
):
    band = lax.axis_index("band")
    core = lax.axis_index("mp")
    bands = lax.axis_size("band")
    device = 2 * band + core
    grid = grid_fields.T
    grid_sent = up_and_down(grid)
    info = jnp.stack([
        core,
        enc_count[0],
        (band - 1) * G_BAND,
        device * ROWS,
        (device == 0).astype(jnp.int32),
        (device == 2 * bands - 1).astype(jnp.int32),
        (band - 1) * 2 * ROWS,
        device * GQ,
    ]).astype(jnp.int32)
    win_peer = swapped(w_in)
    dec_own = w_decode.T
    dec_peer = swapped(dec_own)
    qkv_own = w_qkv.transpose(1, 0, 2)
    qkv_peer = swapped(qkv_own)
    edges = jax.ShapeDtypeStruct(enc_src.shape, jnp.int32)
    spread_out = jax.ShapeDtypeStruct((6 * ROWS, GQ), BF16)
    spread_scratch = [
        pltpu.VMEM(dec_src.shape, jnp.int32),
        pltpu.VMEM((GQ, DEC_ROUNDS * TILE), BF16),
        pltpu.VMEM(dec_weight.shape, F32),
    ]
    spread = call(
        early_body, (info, dec_src, dec_dst, dec_weight), 1, spread_out,
        spread_scratch, 5 * 10 ** 9, 10, "early",
    )
    spread, info = lax.optimization_barrier((spread, info))
    sources, targets, weights, gain, w_in_all, dec_all = call(
        prepare_body,
        (info, enc_src, enc_dst, enc_weight, norm_gain.reshape(1, D), w_in, win_peer,
         dec_own, dec_peer),
        1,
        [
            edges,
            edges,
            jax.ShapeDtypeStruct(enc_weight.shape, F32),
            jax.ShapeDtypeStruct((1, D), F32),
            jax.ShapeDtypeStruct((LANES, D), BF16),
            jax.ShapeDtypeStruct((LANES, D), BF16),
        ],
        [pltpu.VMEM((LANES, D), F32)],
        5 * 10 ** 9, 6, "prepare",
    )
    grid_sent, w_in_all, spread = lax.optimization_barrier((grid_sent, w_in_all, spread))
    grid_swapped = swapped(grid_sent)
    grid_rows, fold_own = call(
        unpack_body,
        (info, grid, grid_sent, w_out_attn, dec_all),
        1,
        [
            jax.ShapeDtypeStruct((3 * G_BAND, LANES), F32),
            jax.ShapeDtypeStruct((2 * LANES, HALF), BF16),
        ],
        [pltpu.VMEM((LANES, G_BAND), F32)],
        2 * 10 ** 9, 6, "unpack",
    )
    fold_peer = swapped(fold_own)
    band_rows = jax.ShapeDtypeStruct((ROWS, D), BF16)
    step_buffers = [pltpu.VMEM((STEP, LANES), F32)] * 2 + [pltpu.VMEM((ROWS, D), F32)]
    _, mesh_zero, normed, to_band = call(
        encode_body,
        (info, sources, grid_rows, grid_swapped, w_in_all, targets, weights, gain),
        2,
        [
            jax.ShapeDtypeStruct((3 * G_BAND, LANES), F32),
            band_rows,
            band_rows,
            jax.ShapeDtypeStruct((WIN, D), BF16),
        ],
        [pltpu.VMEM((LANES, G_BAND), F32)] + step_buffers,
        7 * 10 ** 9, 14, "encode", {2: 0},
    )
    halo_band = over_the_edge(to_band)
    queries, keys, values_t, keys_sent, values_sent, straight = call(
        project_body,
        (info, normed, qkv_own, qkv_peer, mesh_zero, dec_all),
        1,
        [
            jax.ShapeDtypeStruct((ROWS, D), BF16),
            jax.ShapeDtypeStruct((ROWS, D), BF16),
            jax.ShapeDtypeStruct((D, ROWS), BF16),
            jax.ShapeDtypeStruct((WIN, D), BF16),
            jax.ShapeDtypeStruct((D, WIN), BF16),
            jax.ShapeDtypeStruct((LANES, ROWS), F32),
        ],
        [],
        6 * 10 ** 9, 10, "project",
    )
    peer_keys, peer_values = swapped(keys_sent), swapped(values_sent)
    sums, stats, mask = call(
        own_body,
        (offsets, queries, keys, values_t),
        1,
        [
            jax.ShapeDtypeStruct((D, ROWS), F32),
            jax.ShapeDtypeStruct((D // LANES, 8, 2 * ROWS), F32),
            jax.ShapeDtypeStruct((SPAN, TILE), BF16),
        ],
        [pltpu.VMEM((ROWS, 2 * GROUP * TILE), F32)] * 2
        + [pltpu.VMEM((8, SPAN + TILE), F32), pltpu.VMEM((SPAN, TILE), F32)],
        8 * 10 ** 9, 12, "own",
    )
    projected = call(
        attend_body,
        (info, halo_band, peer_keys, peer_values, queries, sums, stats, mask, qkv_own,
         qkv_peer, straight, fold_own, fold_peer),
        1,
        jax.ShapeDtypeStruct((C, ROWS), BF16),
        [
            pltpu.VMEM((2 * WIN, D), BF16),
            pltpu.VMEM((D, 2 * WIN), BF16),
            pltpu.VMEM((TILES, WIN, TILE), BF16),
            pltpu.VMEM((D, ROWS), BF16),
            pltpu.VMEM((WIN, 2 * GROUP * TILE), F32),
            pltpu.VMEM((WIN, 2 * GROUP * TILE), F32),
        ],
        10 ** 10, 16, "attend",
    )
    own_pair = jnp.stack([projected, swapped(projected)])
    pair_sent = up_and_down(own_pair)
    spread, base = call(
        spread_body,
        (info, spread, own_pair, dec_src, dec_dst, dec_weight, grid),
        1,
        [spread_out, jax.ShapeDtypeStruct((C, GQ), F32)],
        spread_scratch, 8 * 10 ** 9, 10, "spread", {1: 0},
    )
    pair_sent, base = lax.optimization_barrier((pair_sent, base))
    pair_swapped = swapped(pair_sent)
    sums_out = jax.ShapeDtypeStruct((C, GQ), F32)
    total = call(
        sent_body, (info, pair_sent, spread, base), 1, sums_out, [],
        10 ** 9, 6, "sent",
    )
    return call(
        decode_body, (info, pair_swapped, spread, total), 1,
        jax.ShapeDtypeStruct((C, GQ), BF16), [], 10 ** 9, 6, "decode",
    ).T


def solution(mesh):
    return jax.shard_map(
        on_device,
        mesh=mesh,
        in_specs=(
            P("band", None),
            P(None, "mp"),
            P("band", None),
            P("band", None),
            P("band", None),
            P("band"),
            P(),
            P(None, None, "mp"),
            P("mp", None),
            P(),
            P("mp", None),
            P(("band", "mp"), None),
            P(("band", "mp"), None),
            P(("band", "mp"), None),
        ),
        out_specs=P(("band", "mp"), None),
        check_vma=False,
    )
```

```python
import math
import jax
import jax.numpy as jnp
from jax import lax
from jax.experimental import pallas as pl
from jax.experimental.pallas import tpu as pltpu
from jax.sharding import PartitionSpec as P

D = 1024
C = 100
LANES = 128
TILE = 128
ROWS = 512
WIN = 384
K_OFF = 32
HALF = 512
G_BAND = 2048
EDGE_ROUNDS = 8
TILES = 4
STEP = 512
SPAN = TILE + 2 * WIN
GQ = 1024
DEC_ROUNDS = 3
DEC_TILES = 8
GROUP = 2
EARLY = 2
MASKED = -1e30
SCALE = 64 ** (-0.5) * math.log2(math.e)
F32 = jnp.float32
BF16 = jnp.bfloat16
MIB = 1024 * 1024


def vmem():
    return pl.BlockSpec(memory_space=pltpu.VMEM)


def smem():
    return pl.BlockSpec(memory_space=pltpu.SMEM)


def call(body, operands, smem_count, outs, scratch, flops, room, name, aliases={}):
    specs = [smem()] * smem_count + [vmem()] * (len(operands) - smem_count)
    return pl.pallas_call(
        body,
        out_shape=outs,
        in_specs=specs,
        out_specs=jax.tree.map(lambda _: vmem(), outs),
        scratch_shapes=scratch,
        compiler_params=pltpu.CompilerParams(vmem_limit_bytes=room * MIB),
        cost_estimate=pl.CostEstimate(flops=flops, bytes_accessed=2 * 10 ** 6, transcendentals=0),
        input_output_aliases=aliases,
        name=name,
    )(*operands)


def matmul(a, b):
    return jnp.dot(a, b, preferred_element_type=F32)


def matmul_t(a, b):
    return lax.dot_general(a, b, (((1,), (1,)), ((), ())), preferred_element_type=F32)


def to_rows(part, wide, rows, begin):
    wide[:C, :] = part[...].astype(F32)
    for block in range(G_BAND // LANES):
        columns = slice(block * LANES, (block + 1) * LANES)
        place = pl.multiple_of(begin + block * LANES, LANES)
        rows[pl.ds(place, LANES), :] = wide[:, columns].T


def by_core(core, wide, own, peer):
    @pl.when(core == 0)
    def _():
        wide[:C, :HALF] = own[...].astype(F32)
        wide[:C, HALF:] = peer[...].astype(F32)

    @pl.when(core != 0)
    def _():
        wide[:C, :HALF] = peer[...].astype(F32)
        wide[:C, HALF:] = own[...].astype(F32)


def make_mask(offsets, mask, strip, mask_wide):
    lane = lax.broadcasted_iota(jnp.int32, strip.shape, 1)
    away = lax.broadcasted_iota(jnp.int32, strip.shape, 0) + (SPAN - WIN - 8) - lane
    hit = away == offsets[0]
    for k in range(1, K_OFF):
        hit = hit | (away == offsets[k])
    strip[...] = jnp.where(hit, 0.0, MASKED)
    for begin in range(0, SPAN, 8):
        shift = SPAN - 8 - begin
        mask_wide[begin : begin + 8, :] = strip[:, shift : shift + TILE]
    mask[...] = mask_wide[...].astype(BF16)


def prepare_body(info, src, dst, weight, gain, sources, targets, weights, gains):
    slots = lax.broadcasted_iota(jnp.int32, weights.shape, 0)
    weights[...] = jnp.where(slots < info[1], weight[...].astype(F32), 0.0)
    targets[...] = dst[...] - info[3]
    sources[...] = src[...] - info[2]
    gains[...] = gain[...]


def unpack_body(info, grid, sent, rows, wide):
    wide[...] = jnp.zeros_like(wide)
    to_rows(grid, wide, rows, G_BAND)
    to_rows(sent, wide, rows, info[0] * 2 * G_BAND)


def encode_tiles(
    core, order, src, w_in, targets, weights, gain, rows, mesh_zero, normed, first, second, total
):
    row_slots = lax.broadcasted_iota(jnp.int32, (TILE, LANES), 0)
    steps = EDGE_ROUNDS * TILE // STEP
    rounds = STEP // TILE
    count = len(order) * steps

    def tile_of(step):
        place = order[0] + step // steps
        return jnp.where(core == 0, place, TILES - 1 - place)

    def slot_of(step, part):
        return (step % steps * rounds + part) * 2 * TILES + core * TILES + tile_of(step)

    def gather(step, buffer):
        for part in range(rounds):
            slot = slot_of(step, part)
            for edge in range(TILE):
                index = src[slot, edge]
                buffer[pl.ds(part * TILE + edge, 1), :] = rows[pl.ds(index, 1), :]

    def add(step, buffer):
        tile = tile_of(step)
        half = matmul(buffer[...].astype(BF16), w_in[...])
        embedded = (half + half * jnp.tanh(half)).astype(BF16)
        tables = []
        for part in range(rounds):
            slot = slot_of(step, part)
            target = targets[pl.ds(slot, 1), :] - tile * TILE
            tables.append(jnp.where(row_slots == target, weights[pl.ds(slot, 1), :], 0.0))
        table = jnp.concatenate(tables, axis=1).astype(BF16)
        place = pl.ds(pl.multiple_of(tile * TILE, TILE), TILE)
        total[place, :] += matmul(table, embedded)

    for step in range(0, count, steps):
        place = pl.ds(pl.multiple_of(tile_of(step) * TILE, TILE), TILE)
        total[place, :] = jnp.zeros((TILE, D), F32)
    gather(0, first)

    def pair(index, carry):
        gather(2 * index + 1, second)
        add(2 * index, first)
        if count > 2:
            gather(jnp.minimum(2 * index + 2, count - 1), first)
        add(2 * index + 1, second)
        return carry

    lax.fori_loop(0, count // 2, pair, 0)

    def finish(step, carry):
        place = pl.ds(pl.multiple_of(tile_of(step * steps) * TILE, TILE), TILE)
        rounded = total[place, :].astype(BF16)
        mesh_zero[place, :] = rounded
        values = rounded.astype(F32)
        inverse = lax.rsqrt(jnp.mean(values * values, axis=1, keepdims=True) + 1e-05)
        normed[place, :] = (values * inverse * gain[...]).astype(BF16)
        return carry

    lax.fori_loop(0, len(order), finish, 0)


def encode_body(
    info, src, grid_rows, swapped_rows, win_own, win_peer, targets, weights, gain,
    rows, mesh_zero, normed, to_band,
    wide, w_wide, w_in, first, second, total,
):
    core = info[0]
    w_wide[...] = jnp.zeros_like(w_wide)
    by_core(core, w_wide, win_own, win_peer)
    w_in[...] = (w_wide[...] * 0.5).astype(BF16)
    wide[...] = jnp.zeros_like(wide)
    to_rows(swapped_rows, wide, rows, (1 - core) * 2 * G_BAND)
    encode_tiles(
        core, range(TILES), src, w_in, targets, weights, gain, rows, mesh_zero, normed,
        first, second, total,
    )
    to_band[...] = normed[pl.ds(pl.multiple_of(core * TILE, TILE), WIN), :]


def identity_pair():
    row = lax.broadcasted_iota(jnp.int32, (TILE, LANES), 0)
    lane = lax.broadcasted_iota(jnp.int32, (TILE, LANES), 1)
    eye = jnp.where(row == lane, 1.0, 0.0).astype(BF16)
    return jnp.concatenate([eye, eye], axis=0), lane


def lanes_of(pair):
    return pl.ds(pl.multiple_of(pair * LANES, LANES), LANES)


def rows_of(block):
    return slice(block * TILE, (block + 1) * TILE)


def score_block(query, lane, eyes, keys, mask, scores):
    query = query.astype(F32)
    stacked = jnp.concatenate(
        [jnp.where(lane < 64, query, 0.0), jnp.where(lane < 64, 0.0, query)], axis=0
    ).astype(BF16)
    scores[...] = matmul_t(
        jnp.concatenate([keys, mask], axis=1), jnp.concatenate([stacked, eyes], axis=1)
    )


def column_top(scores):
    top = scores[:TILE, :]
    for begin in range(TILE, scores.shape[0], TILE):
        top = jnp.maximum(top, scores[begin : begin + TILE, :])
    return jnp.max(top, axis=0, keepdims=True)


def weigh(scores, top, values):
    expos = jnp.exp2(scores[...] - top).astype(BF16)
    ones = jnp.ones((16, scores.shape[0]), BF16)
    result = matmul(jnp.concatenate([values, ones], axis=0), expos)
    both = jnp.concatenate([result[:64, :TILE], result[64:TILE, TILE:]], axis=0)
    return both, result[TILE : TILE + 1, :]


def pipeline(score, finish, first, second):
    buffers = (first, second)
    groups = D // LANES // GROUP

    def part_of(buffer, member):
        return buffer.at[:, member * 2 * TILE : (member + 1) * 2 * TILE]

    for member in range(GROUP):
        score(member, 0, part_of(first, member))

    def head_group(group, carry):
        for block in range(TILES):
            here, ahead = buffers[block % 2], buffers[(block + 1) % 2]
            for member in range(GROUP):
                if block + 1 < TILES:
                    pair = group * GROUP + member
                else:
                    pair = jnp.minimum(group + 1, groups - 1) * GROUP + member
                score(pair, (block + 1) % TILES, part_of(ahead, member))
            for member in range(GROUP):
                finish(group * GROUP + member, block, part_of(here, member))
        return carry

    lax.fori_loop(0, groups, head_group, 0)


def project_body(
    info, normed, w_own, w_peer, mesh_zero, dec_own, dec_peer, w_out,
    queries, keys, values_t, keys_sent, values_sent, straight, fold,
    w_wide, w_decode,
):
    w_wide[...] = jnp.zeros_like(w_wide)
    by_core(info[0], w_wide, dec_own, dec_peer)
    w_decode[...] = w_wide[...].astype(BF16)
    folded = matmul_t(w_decode[...], w_out[...])
    upper = folded.astype(BF16)
    fold[:LANES, :] = upper
    fold[LANES:, :] = (folded - upper.astype(F32)).astype(BF16)
    rows = normed[...]
    straight[...] = matmul_t(w_decode[...], mesh_zero[...])
    for half, weight in enumerate((w_own, w_peer)):
        place = slice(half * HALF, (half + 1) * HALF)
        keys[:, place] = matmul(rows, weight[1]).astype(BF16)
        values_t[place, :] = matmul(rows, weight[2]).T.astype(BF16)
        queries[:, place] = (matmul(rows, weight[0]) * SCALE).astype(BF16)

    @pl.when(info[0] == 0)
    def _():
        for half in range(2):
            place = slice(half * HALF, (half + 1) * HALF)
            other = slice((1 - half) * HALF, (2 - half) * HALF)
            keys_sent[:, other] = keys[ROWS - WIN :, place]
            values_sent[other, :] = values_t[place, ROWS - WIN :]

    @pl.when(info[0] != 0)
    def _():
        for half in range(2):
            place = slice(half * HALF, (half + 1) * HALF)
            other = slice((1 - half) * HALF, (2 - half) * HALF)
            keys_sent[:, other] = keys[:WIN, place]
            values_sent[other, :] = values_t[place, :WIN]


def own_body(
    offsets, queries, keys, values_t, sums, stats, mask, first, second, strip, mask_wide
):
    make_mask(offsets, mask, strip, mask_wide)
    eyes, lane = identity_pair()

    def score(pair, block, scores):
        begin = WIN - block * TILE
        score_block(
            queries[rows_of(block), lanes_of(pair)], lane, eyes, keys[:, lanes_of(pair)],
            mask[begin : begin + ROWS, :], scores,
        )

    def finish(pair, block, scores):
        top = column_top(scores)
        both, total = weigh(scores, top, values_t[lanes_of(pair), :])
        sums[lanes_of(pair), rows_of(block)] = both
        columns = slice(2 * block * TILE, 2 * (block + 1) * TILE)
        stats[pair, 0:1, columns] = top
        stats[pair, 1:2, columns] = total

    pipeline(score, finish, first, second)


def attend_body(
    info, halo, peer_keys, peer_values, queries, sums, stats, mask, w_own, w_peer,
    straight, fold_own, fold_peer,
    projected,
    keys, values_t, masks, attended, first, second,
):
    core, first_device, last_device = info[0], info[4], info[5]

    @pl.when(core == 0)
    def _():
        keys[WIN:, :] = peer_keys[...]
        values_t[:, WIN:] = peer_values[...]

    @pl.when(core != 0)
    def _():
        keys[:WIN, :] = peer_keys[...]
        values_t[:, :WIN] = peer_values[...]

    begin = pl.ds(pl.multiple_of(core * WIN, WIN), WIN)
    beside = halo[...]
    for half, weight in enumerate((w_own, w_peer)):
        place = slice(half * HALF, (half + 1) * HALF)
        keys[begin, place] = matmul(beside, weight[1]).astype(BF16)
        values_t[place, begin] = matmul(beside, weight[2]).T.astype(BF16)
    low = jnp.where(first_device == 1, MASKED, 0.0)
    high = jnp.where(last_device == 1, MASKED, 0.0)
    for block in range(TILES):
        below, above = WIN - block * TILE, SPAN - block * TILE
        if below > 0:
            masks[block, :below, :] = (mask[:below, :].astype(F32) + low).astype(BF16)
        if above < SPAN:
            masks[block, below:, :] = (mask[above:, :].astype(F32) + high).astype(BF16)
    eyes, lane = identity_pair()

    def score(pair, block, scores):
        seen = slice(block * TILE, block * TILE + WIN)
        score_block(
            queries[rows_of(block), lanes_of(pair)], lane, eyes, keys[seen, lanes_of(pair)],
            masks[block], scores,
        )

    def finish(pair, block, scores):
        seen = slice(block * TILE, block * TILE + WIN)
        columns = slice(2 * block * TILE, 2 * (block + 1) * TILE)
        old, sum_old = stats[pair, 0:1, columns], stats[pair, 1:2, columns]
        top = jnp.maximum(old, column_top(scores))
        both, total = weigh(scores, top, values_t[lanes_of(pair), seen])
        shrink = jnp.exp2(old - top)
        inverse = 1.0 / (sum_old * shrink + total)
        shrink = shrink * inverse
        before = sums[lanes_of(pair), rows_of(block)]
        result = jnp.concatenate([
            before[:64] * shrink[:, :TILE] + both[:64] * inverse[:, :TILE],
            before[64:] * shrink[:, TILE:] + both[64:] * inverse[:, TILE:],
        ], axis=0)
        attended[lanes_of(pair), rows_of(block)] = result.astype(BF16)

    pipeline(score, finish, first, second)
    both = matmul(fold_own[...], attended[:HALF, :]) + matmul(fold_peer[...], attended[HALF:, :])
    projected[...] = (straight[...] + both[:LANES, :] + both[LANES:, :])[:C, :].astype(BF16)


def pair_term(core, pair, spread, place):
    rows = pl.ds(pl.multiple_of(place * ROWS, 2 * ROWS), 2 * ROWS)
    low = jnp.where(core == 0, pair[0].astype(F32), pair[1].astype(F32))
    high = jnp.where(core == 0, pair[1].astype(F32), pair[0].astype(F32))
    halves = jnp.concatenate([low, high], axis=1).astype(BF16)
    return matmul(halves, spread[rows, :])


def spread_halves(info, src, dst, weight, spread, sources, tables, weights, places):
    mesh_base, row_base = info[6], info[7]
    sources[...] = src[...] - mesh_base
    weights[...] = weight[...].astype(F32)
    row_slots = lax.broadcasted_iota(jnp.int32, (TILE, LANES), 0)
    for tile in range(DEC_TILES):
        for part in range(DEC_ROUNDS):
            slot = slice(part * DEC_TILES + tile, part * DEC_TILES + tile + 1)
            target = dst[slot, :] - (row_base + tile * TILE)
            tables[rows_of(tile), rows_of(part)] = jnp.where(
                row_slots == target, weights[slot, :], 0.0
            ).astype(BF16)
    mesh_slots = lax.broadcasted_iota(jnp.int32, (ROWS, LANES), 0)

    def half(place, carry):
        begin = pl.multiple_of(place * ROWS, ROWS)
        for tile in range(DEC_TILES):
            picks = []
            for part in range(DEC_ROUNDS):
                slot = slice(part * DEC_TILES + tile, part * DEC_TILES + tile + 1)
                hit = mesh_slots == sources[slot, :] - begin
                picks.append(jnp.where(hit, 1.0, 0.0).astype(BF16))
            spread[pl.ds(begin, ROWS), rows_of(tile)] = matmul_t(
                jnp.concatenate(picks, axis=1), tables[rows_of(tile), :]
            ).astype(BF16)
        return carry

    lax.fori_loop(places[0], places[-1] + 1, half, 0)


def early_body(info, src, dst, weight, spread, sources, tables, weights):
    spread_halves(info, src, dst, weight, spread, sources, tables, weights, range(EARLY))


def spread_body(
    info, spread_in, own, src, dst, weight, grid, spread, base, sources, tables, weights
):
    core = info[0]
    spread_halves(info, src, dst, weight, spread, sources, tables, weights, range(EARLY, 6))
    fields = grid[:, pl.ds(pl.multiple_of(core * GQ, GQ), GQ)].astype(F32)
    base[...] = fields + pair_term(core, own, spread, 2)


def sent_body(info, sent, spread, base, total):
    core = info[0]
    total[...] = base[...] + pair_term(core, sent, spread, 4 * core)


def decode_body(info, swapped_rows, spread, total, out):
    other = 1 - info[0]
    out[...] = (total[...] + pair_term(other, swapped_rows, spread, 4 * other)).astype(BF16)


def swapped(value):
    return lax.ppermute(value, "mp", [(0, 1), (1, 0)])


def up_and_down(value):
    bands = lax.axis_size("band")
    pairs = [(2 * i, 2 * i + 2) for i in range(bands - 1)]
    pairs += [(2 * i + 3, 2 * i + 1) for i in range(bands - 1)]
    return lax.ppermute(value, ("band", "mp"), pairs)


def over_the_edge(value):
    bands = lax.axis_size("band")
    pairs = [(2 * i + 1, 2 * i + 2) for i in range(bands - 1)]
    pairs += [(j, i) for i, j in pairs]
    return lax.ppermute(value, ("band", "mp"), pairs)


def on_device(
    grid_fields, w_in, enc_src, enc_dst, enc_weight, enc_count, norm_gain, w_qkv, w_out_attn,
    offsets, w_decode, dec_src, dec_dst, dec_weight,
):
    band = lax.axis_index("band")
    core = lax.axis_index("mp")
    bands = lax.axis_size("band")
    device = 2 * band + core
    grid = grid_fields.T
    grid_sent = up_and_down(grid)
    info = jnp.stack([
        core,
        enc_count[0],
        (band - 1) * G_BAND,
        device * ROWS,
        (device == 0).astype(jnp.int32),
        (device == 2 * bands - 1).astype(jnp.int32),
        (band - 1) * 2 * ROWS,
        device * GQ,
    ]).astype(jnp.int32)
    dec_own = w_decode.T
    qkv_own = w_qkv.transpose(1, 0, 2)
    edges = jax.ShapeDtypeStruct(enc_src.shape, jnp.int32)
    spread_out = jax.ShapeDtypeStruct((6 * ROWS, GQ), BF16)
    spread_scratch = [
        pltpu.VMEM(dec_src.shape, jnp.int32),
        pltpu.VMEM((GQ, DEC_ROUNDS * TILE), BF16),
        pltpu.VMEM(dec_weight.shape, F32),
    ]
    spread = call(
        early_body, (info, dec_src, dec_dst, dec_weight), 1, spread_out,
        spread_scratch, 5 * 10 ** 9, 10, "early",
    )
    spread, info = lax.optimization_barrier((spread, info))
    sources, targets, weights, gain = call(
        prepare_body,
        (info, enc_src, enc_dst, enc_weight, norm_gain.reshape(1, D)),
        1,
        [
            edges,
            edges,
            jax.ShapeDtypeStruct(enc_weight.shape, F32),
            jax.ShapeDtypeStruct((1, D), F32),
        ],
        [],
        5 * 10 ** 9, 4, "prepare",
    )
    grid_sent, gain, spread, w_in = lax.optimization_barrier((grid_sent, gain, spread, w_in))
    grid_swapped, win_peer = swapped(grid_sent), swapped(w_in)
    grid_rows = call(
        unpack_body,
        (info, grid, grid_sent),
        1,
        jax.ShapeDtypeStruct((3 * G_BAND, LANES), F32),
        [pltpu.VMEM((LANES, G_BAND), F32)],
        2 * 10 ** 9, 6, "unpack",
    )
    grid_swapped, grid_rows, win_peer, dec_own, qkv_own = lax.optimization_barrier(
        (grid_swapped, grid_rows, win_peer, dec_own, qkv_own)
    )
    dec_peer, qkv_peer = swapped(dec_own), swapped(qkv_own)
    band_rows = jax.ShapeDtypeStruct((ROWS, D), BF16)
    step_buffers = [pltpu.VMEM((STEP, LANES), F32)] * 2 + [pltpu.VMEM((ROWS, D), F32)]
    _, mesh_zero, normed, to_band = call(
        encode_body,
        (info, sources, grid_rows, grid_swapped, w_in, win_peer, targets, weights, gain),
        2,
        [
            jax.ShapeDtypeStruct((3 * G_BAND, LANES), F32),
            band_rows,
            band_rows,
            jax.ShapeDtypeStruct((WIN, D), BF16),
        ],
        [
            pltpu.VMEM((LANES, G_BAND), F32),
            pltpu.VMEM((LANES, D), F32),
            pltpu.VMEM((LANES, D), BF16),
        ] + step_buffers,
        7 * 10 ** 9, 14, "encode", {2: 0},
    )
    halo_band = over_the_edge(to_band)
    queries, keys, values_t, keys_sent, values_sent, straight, fold_own = call(
        project_body,
        (info, normed, qkv_own, qkv_peer, mesh_zero, dec_own, dec_peer, w_out_attn),
        1,
        [
            jax.ShapeDtypeStruct((ROWS, D), BF16),
            jax.ShapeDtypeStruct((ROWS, D), BF16),
            jax.ShapeDtypeStruct((D, ROWS), BF16),
            jax.ShapeDtypeStruct((WIN, D), BF16),
            jax.ShapeDtypeStruct((D, WIN), BF16),
            jax.ShapeDtypeStruct((LANES, ROWS), F32),
            jax.ShapeDtypeStruct((2 * LANES, HALF), BF16),
        ],
        [pltpu.VMEM((LANES, D), F32), pltpu.VMEM((LANES, D), BF16)],
        6 * 10 ** 9, 10, "project",
    )
    peer_keys, peer_values = swapped(keys_sent), swapped(values_sent)
    fold_peer = swapped(fold_own)
    sums, stats, mask = call(
        own_body,
        (offsets, queries, keys, values_t),
        1,
        [
            jax.ShapeDtypeStruct((D, ROWS), F32),
            jax.ShapeDtypeStruct((D // LANES, 8, 2 * ROWS), F32),
            jax.ShapeDtypeStruct((SPAN, TILE), BF16),
        ],
        [pltpu.VMEM((ROWS, 2 * GROUP * TILE), F32)] * 2
        + [pltpu.VMEM((8, SPAN + TILE), F32), pltpu.VMEM((SPAN, TILE), F32)],
        8 * 10 ** 9, 12, "own",
    )
    projected = call(
        attend_body,
        (info, halo_band, peer_keys, peer_values, queries, sums, stats, mask, qkv_own,
         qkv_peer, straight, fold_own, fold_peer),
        1,
        jax.ShapeDtypeStruct((C, ROWS), BF16),
        [
            pltpu.VMEM((2 * WIN, D), BF16),
            pltpu.VMEM((D, 2 * WIN), BF16),
            pltpu.VMEM((TILES, WIN, TILE), BF16),
            pltpu.VMEM((D, ROWS), BF16),
            pltpu.VMEM((WIN, 2 * GROUP * TILE), F32),
            pltpu.VMEM((WIN, 2 * GROUP * TILE), F32),
        ],
        10 ** 10, 16, "attend",
    )
    own_pair = jnp.stack([projected, swapped(projected)])
    pair_sent = up_and_down(own_pair)
    spread, base = call(
        spread_body,
        (info, spread, own_pair, dec_src, dec_dst, dec_weight, grid),
        1,
        [spread_out, jax.ShapeDtypeStruct((C, GQ), F32)],
        spread_scratch, 8 * 10 ** 9, 10, "spread", {1: 0},
    )
    pair_sent, base = lax.optimization_barrier((pair_sent, base))
    pair_swapped = swapped(pair_sent)
    sums_out = jax.ShapeDtypeStruct((C, GQ), F32)
    total = call(
        sent_body, (info, pair_sent, spread, base), 1, sums_out, [],
        10 ** 9, 6, "sent",
    )
    return call(
        decode_body, (info, pair_swapped, spread, total), 1,
        jax.ShapeDtypeStruct((C, GQ), BF16), [], 10 ** 9, 6, "decode",
    ).T


def solution(mesh):
    return jax.shard_map(
        on_device,
        mesh=mesh,
        in_specs=(
            P("band", None),
            P(None, "mp"),
            P("band", None),
            P("band", None),
            P("band", None),
            P("band"),
            P(),
            P(None, None, "mp"),
            P("mp", None),
            P(),
            P("mp", None),
            P(("band", "mp"), None),
            P(("band", "mp"), None),
            P(("band", "mp"), None),
        ),
        out_specs=P(("band", "mp"), None),
        check_vma=False,
    )
```

```python
import math
import jax
import jax.numpy as jnp
from jax import lax
from jax.experimental import pallas as pl
from jax.experimental.pallas import tpu as pltpu
from jax.sharding import PartitionSpec as P

D = 1024
C = 100
LANES = 128
TILE = 128
ROWS = 512
WIN = 384
K_OFF = 32
HALF = 512
G_BAND = 2048
EDGE_ROUNDS = 8
TILES = 4
STEP = 512
SPAN = TILE + 2 * WIN
GQ = 1024
DEC_ROUNDS = 3
DEC_TILES = 8
GROUP = 2
EARLY = 2
MASKED = -1e30
SCALE = 64 ** (-0.5) * math.log2(math.e)
F32 = jnp.float32
BF16 = jnp.bfloat16
MIB = 1024 * 1024


def vmem():
    return pl.BlockSpec(memory_space=pltpu.VMEM)


def smem():
    return pl.BlockSpec(memory_space=pltpu.SMEM)


def call(body, operands, smem_count, outs, scratch, flops, room, name, aliases={}):
    specs = [smem()] * smem_count + [vmem()] * (len(operands) - smem_count)
    return pl.pallas_call(
        body,
        out_shape=outs,
        in_specs=specs,
        out_specs=jax.tree.map(lambda _: vmem(), outs),
        scratch_shapes=scratch,
        compiler_params=pltpu.CompilerParams(vmem_limit_bytes=room * MIB),
        cost_estimate=pl.CostEstimate(flops=flops, bytes_accessed=2 * 10 ** 6, transcendentals=0),
        input_output_aliases=aliases,
        name=name,
    )(*operands)


def matmul(a, b):
    return jnp.dot(a, b, preferred_element_type=F32)


def matmul_t(a, b):
    return lax.dot_general(a, b, (((1,), (1,)), ((), ())), preferred_element_type=F32)


def to_rows(part, wide, rows, begin):
    wide[:C, :] = part[...].astype(F32)
    for block in range(G_BAND // LANES):
        columns = slice(block * LANES, (block + 1) * LANES)
        place = pl.multiple_of(begin + block * LANES, LANES)
        rows[pl.ds(place, LANES), :] = wide[:, columns].T


def by_core(core, wide, own, peer):
    @pl.when(core == 0)
    def _():
        wide[:C, :HALF] = own[...].astype(F32)
        wide[:C, HALF:] = peer[...].astype(F32)

    @pl.when(core != 0)
    def _():
        wide[:C, :HALF] = peer[...].astype(F32)
        wide[:C, HALF:] = own[...].astype(F32)


def make_mask(offsets, mask, strip, mask_wide):
    lane = lax.broadcasted_iota(jnp.int32, strip.shape, 1)
    away = lax.broadcasted_iota(jnp.int32, strip.shape, 0) + (SPAN - WIN - 8) - lane
    hit = away == offsets[0]
    for k in range(1, K_OFF):
        hit = hit | (away == offsets[k])
    strip[...] = jnp.where(hit, 0.0, MASKED)
    for begin in range(0, SPAN, 8):
        shift = SPAN - 8 - begin
        mask_wide[begin : begin + 8, :] = strip[:, shift : shift + TILE]
    mask[...] = mask_wide[...].astype(BF16)


def prepare_body(info, src, dst, weight, gain, sources, targets, weights, gains):
    slots = lax.broadcasted_iota(jnp.int32, weights.shape, 0)
    weights[...] = jnp.where(slots < info[1], weight[...].astype(F32), 0.0)
    targets[...] = dst[...] - info[3]
    sources[...] = src[...] - info[2]
    gains[...] = gain[...]


def unpack_body(info, grid, sent, rows, wide):
    wide[96:, :] = jnp.zeros((LANES - 96, G_BAND), F32)
    to_rows(grid, wide, rows, G_BAND)
    to_rows(sent, wide, rows, info[0] * 2 * G_BAND)


def encode_tiles(
    core, order, src, w_in, targets, weights, gain, rows, mesh_zero, normed, first, second, total
):
    row_slots = lax.broadcasted_iota(jnp.int32, (TILE, LANES), 0)
    steps = EDGE_ROUNDS * TILE // STEP
    rounds = STEP // TILE
    count = len(order) * steps

    def tile_of(step):
        place = order[0] + step // steps
        return jnp.where(core == 0, place, TILES - 1 - place)

    def slot_of(step, part):
        return (step % steps * rounds + part) * 2 * TILES + core * TILES + tile_of(step)

    def gather(step, buffer):
        for part in range(rounds):
            slot = slot_of(step, part)
            for edge in range(TILE):
                index = src[slot, edge]
                buffer[pl.ds(part * TILE + edge, 1), :] = rows[pl.ds(index, 1), :]

    def add(step, buffer):
        tile = tile_of(step)
        half = matmul(buffer[...].astype(BF16), w_in[...])
        embedded = (half + half * jnp.tanh(half)).astype(BF16)
        tables = []
        for part in range(rounds):
            slot = slot_of(step, part)
            target = targets[pl.ds(slot, 1), :] - tile * TILE
            tables.append(jnp.where(row_slots == target, weights[pl.ds(slot, 1), :], 0.0))
        table = jnp.concatenate(tables, axis=1).astype(BF16)
        place = pl.ds(pl.multiple_of(tile * TILE, TILE), TILE)
        total[place, :] += matmul(table, embedded)

    for step in range(0, count, steps):
        place = pl.ds(pl.multiple_of(tile_of(step) * TILE, TILE), TILE)
        total[place, :] = jnp.zeros((TILE, D), F32)
    gather(0, first)

    def pair(index, carry):
        gather(2 * index + 1, second)
        add(2 * index, first)
        if count > 2:
            gather(jnp.minimum(2 * index + 2, count - 1), first)
        add(2 * index + 1, second)
        return carry

    lax.fori_loop(0, count // 2, pair, 0)

    def finish(step, carry):
        place = pl.ds(pl.multiple_of(tile_of(step * steps) * TILE, TILE), TILE)
        rounded = total[place, :].astype(BF16)
        mesh_zero[place, :] = rounded
        values = rounded.astype(F32)
        inverse = lax.rsqrt(jnp.mean(values * values, axis=1, keepdims=True) + 1e-05)
        normed[place, :] = (values * inverse * gain[...]).astype(BF16)
        return carry

    lax.fori_loop(0, len(order), finish, 0)


def encode_body(
    info, src, grid_rows, swapped_rows, win_own, win_peer, targets, weights, gain,
    rows, mesh_zero, normed, to_band,
    wide, w_wide, w_in, first, second, total,
):
    core = info[0]
    w_wide[...] = jnp.zeros_like(w_wide)
    by_core(core, w_wide, win_own, win_peer)
    w_in[...] = (w_wide[...] * 0.5).astype(BF16)
    wide[96:, :] = jnp.zeros((LANES - 96, G_BAND), F32)
    to_rows(swapped_rows, wide, rows, (1 - core) * 2 * G_BAND)
    encode_tiles(
        core, range(TILES), src, w_in, targets, weights, gain, rows, mesh_zero, normed,
        first, second, total,
    )
    to_band[...] = normed[pl.ds(pl.multiple_of(core * TILE, TILE), WIN), :]


def identity_pair():
    row = lax.broadcasted_iota(jnp.int32, (TILE, LANES), 0)
    lane = lax.broadcasted_iota(jnp.int32, (TILE, LANES), 1)
    eye = jnp.where(row == lane, 1.0, 0.0).astype(BF16)
    return jnp.concatenate([eye, eye], axis=0), lane


def lanes_of(pair):
    return pl.ds(pl.multiple_of(pair * LANES, LANES), LANES)


def rows_of(block):
    return slice(block * TILE, (block + 1) * TILE)


def score_block(query, lane, eyes, keys, mask, scores):
    query = query.astype(F32)
    stacked = jnp.concatenate(
        [jnp.where(lane < 64, query, 0.0), jnp.where(lane < 64, 0.0, query)], axis=0
    ).astype(BF16)
    scores[...] = matmul_t(
        jnp.concatenate([keys, mask], axis=1), jnp.concatenate([stacked, eyes], axis=1)
    )


def column_top(scores):
    top = scores[:TILE, :]
    for begin in range(TILE, scores.shape[0], TILE):
        top = jnp.maximum(top, scores[begin : begin + TILE, :])
    return jnp.max(top, axis=0, keepdims=True)


def weigh(scores, top, values):
    expos = jnp.exp2(scores[...] - top).astype(BF16)
    ones = jnp.ones((16, scores.shape[0]), BF16)
    result = matmul(jnp.concatenate([values, ones], axis=0), expos)
    both = jnp.concatenate([result[:64, :TILE], result[64:TILE, TILE:]], axis=0)
    return both, result[TILE : TILE + 1, :]


def pipeline(score, finish, first, second):
    buffers = (first, second)
    groups = D // LANES // GROUP

    def part_of(buffer, member):
        return buffer.at[:, member * 2 * TILE : (member + 1) * 2 * TILE]

    for member in range(GROUP):
        score(member, 0, part_of(first, member))

    def head_group(group, carry):
        for block in range(TILES):
            here, ahead = buffers[block % 2], buffers[(block + 1) % 2]
            for member in range(GROUP):
                if block + 1 < TILES:
                    pair = group * GROUP + member
                else:
                    pair = jnp.minimum(group + 1, groups - 1) * GROUP + member
                score(pair, (block + 1) % TILES, part_of(ahead, member))
            for member in range(GROUP):
                finish(group * GROUP + member, block, part_of(here, member))
        return carry

    lax.fori_loop(0, groups, head_group, 0)


def project_body(
    info, normed, w_own, w_peer, mesh_zero, dec_own, dec_peer, w_out,
    queries, keys, values_t, keys_sent, values_sent, straight, fold,
    w_wide, w_decode,
):
    w_wide[...] = jnp.zeros_like(w_wide)
    by_core(info[0], w_wide, dec_own, dec_peer)
    w_decode[...] = w_wide[...].astype(BF16)
    folded = matmul_t(w_decode[...], w_out[...])
    upper = folded.astype(BF16)
    fold[:LANES, :] = upper
    fold[LANES:, :] = (folded - upper.astype(F32)).astype(BF16)
    rows = normed[...]
    straight[...] = matmul_t(w_decode[...], mesh_zero[...])
    for half, weight in enumerate((w_own, w_peer)):
        place = slice(half * HALF, (half + 1) * HALF)
        keys[:, place] = matmul(rows, weight[1]).astype(BF16)
        values_t[place, :] = matmul(rows, weight[2]).T.astype(BF16)
        queries[:, place] = (matmul(rows, weight[0]) * SCALE).astype(BF16)

    @pl.when(info[0] == 0)
    def _():
        for half in range(2):
            place = slice(half * HALF, (half + 1) * HALF)
            other = slice((1 - half) * HALF, (2 - half) * HALF)
            keys_sent[:, other] = keys[ROWS - WIN :, place]
            values_sent[other, :] = values_t[place, ROWS - WIN :]

    @pl.when(info[0] != 0)
    def _():
        for half in range(2):
            place = slice(half * HALF, (half + 1) * HALF)
            other = slice((1 - half) * HALF, (2 - half) * HALF)
            keys_sent[:, other] = keys[:WIN, place]
            values_sent[other, :] = values_t[place, :WIN]


def own_body(
    offsets, queries, keys, values_t, sums, stats, mask, first, second, strip, mask_wide
):
    make_mask(offsets, mask, strip, mask_wide)
    eyes, lane = identity_pair()

    def score(pair, block, scores):
        begin = WIN - block * TILE
        score_block(
            queries[rows_of(block), lanes_of(pair)], lane, eyes, keys[:, lanes_of(pair)],
            mask[begin : begin + ROWS, :], scores,
        )

    def finish(pair, block, scores):
        top = column_top(scores)
        both, total = weigh(scores, top, values_t[lanes_of(pair), :])
        sums[lanes_of(pair), rows_of(block)] = both
        columns = slice(2 * block * TILE, 2 * (block + 1) * TILE)
        stats[pair, 0:1, columns] = top
        stats[pair, 1:2, columns] = total

    pipeline(score, finish, first, second)


def attend_body(
    info, halo, peer_keys, peer_values, queries, sums, stats, mask, w_own, w_peer,
    straight, fold_own, fold_peer,
    projected,
    keys, values_t, masks, attended, first, second,
):
    core, first_device, last_device = info[0], info[4], info[5]

    @pl.when(core == 0)
    def _():
        keys[WIN:, :] = peer_keys[...]
        values_t[:, WIN:] = peer_values[...]

    @pl.when(core != 0)
    def _():
        keys[:WIN, :] = peer_keys[...]
        values_t[:, :WIN] = peer_values[...]

    begin = pl.ds(pl.multiple_of(core * WIN, WIN), WIN)
    beside = halo[...]
    for half, weight in enumerate((w_own, w_peer)):
        place = slice(half * HALF, (half + 1) * HALF)
        keys[begin, place] = matmul(beside, weight[1]).astype(BF16)
        values_t[place, begin] = matmul(beside, weight[2]).T.astype(BF16)
    low = jnp.where(first_device == 1, MASKED, 0.0)
    high = jnp.where(last_device == 1, MASKED, 0.0)
    for block in range(TILES):
        below, above = WIN - block * TILE, SPAN - block * TILE
        if below > 0:
            masks[block, :below, :] = (mask[:below, :].astype(F32) + low).astype(BF16)
        if above < SPAN:
            masks[block, below:, :] = (mask[above:, :].astype(F32) + high).astype(BF16)
    eyes, lane = identity_pair()

    def score(pair, block, scores):
        seen = slice(block * TILE, block * TILE + WIN)
        score_block(
            queries[rows_of(block), lanes_of(pair)], lane, eyes, keys[seen, lanes_of(pair)],
            masks[block], scores,
        )

    def finish(pair, block, scores):
        seen = slice(block * TILE, block * TILE + WIN)
        columns = slice(2 * block * TILE, 2 * (block + 1) * TILE)
        old, sum_old = stats[pair, 0:1, columns], stats[pair, 1:2, columns]
        top = jnp.maximum(old, column_top(scores))
        both, total = weigh(scores, top, values_t[lanes_of(pair), seen])
        shrink = jnp.exp2(old - top)
        inverse = 1.0 / (sum_old * shrink + total)
        shrink = shrink * inverse
        before = sums[lanes_of(pair), rows_of(block)]
        result = jnp.concatenate([
            before[:64] * shrink[:, :TILE] + both[:64] * inverse[:, :TILE],
            before[64:] * shrink[:, TILE:] + both[64:] * inverse[:, TILE:],
        ], axis=0)
        attended[lanes_of(pair), rows_of(block)] = result.astype(BF16)

    pipeline(score, finish, first, second)
    both = matmul(fold_own[...], attended[:HALF, :]) + matmul(fold_peer[...], attended[HALF:, :])
    projected[...] = (straight[...] + both[:LANES, :] + both[LANES:, :])[:C, :].astype(BF16)


def pair_term(core, pair, spread, place):
    rows = pl.ds(pl.multiple_of(place * ROWS, 2 * ROWS), 2 * ROWS)
    low = jnp.where(core == 0, pair[0].astype(F32), pair[1].astype(F32))
    high = jnp.where(core == 0, pair[1].astype(F32), pair[0].astype(F32))
    halves = jnp.concatenate([low, high], axis=1).astype(BF16)
    return matmul(halves, spread[rows, :])


def spread_halves(info, src, dst, weight, spread, sources, tables, weights, places):
    mesh_base, row_base = info[6], info[7]
    sources[...] = src[...] - mesh_base
    weights[...] = weight[...].astype(F32)
    row_slots = lax.broadcasted_iota(jnp.int32, (TILE, LANES), 0)
    for tile in range(DEC_TILES):
        for part in range(DEC_ROUNDS):
            slot = slice(part * DEC_TILES + tile, part * DEC_TILES + tile + 1)
            target = dst[slot, :] - (row_base + tile * TILE)
            tables[rows_of(tile), rows_of(part)] = jnp.where(
                row_slots == target, weights[slot, :], 0.0
            ).astype(BF16)
    mesh_slots = lax.broadcasted_iota(jnp.int32, (ROWS, LANES), 0)

    def half(place, carry):
        begin = pl.multiple_of(place * ROWS, ROWS)
        for tile in range(DEC_TILES):
            picks = []
            for part in range(DEC_ROUNDS):
                slot = slice(part * DEC_TILES + tile, part * DEC_TILES + tile + 1)
                hit = mesh_slots == sources[slot, :] - begin
                picks.append(jnp.where(hit, 1.0, 0.0).astype(BF16))
            spread[pl.ds(begin, ROWS), rows_of(tile)] = matmul_t(
                jnp.concatenate(picks, axis=1), tables[rows_of(tile), :]
            ).astype(BF16)
        return carry

    lax.fori_loop(places[0], places[-1] + 1, half, 0)


def early_body(info, src, dst, weight, spread, sources, tables, weights):
    spread_halves(info, src, dst, weight, spread, sources, tables, weights, range(EARLY))


def spread_body(
    info, spread_in, own, src, dst, weight, grid, spread, base, sources, tables, weights
):
    core = info[0]
    spread_halves(info, src, dst, weight, spread, sources, tables, weights, range(EARLY, 6))
    fields = grid[:, pl.ds(pl.multiple_of(core * GQ, GQ), GQ)].astype(F32)
    base[...] = fields + pair_term(core, own, spread, 2)


def sent_body(info, sent, spread, base, total):
    core = info[0]
    total[...] = base[...] + pair_term(core, sent, spread, 4 * core)


def decode_body(info, swapped_rows, spread, total, out):
    other = 1 - info[0]
    out[...] = (total[...] + pair_term(other, swapped_rows, spread, 4 * other)).astype(BF16)


def swapped(value):
    return lax.ppermute(value, "mp", [(0, 1), (1, 0)])


def up_and_down(value):
    bands = lax.axis_size("band")
    pairs = [(2 * i, 2 * i + 2) for i in range(bands - 1)]
    pairs += [(2 * i + 3, 2 * i + 1) for i in range(bands - 1)]
    return lax.ppermute(value, ("band", "mp"), pairs)


def over_the_edge(value):
    bands = lax.axis_size("band")
    pairs = [(2 * i + 1, 2 * i + 2) for i in range(bands - 1)]
    pairs += [(j, i) for i, j in pairs]
    return lax.ppermute(value, ("band", "mp"), pairs)


def on_device(
    grid_fields, w_in, enc_src, enc_dst, enc_weight, enc_count, norm_gain, w_qkv, w_out_attn,
    offsets, w_decode, dec_src, dec_dst, dec_weight,
):
    band = lax.axis_index("band")
    core = lax.axis_index("mp")
    bands = lax.axis_size("band")
    device = 2 * band + core
    grid = grid_fields.T
    grid_sent = up_and_down(grid)
    info = jnp.stack([
        core,
        enc_count[0],
        (band - 1) * G_BAND,
        device * ROWS,
        (device == 0).astype(jnp.int32),
        (device == 2 * bands - 1).astype(jnp.int32),
        (band - 1) * 2 * ROWS,
        device * GQ,
    ]).astype(jnp.int32)
    dec_own = w_decode.T
    qkv_own = w_qkv.transpose(1, 0, 2)
    edges = jax.ShapeDtypeStruct(enc_src.shape, jnp.int32)
    spread_out = jax.ShapeDtypeStruct((6 * ROWS, GQ), BF16)
    spread_scratch = [
        pltpu.VMEM(dec_src.shape, jnp.int32),
        pltpu.VMEM((GQ, DEC_ROUNDS * TILE), BF16),
        pltpu.VMEM(dec_weight.shape, F32),
    ]
    spread = call(
        early_body, (info, dec_src, dec_dst, dec_weight), 1, spread_out,
        spread_scratch, 5 * 10 ** 9, 10, "early",
    )
    spread, info = lax.optimization_barrier((spread, info))
    sources, targets, weights, gain = call(
        prepare_body,
        (info, enc_src, enc_dst, enc_weight, norm_gain.reshape(1, D)),
        1,
        [
            edges,
            edges,
            jax.ShapeDtypeStruct(enc_weight.shape, F32),
            jax.ShapeDtypeStruct((1, D), F32),
        ],
        [],
        5 * 10 ** 9, 4, "prepare",
    )
    gain, w_in, dec_own = lax.optimization_barrier((gain, w_in, dec_own))
    win_peer, dec_peer = swapped(w_in), swapped(dec_own)
    grid_sent, gain, spread, win_peer, dec_peer = lax.optimization_barrier(
        (grid_sent, gain, spread, win_peer, dec_peer)
    )
    grid_swapped = swapped(grid_sent)
    grid_rows = call(
        unpack_body,
        (info, grid, grid_sent),
        1,
        jax.ShapeDtypeStruct((3 * G_BAND, LANES), F32),
        [pltpu.VMEM((LANES, G_BAND), F32)],
        2 * 10 ** 9, 6, "unpack",
    )
    grid_swapped, grid_rows, qkv_own = lax.optimization_barrier(
        (grid_swapped, grid_rows, qkv_own)
    )
    qkv_peer = swapped(qkv_own)
    band_rows = jax.ShapeDtypeStruct((ROWS, D), BF16)
    step_buffers = [pltpu.VMEM((STEP, LANES), F32)] * 2 + [pltpu.VMEM((ROWS, D), F32)]
    _, mesh_zero, normed, to_band = call(
        encode_body,
        (info, sources, grid_rows, grid_swapped, w_in, win_peer, targets, weights, gain),
        2,
        [
            jax.ShapeDtypeStruct((3 * G_BAND, LANES), F32),
            band_rows,
            band_rows,
            jax.ShapeDtypeStruct((WIN, D), BF16),
        ],
        [
            pltpu.VMEM((LANES, G_BAND), F32),
            pltpu.VMEM((LANES, D), F32),
            pltpu.VMEM((LANES, D), BF16),
        ] + step_buffers,
        7 * 10 ** 9, 14, "encode", {2: 0},
    )
    halo_band = over_the_edge(to_band)
    queries, keys, values_t, keys_sent, values_sent, straight, fold_own = call(
        project_body,
        (info, normed, qkv_own, qkv_peer, mesh_zero, dec_own, dec_peer, w_out_attn),
        1,
        [
            jax.ShapeDtypeStruct((ROWS, D), BF16),
            jax.ShapeDtypeStruct((ROWS, D), BF16),
            jax.ShapeDtypeStruct((D, ROWS), BF16),
            jax.ShapeDtypeStruct((WIN, D), BF16),
            jax.ShapeDtypeStruct((D, WIN), BF16),
            jax.ShapeDtypeStruct((LANES, ROWS), F32),
            jax.ShapeDtypeStruct((2 * LANES, HALF), BF16),
        ],
        [pltpu.VMEM((LANES, D), F32), pltpu.VMEM((LANES, D), BF16)],
        6 * 10 ** 9, 10, "project",
    )
    peer_keys, peer_values = swapped(keys_sent), swapped(values_sent)
    fold_peer = swapped(fold_own)
    sums, stats, mask = call(
        own_body,
        (offsets, queries, keys, values_t),
        1,
        [
            jax.ShapeDtypeStruct((D, ROWS), F32),
            jax.ShapeDtypeStruct((D // LANES, 8, 2 * ROWS), F32),
            jax.ShapeDtypeStruct((SPAN, TILE), BF16),
        ],
        [pltpu.VMEM((ROWS, 2 * GROUP * TILE), F32)] * 2
        + [pltpu.VMEM((8, SPAN + TILE), F32), pltpu.VMEM((SPAN, TILE), F32)],
        8 * 10 ** 9, 12, "own",
    )
    projected = call(
        attend_body,
        (info, halo_band, peer_keys, peer_values, queries, sums, stats, mask, qkv_own,
         qkv_peer, straight, fold_own, fold_peer),
        1,
        jax.ShapeDtypeStruct((C, ROWS), BF16),
        [
            pltpu.VMEM((2 * WIN, D), BF16),
            pltpu.VMEM((D, 2 * WIN), BF16),
            pltpu.VMEM((TILES, WIN, TILE), BF16),
            pltpu.VMEM((D, ROWS), BF16),
            pltpu.VMEM((WIN, 2 * GROUP * TILE), F32),
            pltpu.VMEM((WIN, 2 * GROUP * TILE), F32),
        ],
        10 ** 10, 16, "attend",
    )
    own_pair = jnp.stack([projected, swapped(projected)])
    pair_sent = up_and_down(own_pair)
    spread, base = call(
        spread_body,
        (info, spread, own_pair, dec_src, dec_dst, dec_weight, grid),
        1,
        [spread_out, jax.ShapeDtypeStruct((C, GQ), F32)],
        spread_scratch, 8 * 10 ** 9, 10, "spread", {1: 0},
    )
    pair_sent, base = lax.optimization_barrier((pair_sent, base))
    pair_swapped = swapped(pair_sent)
    sums_out = jax.ShapeDtypeStruct((C, GQ), F32)
    total = call(
        sent_body, (info, pair_sent, spread, base), 1, sums_out, [],
        10 ** 9, 6, "sent",
    )
    return call(
        decode_body, (info, pair_swapped, spread, total), 1,
        jax.ShapeDtypeStruct((C, GQ), BF16), [], 10 ** 9, 6, "decode",
    ).T


def solution(mesh):
    return jax.shard_map(
        on_device,
        mesh=mesh,
        in_specs=(
            P("band", None),
            P(None, "mp"),
            P("band", None),
            P("band", None),
            P("band", None),
            P("band"),
            P(),
            P(None, None, "mp"),
            P("mp", None),
            P(),
            P("mp", None),
            P(("band", "mp"), None),
            P(("band", "mp"), None),
            P(("band", "mp"), None),
        ),
        out_specs=P(("band", "mp"), None),
        check_vma=False,
    )
```

```python
import math
import jax
import jax.numpy as jnp
from jax import lax
from jax.experimental import pallas as pl
from jax.experimental.pallas import tpu as pltpu
from jax.sharding import PartitionSpec as P

D = 1024
C = 100
LANES = 128
TILE = 128
ROWS = 512
WIN = 384
K_OFF = 32
HALF = 512
G_BAND = 2048
EDGE_ROUNDS = 8
TILES = 4
STEP = 512
SPAN = TILE + 2 * WIN
GQ = 1024
DEC_ROUNDS = 3
DEC_TILES = 8
GROUP = 2
HALO_GROUP = 4
EARLY = 2
MASKED = -1e30
SCALE = 64 ** (-0.5) * math.log2(math.e)
F32 = jnp.float32
BF16 = jnp.bfloat16
MIB = 1024 * 1024


def vmem():
    return pl.BlockSpec(memory_space=pltpu.VMEM)


def smem():
    return pl.BlockSpec(memory_space=pltpu.SMEM)


def call(body, operands, smem_count, outs, scratch, flops, room, name, aliases={}):
    specs = [smem()] * smem_count + [vmem()] * (len(operands) - smem_count)
    return pl.pallas_call(
        body,
        out_shape=outs,
        in_specs=specs,
        out_specs=jax.tree.map(lambda _: vmem(), outs),
        scratch_shapes=scratch,
        compiler_params=pltpu.CompilerParams(vmem_limit_bytes=room * MIB),
        cost_estimate=pl.CostEstimate(flops=flops, bytes_accessed=2 * 10 ** 6, transcendentals=0),
        input_output_aliases=aliases,
        name=name,
    )(*operands)


def matmul(a, b):
    return jnp.dot(a, b, preferred_element_type=F32)


def matmul_t(a, b):
    return lax.dot_general(a, b, (((1,), (1,)), ((), ())), preferred_element_type=F32)


def to_rows(part, wide, rows, begin):
    wide[:C, :] = part[...].astype(F32)
    for block in range(G_BAND // LANES):
        columns = slice(block * LANES, (block + 1) * LANES)
        place = pl.multiple_of(begin + block * LANES, LANES)
        rows[pl.ds(place, LANES), :] = wide[:, columns].T


def by_core(core, wide, own, peer):
    @pl.when(core == 0)
    def _():
        wide[:C, :HALF] = own[...].astype(F32)
        wide[:C, HALF:] = peer[...].astype(F32)

    @pl.when(core != 0)
    def _():
        wide[:C, :HALF] = peer[...].astype(F32)
        wide[:C, HALF:] = own[...].astype(F32)


def make_mask(offsets, mask, strip, mask_wide):
    lane = lax.broadcasted_iota(jnp.int32, strip.shape, 1)
    away = lax.broadcasted_iota(jnp.int32, strip.shape, 0) + (SPAN - WIN - 8) - lane
    hit = away == offsets[0]
    for k in range(1, K_OFF):
        hit = hit | (away == offsets[k])
    strip[...] = jnp.where(hit, 0.0, MASKED)
    for begin in range(0, SPAN, 8):
        shift = SPAN - 8 - begin
        mask_wide[begin : begin + 8, :] = strip[:, shift : shift + TILE]
    mask[...] = mask_wide[...].astype(BF16)


def prepare_body(info, src, dst, weight, gain, sources, targets, weights, gains):
    slots = lax.broadcasted_iota(jnp.int32, weights.shape, 0)
    weights[...] = jnp.where(slots < info[1], weight[...].astype(F32), 0.0)
    targets[...] = dst[...] - info[3]
    sources[...] = src[...] - info[2]
    gains[...] = gain[...]


def unpack_body(info, grid, sent, rows, wide):
    wide[96:, :] = jnp.zeros((LANES - 96, G_BAND), F32)
    to_rows(grid, wide, rows, G_BAND)
    to_rows(sent, wide, rows, info[0] * 2 * G_BAND)


def encode_tiles(
    core, order, src, w_in, targets, weights, gain, rows, mesh_zero, normed, first, second, total
):
    row_slots = lax.broadcasted_iota(jnp.int32, (TILE, LANES), 0)
    steps = EDGE_ROUNDS * TILE // STEP
    rounds = STEP // TILE
    count = len(order) * steps

    def tile_of(step):
        place = order[0] + step // steps
        return jnp.where(core == 0, place, TILES - 1 - place)

    def slot_of(step, part):
        return (step % steps * rounds + part) * 2 * TILES + core * TILES + tile_of(step)

    def gather(step, buffer):
        for part in range(rounds):
            slot = slot_of(step, part)
            for edge in range(TILE):
                index = src[slot, edge]
                buffer[pl.ds(part * TILE + edge, 1), :] = rows[pl.ds(index, 1), :]

    def add(step, buffer):
        tile = tile_of(step)
        half = matmul(buffer[...].astype(BF16), w_in[...])
        embedded = (half + half * jnp.tanh(half)).astype(BF16)
        tables = []
        for part in range(rounds):
            slot = slot_of(step, part)
            target = targets[pl.ds(slot, 1), :] - tile * TILE
            tables.append(jnp.where(row_slots == target, weights[pl.ds(slot, 1), :], 0.0))
        table = jnp.concatenate(tables, axis=1).astype(BF16)
        place = pl.ds(pl.multiple_of(tile * TILE, TILE), TILE)
        total[place, :] += matmul(table, embedded)

    for step in range(0, count, steps):
        place = pl.ds(pl.multiple_of(tile_of(step) * TILE, TILE), TILE)
        total[place, :] = jnp.zeros((TILE, D), F32)
    gather(0, first)

    def pair(index, carry):
        gather(2 * index + 1, second)
        add(2 * index, first)
        if count > 2:
            gather(jnp.minimum(2 * index + 2, count - 1), first)
        add(2 * index + 1, second)
        return carry

    lax.fori_loop(0, count // 2, pair, 0)

    def finish(step, carry):
        place = pl.ds(pl.multiple_of(tile_of(step * steps) * TILE, TILE), TILE)
        rounded = total[place, :].astype(BF16)
        mesh_zero[place, :] = rounded
        values = rounded.astype(F32)
        inverse = lax.rsqrt(jnp.mean(values * values, axis=1, keepdims=True) + 1e-05)
        normed[place, :] = (values * inverse * gain[...]).astype(BF16)
        return carry

    lax.fori_loop(0, len(order), finish, 0)


def encode_body(
    info, src, grid_rows, swapped_rows, win_own, win_peer, targets, weights, gain,
    rows, mesh_zero, normed, to_band,
    wide, w_wide, w_in, first, second, total,
):
    core = info[0]
    w_wide[...] = jnp.zeros_like(w_wide)
    by_core(core, w_wide, win_own, win_peer)
    w_in[...] = (w_wide[...] * 0.5).astype(BF16)
    wide[96:, :] = jnp.zeros((LANES - 96, G_BAND), F32)
    to_rows(swapped_rows, wide, rows, (1 - core) * 2 * G_BAND)
    encode_tiles(
        core, range(TILES), src, w_in, targets, weights, gain, rows, mesh_zero, normed,
        first, second, total,
    )
    to_band[...] = normed[pl.ds(pl.multiple_of(core * TILE, TILE), WIN), :]


def identity_pair():
    row = lax.broadcasted_iota(jnp.int32, (TILE, LANES), 0)
    lane = lax.broadcasted_iota(jnp.int32, (TILE, LANES), 1)
    eye = jnp.where(row == lane, 1.0, 0.0).astype(BF16)
    return jnp.concatenate([eye, eye], axis=0), lane


def lanes_of(pair):
    return pl.ds(pl.multiple_of(pair * LANES, LANES), LANES)


def rows_of(block):
    return slice(block * TILE, (block + 1) * TILE)


def score_block(query, lane, eyes, keys, mask, scores):
    query = query.astype(F32)
    stacked = jnp.concatenate(
        [jnp.where(lane < 64, query, 0.0), jnp.where(lane < 64, 0.0, query)], axis=0
    ).astype(BF16)
    scores[...] = matmul_t(
        jnp.concatenate([keys, mask], axis=1), jnp.concatenate([stacked, eyes], axis=1)
    )


def column_top(scores):
    top = scores[:TILE, :]
    for begin in range(TILE, scores.shape[0], TILE):
        top = jnp.maximum(top, scores[begin : begin + TILE, :])
    return jnp.max(top, axis=0, keepdims=True)


def weigh(scores, top, values):
    expos = jnp.exp2(scores[...] - top).astype(BF16)
    ones = jnp.ones((16, scores.shape[0]), BF16)
    result = matmul(jnp.concatenate([values, ones], axis=0), expos)
    both = jnp.concatenate([result[:64, :TILE], result[64:TILE, TILE:]], axis=0)
    return both, result[TILE : TILE + 1, :]


def pipeline(score, finish, first, second, size):
    buffers = (first, second)
    groups = D // LANES // size

    def part_of(buffer, member):
        return buffer.at[:, member * 2 * TILE : (member + 1) * 2 * TILE]

    for member in range(size):
        score(member, 0, part_of(first, member))

    def head_group(group, carry):
        for block in range(TILES):
            here, ahead = buffers[block % 2], buffers[(block + 1) % 2]
            for member in range(size):
                if block + 1 < TILES:
                    pair = group * size + member
                else:
                    pair = jnp.minimum(group + 1, groups - 1) * size + member
                score(pair, (block + 1) % TILES, part_of(ahead, member))
            for member in range(size):
                finish(group * size + member, block, part_of(here, member))
        return carry

    lax.fori_loop(0, groups, head_group, 0)


def project_body(
    info, normed, w_own, w_peer, mesh_zero, dec_own, dec_peer, w_out,
    queries, keys, values_t, keys_sent, values_sent, straight, fold,
    w_wide, w_decode,
):
    w_wide[...] = jnp.zeros_like(w_wide)
    by_core(info[0], w_wide, dec_own, dec_peer)
    w_decode[...] = w_wide[...].astype(BF16)
    folded = matmul_t(w_decode[...], w_out[...])
    upper = folded.astype(BF16)
    fold[:LANES, :] = upper
    fold[LANES:, :] = (folded - upper.astype(F32)).astype(BF16)
    rows = normed[...]
    straight[...] = matmul_t(w_decode[...], mesh_zero[...])
    for half, weight in enumerate((w_own, w_peer)):
        place = slice(half * HALF, (half + 1) * HALF)
        keys[:, place] = matmul(rows, weight[1]).astype(BF16)
        values_t[place, :] = matmul(rows, weight[2]).T.astype(BF16)
        queries[:, place] = (matmul(rows, weight[0]) * SCALE).astype(BF16)

    @pl.when(info[0] == 0)
    def _():
        for half in range(2):
            place = slice(half * HALF, (half + 1) * HALF)
            other = slice((1 - half) * HALF, (2 - half) * HALF)
            keys_sent[:, other] = keys[ROWS - WIN :, place]
            values_sent[other, :] = values_t[place, ROWS - WIN :]

    @pl.when(info[0] != 0)
    def _():
        for half in range(2):
            place = slice(half * HALF, (half + 1) * HALF)
            other = slice((1 - half) * HALF, (2 - half) * HALF)
            keys_sent[:, other] = keys[:WIN, place]
            values_sent[other, :] = values_t[place, :WIN]


def own_body(
    offsets, queries, keys, values_t, sums, stats, mask, first, second, strip, mask_wide
):
    make_mask(offsets, mask, strip, mask_wide)
    eyes, lane = identity_pair()

    def score(pair, block, scores):
        begin = WIN - block * TILE
        score_block(
            queries[rows_of(block), lanes_of(pair)], lane, eyes, keys[:, lanes_of(pair)],
            mask[begin : begin + ROWS, :], scores,
        )

    def finish(pair, block, scores):
        top = column_top(scores)
        both, total = weigh(scores, top, values_t[lanes_of(pair), :])
        sums[lanes_of(pair), rows_of(block)] = both
        columns = slice(2 * block * TILE, 2 * (block + 1) * TILE)
        stats[pair, 0:1, columns] = top
        stats[pair, 1:2, columns] = total

    pipeline(score, finish, first, second, GROUP)


def attend_body(
    info, halo, peer_keys, peer_values, queries, sums, stats, mask, w_own, w_peer,
    straight, fold_own, fold_peer,
    projected,
    keys, values_t, masks, attended, first, second,
):
    core, first_device, last_device = info[0], info[4], info[5]

    @pl.when(core == 0)
    def _():
        keys[WIN:, :] = peer_keys[...]
        values_t[:, WIN:] = peer_values[...]

    @pl.when(core != 0)
    def _():
        keys[:WIN, :] = peer_keys[...]
        values_t[:, :WIN] = peer_values[...]

    begin = pl.ds(pl.multiple_of(core * WIN, WIN), WIN)
    beside = halo[...]
    for half, weight in enumerate((w_own, w_peer)):
        place = slice(half * HALF, (half + 1) * HALF)
        keys[begin, place] = matmul(beside, weight[1]).astype(BF16)
        values_t[place, begin] = matmul(beside, weight[2]).T.astype(BF16)
    low = jnp.where(first_device == 1, MASKED, 0.0)
    high = jnp.where(last_device == 1, MASKED, 0.0)
    for block in range(TILES):
        below, above = WIN - block * TILE, SPAN - block * TILE
        if below > 0:
            masks[block, :below, :] = (mask[:below, :].astype(F32) + low).astype(BF16)
        if above < SPAN:
            masks[block, below:, :] = (mask[above:, :].astype(F32) + high).astype(BF16)
    eyes, lane = identity_pair()

    def score(pair, block, scores):
        seen = slice(block * TILE, block * TILE + WIN)
        score_block(
            queries[rows_of(block), lanes_of(pair)], lane, eyes, keys[seen, lanes_of(pair)],
            masks[block], scores,
        )

    def finish(pair, block, scores):
        seen = slice(block * TILE, block * TILE + WIN)
        columns = slice(2 * block * TILE, 2 * (block + 1) * TILE)
        old, sum_old = stats[pair, 0:1, columns], stats[pair, 1:2, columns]
        top = jnp.maximum(old, column_top(scores))
        both, total = weigh(scores, top, values_t[lanes_of(pair), seen])
        shrink = jnp.exp2(old - top)
        inverse = 1.0 / (sum_old * shrink + total)
        shrink = shrink * inverse
        before = sums[lanes_of(pair), rows_of(block)]
        result = jnp.concatenate([
            before[:64] * shrink[:, :TILE] + both[:64] * inverse[:, :TILE],
            before[64:] * shrink[:, TILE:] + both[64:] * inverse[:, TILE:],
        ], axis=0)
        attended[lanes_of(pair), rows_of(block)] = result.astype(BF16)

    pipeline(score, finish, first, second, HALO_GROUP)
    both = matmul(fold_own[...], attended[:HALF, :]) + matmul(fold_peer[...], attended[HALF:, :])
    projected[...] = (straight[...] + both[:LANES, :] + both[LANES:, :])[:C, :].astype(BF16)


def pair_term(core, pair, spread, place):
    rows = pl.ds(pl.multiple_of(place * ROWS, 2 * ROWS), 2 * ROWS)
    low = jnp.where(core == 0, pair[0].astype(F32), pair[1].astype(F32))
    high = jnp.where(core == 0, pair[1].astype(F32), pair[0].astype(F32))
    halves = jnp.concatenate([low, high], axis=1).astype(BF16)
    return matmul(halves, spread[rows, :])


def spread_halves(info, src, dst, weight, spread, sources, tables, weights, places):
    mesh_base, row_base = info[6], info[7]
    sources[...] = src[...] - mesh_base
    weights[...] = weight[...].astype(F32)
    row_slots = lax.broadcasted_iota(jnp.int32, (TILE, LANES), 0)
    for tile in range(DEC_TILES):
        for part in range(DEC_ROUNDS):
            slot = slice(part * DEC_TILES + tile, part * DEC_TILES + tile + 1)
            target = dst[slot, :] - (row_base + tile * TILE)
            tables[rows_of(tile), rows_of(part)] = jnp.where(
                row_slots == target, weights[slot, :], 0.0
            ).astype(BF16)
    mesh_slots = lax.broadcasted_iota(jnp.int32, (ROWS, LANES), 0)

    def half(place, carry):
        begin = pl.multiple_of(place * ROWS, ROWS)
        for tile in range(DEC_TILES):
            picks = []
            for part in range(DEC_ROUNDS):
                slot = slice(part * DEC_TILES + tile, part * DEC_TILES + tile + 1)
                hit = mesh_slots == sources[slot, :] - begin
                picks.append(jnp.where(hit, 1.0, 0.0).astype(BF16))
            spread[pl.ds(begin, ROWS), rows_of(tile)] = matmul_t(
                jnp.concatenate(picks, axis=1), tables[rows_of(tile), :]
            ).astype(BF16)
        return carry

    lax.fori_loop(places[0], places[-1] + 1, half, 0)


def early_body(info, src, dst, weight, spread, sources, tables, weights):
    spread_halves(info, src, dst, weight, spread, sources, tables, weights, range(EARLY))


def spread_body(
    info, spread_in, own, src, dst, weight, grid, spread, base, sources, tables, weights
):
    core = info[0]
    spread_halves(info, src, dst, weight, spread, sources, tables, weights, range(EARLY, 6))
    fields = grid[:, pl.ds(pl.multiple_of(core * GQ, GQ), GQ)].astype(F32)
    base[...] = fields + pair_term(core, own, spread, 2)


def sent_body(info, sent, spread, base, total):
    core = info[0]
    total[...] = base[...] + pair_term(core, sent, spread, 4 * core)


def decode_body(info, swapped_rows, spread, total, out):
    other = 1 - info[0]
    out[...] = (total[...] + pair_term(other, swapped_rows, spread, 4 * other)).astype(BF16)


def swapped(value):
    return lax.ppermute(value, "mp", [(0, 1), (1, 0)])


def up_and_down(value):
    bands = lax.axis_size("band")
    pairs = [(2 * i, 2 * i + 2) for i in range(bands - 1)]
    pairs += [(2 * i + 3, 2 * i + 1) for i in range(bands - 1)]
    return lax.ppermute(value, ("band", "mp"), pairs)


def over_the_edge(value):
    bands = lax.axis_size("band")
    pairs = [(2 * i + 1, 2 * i + 2) for i in range(bands - 1)]
    pairs += [(j, i) for i, j in pairs]
    return lax.ppermute(value, ("band", "mp"), pairs)


def on_device(
    grid_fields, w_in, enc_src, enc_dst, enc_weight, enc_count, norm_gain, w_qkv, w_out_attn,
    offsets, w_decode, dec_src, dec_dst, dec_weight,
):
    band = lax.axis_index("band")
    core = lax.axis_index("mp")
    bands = lax.axis_size("band")
    device = 2 * band + core
    grid = grid_fields.T
    grid_sent = up_and_down(grid)
    info = jnp.stack([
        core,
        enc_count[0],
        (band - 1) * G_BAND,
        device * ROWS,
        (device == 0).astype(jnp.int32),
        (device == 2 * bands - 1).astype(jnp.int32),
        (band - 1) * 2 * ROWS,
        device * GQ,
    ]).astype(jnp.int32)
    dec_own = w_decode.T
    qkv_own = w_qkv.transpose(1, 0, 2)
    edges = jax.ShapeDtypeStruct(enc_src.shape, jnp.int32)
    spread_out = jax.ShapeDtypeStruct((6 * ROWS, GQ), BF16)
    spread_scratch = [
        pltpu.VMEM(dec_src.shape, jnp.int32),
        pltpu.VMEM((GQ, DEC_ROUNDS * TILE), BF16),
        pltpu.VMEM(dec_weight.shape, F32),
    ]
    spread = call(
        early_body, (info, dec_src, dec_dst, dec_weight), 1, spread_out,
        spread_scratch, 5 * 10 ** 9, 10, "early",
    )
    spread, info = lax.optimization_barrier((spread, info))
    sources, targets, weights, gain = call(
        prepare_body,
        (info, enc_src, enc_dst, enc_weight, norm_gain.reshape(1, D)),
        1,
        [
            edges,
            edges,
            jax.ShapeDtypeStruct(enc_weight.shape, F32),
            jax.ShapeDtypeStruct((1, D), F32),
        ],
        [],
        5 * 10 ** 9, 4, "prepare",
    )
    gain, w_in, dec_own = lax.optimization_barrier((gain, w_in, dec_own))
    win_peer, dec_peer = swapped(w_in), swapped(dec_own)
    grid_sent, gain, spread, win_peer, dec_peer = lax.optimization_barrier(
        (grid_sent, gain, spread, win_peer, dec_peer)
    )
    grid_swapped = swapped(grid_sent)
    grid_rows = call(
        unpack_body,
        (info, grid, grid_sent),
        1,
        jax.ShapeDtypeStruct((3 * G_BAND, LANES), F32),
        [pltpu.VMEM((LANES, G_BAND), F32)],
        2 * 10 ** 9, 6, "unpack",
    )
    grid_swapped, grid_rows, qkv_own = lax.optimization_barrier(
        (grid_swapped, grid_rows, qkv_own)
    )
    qkv_peer = swapped(qkv_own)
    band_rows = jax.ShapeDtypeStruct((ROWS, D), BF16)
    step_buffers = [pltpu.VMEM((STEP, LANES), F32)] * 2 + [pltpu.VMEM((ROWS, D), F32)]
    _, mesh_zero, normed, to_band = call(
        encode_body,
        (info, sources, grid_rows, grid_swapped, w_in, win_peer, targets, weights, gain),
        2,
        [
            jax.ShapeDtypeStruct((3 * G_BAND, LANES), F32),
            band_rows,
            band_rows,
            jax.ShapeDtypeStruct((WIN, D), BF16),
        ],
        [
            pltpu.VMEM((LANES, G_BAND), F32),
            pltpu.VMEM((LANES, D), F32),
            pltpu.VMEM((LANES, D), BF16),
        ] + step_buffers,
        7 * 10 ** 9, 14, "encode", {2: 0},
    )
    halo_band = over_the_edge(to_band)
    queries, keys, values_t, keys_sent, values_sent, straight, fold_own = call(
        project_body,
        (info, normed, qkv_own, qkv_peer, mesh_zero, dec_own, dec_peer, w_out_attn),
        1,
        [
            jax.ShapeDtypeStruct((ROWS, D), BF16),
            jax.ShapeDtypeStruct((ROWS, D), BF16),
            jax.ShapeDtypeStruct((D, ROWS), BF16),
            jax.ShapeDtypeStruct((WIN, D), BF16),
            jax.ShapeDtypeStruct((D, WIN), BF16),
            jax.ShapeDtypeStruct((LANES, ROWS), F32),
            jax.ShapeDtypeStruct((2 * LANES, HALF), BF16),
        ],
        [pltpu.VMEM((LANES, D), F32), pltpu.VMEM((LANES, D), BF16)],
        6 * 10 ** 9, 10, "project",
    )
    peer_keys, peer_values = swapped(keys_sent), swapped(values_sent)
    fold_peer = swapped(fold_own)
    sums, stats, mask = call(
        own_body,
        (offsets, queries, keys, values_t),
        1,
        [
            jax.ShapeDtypeStruct((D, ROWS), F32),
            jax.ShapeDtypeStruct((D // LANES, 8, 2 * ROWS), F32),
            jax.ShapeDtypeStruct((SPAN, TILE), BF16),
        ],
        [pltpu.VMEM((ROWS, 2 * GROUP * TILE), F32)] * 2
        + [pltpu.VMEM((8, SPAN + TILE), F32), pltpu.VMEM((SPAN, TILE), F32)],
        8 * 10 ** 9, 12, "own",
    )
    projected = call(
        attend_body,
        (info, halo_band, peer_keys, peer_values, queries, sums, stats, mask, qkv_own,
         qkv_peer, straight, fold_own, fold_peer),
        1,
        jax.ShapeDtypeStruct((C, ROWS), BF16),
        [
            pltpu.VMEM((2 * WIN, D), BF16),
            pltpu.VMEM((D, 2 * WIN), BF16),
            pltpu.VMEM((TILES, WIN, TILE), BF16),
            pltpu.VMEM((D, ROWS), BF16),
            pltpu.VMEM((WIN, 2 * HALO_GROUP * TILE), F32),
            pltpu.VMEM((WIN, 2 * HALO_GROUP * TILE), F32),
        ],
        10 ** 10, 16, "attend",
    )
    own_pair = jnp.stack([projected, swapped(projected)])
    pair_sent = up_and_down(own_pair)
    spread, base = call(
        spread_body,
        (info, spread, own_pair, dec_src, dec_dst, dec_weight, grid),
        1,
        [spread_out, jax.ShapeDtypeStruct((C, GQ), F32)],
        spread_scratch, 8 * 10 ** 9, 10, "spread", {1: 0},
    )
    pair_sent, base = lax.optimization_barrier((pair_sent, base))
    pair_swapped = swapped(pair_sent)
    sums_out = jax.ShapeDtypeStruct((C, GQ), F32)
    total = call(
        sent_body, (info, pair_sent, spread, base), 1, sums_out, [],
        10 ** 9, 6, "sent",
    )
    return call(
        decode_body, (info, pair_swapped, spread, total), 1,
        jax.ShapeDtypeStruct((C, GQ), BF16), [], 10 ** 9, 6, "decode",
    ).T


def solution(mesh):
    return jax.shard_map(
        on_device,
        mesh=mesh,
        in_specs=(
            P("band", None),
            P(None, "mp"),
            P("band", None),
            P("band", None),
            P("band", None),
            P("band"),
            P(),
            P(None, None, "mp"),
            P("mp", None),
            P(),
            P("mp", None),
            P(("band", "mp"), None),
            P(("band", "mp"), None),
            P(("band", "mp"), None),
        ),
        out_specs=P(("band", "mp"), None),
        check_vma=False,
    )
```

```python
import math
import jax
import jax.numpy as jnp
from jax import lax
from jax.experimental import pallas as pl
from jax.experimental.pallas import tpu as pltpu
from jax.sharding import PartitionSpec as P

D = 1024
C = 100
LANES = 128
TILE = 128
ROWS = 512
WIN = 384
K_OFF = 32
HALF = 512
G_BAND = 2048
EDGE_ROUNDS = 8
TILES = 4
STEP = 512
SPAN = TILE + 2 * WIN
GQ = 1024
DEC_ROUNDS = 3
DEC_TILES = 8
GROUP = 2
HALO_GROUP = 8
EARLY = 2
MASKED = -1e30
SCALE = 64 ** (-0.5) * math.log2(math.e)
F32 = jnp.float32
BF16 = jnp.bfloat16
MIB = 1024 * 1024


def vmem():
    return pl.BlockSpec(memory_space=pltpu.VMEM)


def smem():
    return pl.BlockSpec(memory_space=pltpu.SMEM)


def call(body, operands, smem_count, outs, scratch, flops, room, name, aliases={}):
    specs = [smem()] * smem_count + [vmem()] * (len(operands) - smem_count)
    return pl.pallas_call(
        body,
        out_shape=outs,
        in_specs=specs,
        out_specs=jax.tree.map(lambda _: vmem(), outs),
        scratch_shapes=scratch,
        compiler_params=pltpu.CompilerParams(vmem_limit_bytes=room * MIB),
        cost_estimate=pl.CostEstimate(flops=flops, bytes_accessed=2 * 10 ** 6, transcendentals=0),
        input_output_aliases=aliases,
        name=name,
    )(*operands)


def matmul(a, b):
    return jnp.dot(a, b, preferred_element_type=F32)


def matmul_t(a, b):
    return lax.dot_general(a, b, (((1,), (1,)), ((), ())), preferred_element_type=F32)


def to_rows(part, wide, rows, begin):
    wide[:C, :] = part[...].astype(F32)
    for block in range(G_BAND // LANES):
        columns = slice(block * LANES, (block + 1) * LANES)
        place = pl.multiple_of(begin + block * LANES, LANES)
        rows[pl.ds(place, LANES), :] = wide[:, columns].T


def by_core(core, wide, own, peer):
    @pl.when(core == 0)
    def _():
        wide[:C, :HALF] = own[...].astype(F32)
        wide[:C, HALF:] = peer[...].astype(F32)

    @pl.when(core != 0)
    def _():
        wide[:C, :HALF] = peer[...].astype(F32)
        wide[:C, HALF:] = own[...].astype(F32)


def make_mask(offsets, mask, strip, mask_wide):
    lane = lax.broadcasted_iota(jnp.int32, strip.shape, 1)
    away = lax.broadcasted_iota(jnp.int32, strip.shape, 0) + (SPAN - WIN - 8) - lane
    hit = away == offsets[0]
    for k in range(1, K_OFF):
        hit = hit | (away == offsets[k])
    strip[...] = jnp.where(hit, 0.0, MASKED)
    for begin in range(0, SPAN, 8):
        shift = SPAN - 8 - begin
        mask_wide[begin : begin + 8, :] = strip[:, shift : shift + TILE]
    mask[...] = mask_wide[...].astype(BF16)


def prepare_body(info, src, dst, weight, gain, sources, targets, weights, gains):
    slots = lax.broadcasted_iota(jnp.int32, weights.shape, 0)
    weights[...] = jnp.where(slots < info[1], weight[...].astype(F32), 0.0)
    targets[...] = dst[...] - info[3]
    sources[...] = src[...] - info[2]
    gains[...] = gain[...]


def unpack_body(info, grid, sent, rows, wide):
    wide[96:, :] = jnp.zeros((LANES - 96, G_BAND), F32)
    to_rows(grid, wide, rows, G_BAND)
    to_rows(sent, wide, rows, info[0] * 2 * G_BAND)


def encode_tiles(
    core, order, src, w_in, targets, weights, gain, rows, mesh_zero, normed, first, second, total
):
    row_slots = lax.broadcasted_iota(jnp.int32, (TILE, LANES), 0)
    steps = EDGE_ROUNDS * TILE // STEP
    rounds = STEP // TILE
    count = len(order) * steps

    def tile_of(step):
        place = order[0] + step // steps
        return jnp.where(core == 0, place, TILES - 1 - place)

    def slot_of(step, part):
        return (step % steps * rounds + part) * 2 * TILES + core * TILES + tile_of(step)

    def gather(step, buffer):
        for part in range(rounds):
            slot = slot_of(step, part)
            for edge in range(TILE):
                index = src[slot, edge]
                buffer[pl.ds(part * TILE + edge, 1), :] = rows[pl.ds(index, 1), :]

    def add(step, buffer):
        tile = tile_of(step)
        half = matmul(buffer[...].astype(BF16), w_in[...])
        embedded = (half + half * jnp.tanh(half)).astype(BF16)
        tables = []
        for part in range(rounds):
            slot = slot_of(step, part)
            target = targets[pl.ds(slot, 1), :] - tile * TILE
            tables.append(jnp.where(row_slots == target, weights[pl.ds(slot, 1), :], 0.0))
        table = jnp.concatenate(tables, axis=1).astype(BF16)
        place = pl.ds(pl.multiple_of(tile * TILE, TILE), TILE)
        total[place, :] += matmul(table, embedded)

    for step in range(0, count, steps):
        place = pl.ds(pl.multiple_of(tile_of(step) * TILE, TILE), TILE)
        total[place, :] = jnp.zeros((TILE, D), F32)
    gather(0, first)

    def pair(index, carry):
        gather(2 * index + 1, second)
        add(2 * index, first)
        if count > 2:
            gather(jnp.minimum(2 * index + 2, count - 1), first)
        add(2 * index + 1, second)
        return carry

    lax.fori_loop(0, count // 2, pair, 0)

    def finish(step, carry):
        place = pl.ds(pl.multiple_of(tile_of(step * steps) * TILE, TILE), TILE)
        rounded = total[place, :].astype(BF16)
        mesh_zero[place, :] = rounded
        values = rounded.astype(F32)
        inverse = lax.rsqrt(jnp.mean(values * values, axis=1, keepdims=True) + 1e-05)
        normed[place, :] = (values * inverse * gain[...]).astype(BF16)
        return carry

    lax.fori_loop(0, len(order), finish, 0)


def encode_body(
    info, src, grid_rows, swapped_rows, win_own, win_peer, targets, weights, gain,
    rows, mesh_zero, normed, to_band,
    wide, w_wide, w_in, first, second, total,
):
    core = info[0]
    w_wide[...] = jnp.zeros_like(w_wide)
    by_core(core, w_wide, win_own, win_peer)
    w_in[...] = (w_wide[...] * 0.5).astype(BF16)
    wide[96:, :] = jnp.zeros((LANES - 96, G_BAND), F32)
    to_rows(swapped_rows, wide, rows, (1 - core) * 2 * G_BAND)
    encode_tiles(
        core, range(TILES), src, w_in, targets, weights, gain, rows, mesh_zero, normed,
        first, second, total,
    )
    to_band[...] = normed[pl.ds(pl.multiple_of(core * TILE, TILE), WIN), :]


def identity_pair():
    row = lax.broadcasted_iota(jnp.int32, (TILE, LANES), 0)
    lane = lax.broadcasted_iota(jnp.int32, (TILE, LANES), 1)
    eye = jnp.where(row == lane, 1.0, 0.0).astype(BF16)
    return jnp.concatenate([eye, eye], axis=0), lane


def lanes_of(pair):
    return pl.ds(pl.multiple_of(pair * LANES, LANES), LANES)


def rows_of(block):
    return slice(block * TILE, (block + 1) * TILE)


def score_block(query, lane, eyes, keys, mask, scores):
    query = query.astype(F32)
    stacked = jnp.concatenate(
        [jnp.where(lane < 64, query, 0.0), jnp.where(lane < 64, 0.0, query)], axis=0
    ).astype(BF16)
    scores[...] = matmul_t(
        jnp.concatenate([keys, mask], axis=1), jnp.concatenate([stacked, eyes], axis=1)
    )


def column_top(scores):
    top = scores[:TILE, :]
    for begin in range(TILE, scores.shape[0], TILE):
        top = jnp.maximum(top, scores[begin : begin + TILE, :])
    return jnp.max(top, axis=0, keepdims=True)


def weigh(scores, top, values):
    expos = jnp.exp2(scores[...] - top).astype(BF16)
    ones = jnp.ones((16, scores.shape[0]), BF16)
    result = matmul(jnp.concatenate([values, ones], axis=0), expos)
    both = jnp.concatenate([result[:64, :TILE], result[64:TILE, TILE:]], axis=0)
    return both, result[TILE : TILE + 1, :]


def pipeline(score, finish, first, second, size):
    buffers = (first, second)
    groups = D // LANES // size

    def part_of(buffer, member):
        return buffer.at[:, member * 2 * TILE : (member + 1) * 2 * TILE]

    for member in range(size):
        score(member, 0, part_of(first, member))

    def head_group(group, carry):
        for block in range(TILES):
            here, ahead = buffers[block % 2], buffers[(block + 1) % 2]
            for member in range(size):
                if block + 1 < TILES:
                    pair = group * size + member
                else:
                    pair = jnp.minimum(group + 1, groups - 1) * size + member
                if block + 1 < TILES or groups > 1:
                    score(pair, (block + 1) % TILES, part_of(ahead, member))
            for member in range(size):
                finish(group * size + member, block, part_of(here, member))
        return carry

    lax.fori_loop(0, groups, head_group, 0)


def project_body(
    info, normed, w_own, w_peer, mesh_zero, dec_own, dec_peer, w_out,
    queries, keys, values_t, keys_sent, values_sent, straight, fold,
    w_wide, w_decode,
):
    w_wide[...] = jnp.zeros_like(w_wide)
    by_core(info[0], w_wide, dec_own, dec_peer)
    w_decode[...] = w_wide[...].astype(BF16)
    folded = matmul_t(w_decode[...], w_out[...])
    upper = folded.astype(BF16)
    fold[:LANES, :] = upper
    fold[LANES:, :] = (folded - upper.astype(F32)).astype(BF16)
    rows = normed[...]
    straight[...] = matmul_t(w_decode[...], mesh_zero[...])
    for half, weight in enumerate((w_own, w_peer)):
        place = slice(half * HALF, (half + 1) * HALF)
        keys[:, place] = matmul(rows, weight[1]).astype(BF16)
        values_t[place, :] = matmul(rows, weight[2]).T.astype(BF16)
        queries[:, place] = (matmul(rows, weight[0]) * SCALE).astype(BF16)

    @pl.when(info[0] == 0)
    def _():
        for half in range(2):
            place = slice(half * HALF, (half + 1) * HALF)
            other = slice((1 - half) * HALF, (2 - half) * HALF)
            keys_sent[:, other] = keys[ROWS - WIN :, place]
            values_sent[other, :] = values_t[place, ROWS - WIN :]

    @pl.when(info[0] != 0)
    def _():
        for half in range(2):
            place = slice(half * HALF, (half + 1) * HALF)
            other = slice((1 - half) * HALF, (2 - half) * HALF)
            keys_sent[:, other] = keys[:WIN, place]
            values_sent[other, :] = values_t[place, :WIN]


def own_body(
    offsets, queries, keys, values_t, sums, stats, mask, first, second, strip, mask_wide
):
    make_mask(offsets, mask, strip, mask_wide)
    eyes, lane = identity_pair()

    def score(pair, block, scores):
        begin = WIN - block * TILE
        score_block(
            queries[rows_of(block), lanes_of(pair)], lane, eyes, keys[:, lanes_of(pair)],
            mask[begin : begin + ROWS, :], scores,
        )

    def finish(pair, block, scores):
        top = column_top(scores)
        both, total = weigh(scores, top, values_t[lanes_of(pair), :])
        sums[lanes_of(pair), rows_of(block)] = both
        columns = slice(2 * block * TILE, 2 * (block + 1) * TILE)
        stats[pair, 0:1, columns] = top
        stats[pair, 1:2, columns] = total

    pipeline(score, finish, first, second, GROUP)


def attend_body(
    info, halo, peer_keys, peer_values, queries, sums, stats, mask, w_own, w_peer,
    straight, fold_own, fold_peer,
    projected,
    keys, values_t, masks, attended, first, second,
):
    core, first_device, last_device = info[0], info[4], info[5]

    @pl.when(core == 0)
    def _():
        keys[WIN:, :] = peer_keys[...]
        values_t[:, WIN:] = peer_values[...]

    @pl.when(core != 0)
    def _():
        keys[:WIN, :] = peer_keys[...]
        values_t[:, :WIN] = peer_values[...]

    begin = pl.ds(pl.multiple_of(core * WIN, WIN), WIN)
    beside = halo[...]
    for half, weight in enumerate((w_own, w_peer)):
        place = slice(half * HALF, (half + 1) * HALF)
        keys[begin, place] = matmul(beside, weight[1]).astype(BF16)
        values_t[place, begin] = matmul(beside, weight[2]).T.astype(BF16)
    low = jnp.where(first_device == 1, MASKED, 0.0)
    high = jnp.where(last_device == 1, MASKED, 0.0)
    for block in range(TILES):
        below, above = WIN - block * TILE, SPAN - block * TILE
        if below > 0:
            masks[block, :below, :] = (mask[:below, :].astype(F32) + low).astype(BF16)
        if above < SPAN:
            masks[block, below:, :] = (mask[above:, :].astype(F32) + high).astype(BF16)
    eyes, lane = identity_pair()

    def score(pair, block, scores):
        seen = slice(block * TILE, block * TILE + WIN)
        score_block(
            queries[rows_of(block), lanes_of(pair)], lane, eyes, keys[seen, lanes_of(pair)],
            masks[block], scores,
        )

    def finish(pair, block, scores):
        seen = slice(block * TILE, block * TILE + WIN)
        columns = slice(2 * block * TILE, 2 * (block + 1) * TILE)
        old, sum_old = stats[pair, 0:1, columns], stats[pair, 1:2, columns]
        top = jnp.maximum(old, column_top(scores))
        both, total = weigh(scores, top, values_t[lanes_of(pair), seen])
        shrink = jnp.exp2(old - top)
        inverse = 1.0 / (sum_old * shrink + total)
        shrink = shrink * inverse
        before = sums[lanes_of(pair), rows_of(block)]
        result = jnp.concatenate([
            before[:64] * shrink[:, :TILE] + both[:64] * inverse[:, :TILE],
            before[64:] * shrink[:, TILE:] + both[64:] * inverse[:, TILE:],
        ], axis=0)
        attended[lanes_of(pair), rows_of(block)] = result.astype(BF16)

    pipeline(score, finish, first, second, HALO_GROUP)
    both = matmul(fold_own[...], attended[:HALF, :]) + matmul(fold_peer[...], attended[HALF:, :])
    projected[...] = (straight[...] + both[:LANES, :] + both[LANES:, :])[:C, :].astype(BF16)


def pair_term(core, pair, spread, place):
    rows = pl.ds(pl.multiple_of(place * ROWS, 2 * ROWS), 2 * ROWS)
    low = jnp.where(core == 0, pair[0].astype(F32), pair[1].astype(F32))
    high = jnp.where(core == 0, pair[1].astype(F32), pair[0].astype(F32))
    halves = jnp.concatenate([low, high], axis=1).astype(BF16)
    return matmul(halves, spread[rows, :])


def spread_halves(info, src, dst, weight, spread, sources, tables, weights, places):
    mesh_base, row_base = info[6], info[7]
    sources[...] = src[...] - mesh_base
    weights[...] = weight[...].astype(F32)
    row_slots = lax.broadcasted_iota(jnp.int32, (TILE, LANES), 0)
    for tile in range(DEC_TILES):
        for part in range(DEC_ROUNDS):
            slot = slice(part * DEC_TILES + tile, part * DEC_TILES + tile + 1)
            target = dst[slot, :] - (row_base + tile * TILE)
            tables[rows_of(tile), rows_of(part)] = jnp.where(
                row_slots == target, weights[slot, :], 0.0
            ).astype(BF16)
    mesh_slots = lax.broadcasted_iota(jnp.int32, (ROWS, LANES), 0)

    def half(place, carry):
        begin = pl.multiple_of(place * ROWS, ROWS)
        for tile in range(DEC_TILES):
            picks = []
            for part in range(DEC_ROUNDS):
                slot = slice(part * DEC_TILES + tile, part * DEC_TILES + tile + 1)
                hit = mesh_slots == sources[slot, :] - begin
                picks.append(jnp.where(hit, 1.0, 0.0).astype(BF16))
            spread[pl.ds(begin, ROWS), rows_of(tile)] = matmul_t(
                jnp.concatenate(picks, axis=1), tables[rows_of(tile), :]
            ).astype(BF16)
        return carry

    lax.fori_loop(places[0], places[-1] + 1, half, 0)


def early_body(info, src, dst, weight, spread, sources, tables, weights):
    spread_halves(info, src, dst, weight, spread, sources, tables, weights, range(EARLY))


def spread_body(
    info, spread_in, own, src, dst, weight, grid, spread, base, sources, tables, weights
):
    core = info[0]
    spread_halves(info, src, dst, weight, spread, sources, tables, weights, range(EARLY, 6))
    fields = grid[:, pl.ds(pl.multiple_of(core * GQ, GQ), GQ)].astype(F32)
    base[...] = fields + pair_term(core, own, spread, 2)


def sent_body(info, sent, spread, base, total):
    core = info[0]
    total[...] = base[...] + pair_term(core, sent, spread, 4 * core)


def decode_body(info, swapped_rows, spread, total, out):
    other = 1 - info[0]
    out[...] = (total[...] + pair_term(other, swapped_rows, spread, 4 * other)).astype(BF16)


def swapped(value):
    return lax.ppermute(value, "mp", [(0, 1), (1, 0)])


def up_and_down(value):
    bands = lax.axis_size("band")
    pairs = [(2 * i, 2 * i + 2) for i in range(bands - 1)]
    pairs += [(2 * i + 3, 2 * i + 1) for i in range(bands - 1)]
    return lax.ppermute(value, ("band", "mp"), pairs)


def over_the_edge(value):
    bands = lax.axis_size("band")
    pairs = [(2 * i + 1, 2 * i + 2) for i in range(bands - 1)]
    pairs += [(j, i) for i, j in pairs]
    return lax.ppermute(value, ("band", "mp"), pairs)


def on_device(
    grid_fields, w_in, enc_src, enc_dst, enc_weight, enc_count, norm_gain, w_qkv, w_out_attn,
    offsets, w_decode, dec_src, dec_dst, dec_weight,
):
    band = lax.axis_index("band")
    core = lax.axis_index("mp")
    bands = lax.axis_size("band")
    device = 2 * band + core
    grid = grid_fields.T
    grid_sent = up_and_down(grid)
    info = jnp.stack([
        core,
        enc_count[0],
        (band - 1) * G_BAND,
        device * ROWS,
        (device == 0).astype(jnp.int32),
        (device == 2 * bands - 1).astype(jnp.int32),
        (band - 1) * 2 * ROWS,
        device * GQ,
    ]).astype(jnp.int32)
    dec_own = w_decode.T
    qkv_own = w_qkv.transpose(1, 0, 2)
    edges = jax.ShapeDtypeStruct(enc_src.shape, jnp.int32)
    spread_out = jax.ShapeDtypeStruct((6 * ROWS, GQ), BF16)
    spread_scratch = [
        pltpu.VMEM(dec_src.shape, jnp.int32),
        pltpu.VMEM((GQ, DEC_ROUNDS * TILE), BF16),
        pltpu.VMEM(dec_weight.shape, F32),
    ]
    spread = call(
        early_body, (info, dec_src, dec_dst, dec_weight), 1, spread_out,
        spread_scratch, 5 * 10 ** 9, 10, "early",
    )
    spread, info = lax.optimization_barrier((spread, info))
    sources, targets, weights, gain = call(
        prepare_body,
        (info, enc_src, enc_dst, enc_weight, norm_gain.reshape(1, D)),
        1,
        [
            edges,
            edges,
            jax.ShapeDtypeStruct(enc_weight.shape, F32),
            jax.ShapeDtypeStruct((1, D), F32),
        ],
        [],
        5 * 10 ** 9, 4, "prepare",
    )
    gain, w_in, dec_own = lax.optimization_barrier((gain, w_in, dec_own))
    win_peer, dec_peer = swapped(w_in), swapped(dec_own)
    grid_sent, gain, spread, win_peer, dec_peer = lax.optimization_barrier(
        (grid_sent, gain, spread, win_peer, dec_peer)
    )
    grid_swapped = swapped(grid_sent)
    grid_rows = call(
        unpack_body,
        (info, grid, grid_sent),
        1,
        jax.ShapeDtypeStruct((3 * G_BAND, LANES), F32),
        [pltpu.VMEM((LANES, G_BAND), F32)],
        2 * 10 ** 9, 6, "unpack",
    )
    grid_swapped, grid_rows, qkv_own = lax.optimization_barrier(
        (grid_swapped, grid_rows, qkv_own)
    )
    qkv_peer = swapped(qkv_own)
    band_rows = jax.ShapeDtypeStruct((ROWS, D), BF16)
    step_buffers = [pltpu.VMEM((STEP, LANES), F32)] * 2 + [pltpu.VMEM((ROWS, D), F32)]
    _, mesh_zero, normed, to_band = call(
        encode_body,
        (info, sources, grid_rows, grid_swapped, w_in, win_peer, targets, weights, gain),
        2,
        [
            jax.ShapeDtypeStruct((3 * G_BAND, LANES), F32),
            band_rows,
            band_rows,
            jax.ShapeDtypeStruct((WIN, D), BF16),
        ],
        [
            pltpu.VMEM((LANES, G_BAND), F32),
            pltpu.VMEM((LANES, D), F32),
            pltpu.VMEM((LANES, D), BF16),
        ] + step_buffers,
        7 * 10 ** 9, 14, "encode", {2: 0},
    )
    halo_band = over_the_edge(to_band)
    queries, keys, values_t, keys_sent, values_sent, straight, fold_own = call(
        project_body,
        (info, normed, qkv_own, qkv_peer, mesh_zero, dec_own, dec_peer, w_out_attn),
        1,
        [
            jax.ShapeDtypeStruct((ROWS, D), BF16),
            jax.ShapeDtypeStruct((ROWS, D), BF16),
            jax.ShapeDtypeStruct((D, ROWS), BF16),
            jax.ShapeDtypeStruct((WIN, D), BF16),
            jax.ShapeDtypeStruct((D, WIN), BF16),
            jax.ShapeDtypeStruct((LANES, ROWS), F32),
            jax.ShapeDtypeStruct((2 * LANES, HALF), BF16),
        ],
        [pltpu.VMEM((LANES, D), F32), pltpu.VMEM((LANES, D), BF16)],
        6 * 10 ** 9, 10, "project",
    )
    peer_keys, peer_values = swapped(keys_sent), swapped(values_sent)
    fold_peer = swapped(fold_own)
    sums, stats, mask = call(
        own_body,
        (offsets, queries, keys, values_t),
        1,
        [
            jax.ShapeDtypeStruct((D, ROWS), F32),
            jax.ShapeDtypeStruct((D // LANES, 8, 2 * ROWS), F32),
            jax.ShapeDtypeStruct((SPAN, TILE), BF16),
        ],
        [pltpu.VMEM((ROWS, 2 * GROUP * TILE), F32)] * 2
        + [pltpu.VMEM((8, SPAN + TILE), F32), pltpu.VMEM((SPAN, TILE), F32)],
        8 * 10 ** 9, 12, "own",
    )
    projected = call(
        attend_body,
        (info, halo_band, peer_keys, peer_values, queries, sums, stats, mask, qkv_own,
         qkv_peer, straight, fold_own, fold_peer),
        1,
        jax.ShapeDtypeStruct((C, ROWS), BF16),
        [
            pltpu.VMEM((2 * WIN, D), BF16),
            pltpu.VMEM((D, 2 * WIN), BF16),
            pltpu.VMEM((TILES, WIN, TILE), BF16),
            pltpu.VMEM((D, ROWS), BF16),
            pltpu.VMEM((WIN, 2 * HALO_GROUP * TILE), F32),
            pltpu.VMEM((WIN, 2 * HALO_GROUP * TILE), F32),
        ],
        10 ** 10, 16, "attend",
    )
    own_pair = jnp.stack([projected, swapped(projected)])
    pair_sent = up_and_down(own_pair)
    spread, base = call(
        spread_body,
        (info, spread, own_pair, dec_src, dec_dst, dec_weight, grid),
        1,
        [spread_out, jax.ShapeDtypeStruct((C, GQ), F32)],
        spread_scratch, 8 * 10 ** 9, 10, "spread", {1: 0},
    )
    pair_sent, base = lax.optimization_barrier((pair_sent, base))
    pair_swapped = swapped(pair_sent)
    sums_out = jax.ShapeDtypeStruct((C, GQ), F32)
    total = call(
        sent_body, (info, pair_sent, spread, base), 1, sums_out, [],
        10 ** 9, 6, "sent",
    )
    return call(
        decode_body, (info, pair_swapped, spread, total), 1,
        jax.ShapeDtypeStruct((C, GQ), BF16), [], 10 ** 9, 6, "decode",
    ).T


def solution(mesh):
    return jax.shard_map(
        on_device,
        mesh=mesh,
        in_specs=(
            P("band", None),
            P(None, "mp"),
            P("band", None),
            P("band", None),
            P("band", None),
            P("band"),
            P(),
            P(None, None, "mp"),
            P("mp", None),
            P(),
            P("mp", None),
            P(("band", "mp"), None),
            P(("band", "mp"), None),
            P(("band", "mp"), None),
        ),
        out_specs=P(("band", "mp"), None),
        check_vma=False,
    )
```
